32 devices in a mesh: members: 2 (over y), tx: 4 (over z), ty: 4 (over x, core).
Axes of the slice: x: 2, y: 2, z: 4, core: 2. Of those that a mesh axis runs over, the one named last changes fastest.
Arguments:
- tracers: float32 [4, 16, 64, 512], P('members', None, 'tx', 'ty'), parts along dimension 0, may hold values from -6 to 6
- costate: float32 [4, 16, 64, 512], P('members', None, 'tx', 'ty'), parts along dimension 0, may hold values from -6 to 6
- mixing_h: float32 [32, 64, 512], P('members', 'tx', 'ty'), parts along dimension 0, may hold values from 0.01 to 0.24
- mixing_v: float32 [32, 64, 512], P('members', 'tx', 'ty'), parts along dimension 0, may hold values from 0.1 to 5
- levels: int32 [64, 512], P('tx', 'ty'), may hold values from 0 to 16
- seam_code: int32 [4], P('ty'), may hold values from 0 to 1
Outputs:
- tracer_adjoint: float32 [4, 16, 64, 512], P('members', None, 'tx', 'ty'), parts along dimension 0
- grad_mixing_h: float32 [32, 64, 512], P('members', 'tx', 'ty'), parts along dimension 0
- grad_mixing_v: float32 [32, 64, 512], P('members', 'tx', 'ty'), parts along dimension 0
The draws below stay inside these ranges and needn't reach their ends.
There are 2 independent parts, one for each index of `members`. The reference program is written for one: setup_inputs(seed, part) draws one part's arguments, and reference() takes and returns one part's arrays. A program takes and returns all parts, laid end to end along the dimension named above; an argument that names none is the same for every part. Nothing has to cross between parts.
All inputs are finite; a program needn't handle non-finite values.
Results may differ from the reference program's by a relative error of at most 0.0001.
Values sent between devices are 32-bit elements; how exact they have to be, the bound alone decides.
No kernel may reach another device: no remote copies, remote signals or barrier semaphores. Data moves between devices by JAX's collectives and lax.ppermute only.
A program may use at most 64 MiB of HBM per device.

```python
import math
import jax
import jax.numpy as jnp

TRACERS = 2
K = 16
CY = 128
NX = 64
NY = 512
SEAM_TILES = 4


def set_ends(values, rng, least, high):
    spot = [jax.random.randint(jax.random.fold_in(rng, axis), (), 0, length) for axis, length in enumerate(values.shape)]
    longest = values.shape.index(max(values.shape))
    beside = spot[:longest] + [(spot[longest] + 1) % values.shape[longest]] + spot[longest + 1:]
    return values.at[tuple(spot)].set(least).at[tuple(beside)].set(high)


def shard_levels(key, extent, shards, low, top_value):
    level = 1.0
    for axis_at, blocks in shards:
        steps = jax.random.uniform(jax.random.fold_in(jax.random.fold_in(key, 6), axis_at), (blocks,), jnp.float32, low / len(shards), top_value / len(shards))
        level = level * jnp.repeat(jnp.exp(steps), extent[axis_at] // blocks).reshape((-1,) + (1,) * (len(extent) - 1 - axis_at))
    return level


def normal_values(own_key, dims, spread, most, cuts=(), kind=jnp.bfloat16):
    drawn = jax.random.normal(own_key, dims, jnp.float32) * spread
    if len(cuts) > 0:
        drawn = shard_levels(own_key, dims, cuts, -0.22, 0.18) * drawn
    return jnp.clip(drawn, min=-most, max=most).astype(kind)


def setup_inputs(seed: int = 0, part: int = 0) -> dict:
    key_of = jax.random.split(jax.random.key(seed), 7)
    own_keys = jax.random.split(jax.random.fold_in(key_of[6], part), 7)
    tracers = normal_values(own_keys[0], (TRACERS, K, NX, NY), 1.0, 6.0, ((2, 4), (3, 4)), jnp.float32)
    costate = normal_values(own_keys[1], (TRACERS, K, NX, NY), 1.0, 6.0, ((2, 4), (3, 4)), jnp.float32)
    mixing_h = jnp.clip(jnp.exp(math.log(0.24) - 3.1780538 * jax.random.uniform(own_keys[2], (K, NX, NY), jnp.float32) ** shard_levels(own_keys[2], (K, NX, NY), ((1, 4), (2, 4)), -0.2, 0.2)), 0.01, 0.24)
    mixing_v = jnp.clip(jnp.exp(math.log(5.0) - 3.912023 * jax.random.uniform(own_keys[3], (K, NX, NY), jnp.float32) ** shard_levels(own_keys[3], (K, NX, NY), ((1, 4), (2, 4)), -0.2, 0.2)), 0.1, 5.0)
    levels = set_ends(jax.random.randint(key_of[4], (NX, NY), 0, K + 1), jax.random.fold_in(key_of[4], 1), 0, K).astype(jnp.int32)
    seam_code = set_ends(jax.random.randint(key_of[5], (SEAM_TILES,), 0, 2), jax.random.fold_in(key_of[5], 1), 0, 1).astype(jnp.int32)
    return dict(tracers=tracers, costate=costate, mixing_h=mixing_h, mixing_v=mixing_v, levels=levels, seam_code=seam_code)


def vertical_solve(rhs, bonds):
    depth = rhs.shape[1]
    factors = []
    reduced = []
    for level_no in range(depth):
        diagonal = 1.0
        if level_no > 0:
            diagonal = diagonal + bonds[level_no - 1]
        if level_no < depth - 1:
            diagonal = diagonal + bonds[level_no]
        if level_no == 0:
            pivot = diagonal
            value = rhs[:, 0]
        else:
            pivot = diagonal + bonds[level_no - 1] * factors[-1]
            value = rhs[:, level_no] + bonds[level_no - 1] * reduced[-1]
        reduced.append(value / pivot)
        if level_no < depth - 1:
            factors.append(-bonds[level_no] / pivot)
    result = [reduced[depth - 1]]
    for level_no in range(depth - 2, -1, -1):
        result.append(reduced[level_no] - factors[level_no] * result[-1])
    result = result[::-1]
    return jnp.stack(result, axis=1)

def reference(tracers, costate, mixing_h, mixing_v, levels, seam_code):
    depth, rows_all, cols_all = mixing_h.shape
    wet = (jnp.arange(depth, dtype=jnp.int32)[:, None, None] < levels[None]).astype(jnp.float32)
    column = jnp.arange(cols_all, dtype=jnp.int32)
    tile_col = column // CY
    flipped = jnp.take(seam_code, tile_col)
    mapped = jnp.where(flipped == 1, tile_col * CY + CY - 1 - column % CY, column).astype(jnp.int32)

    def shifts(values):
        north = jnp.concatenate([values[..., 1:, :], jnp.take(values[..., :1, :], mapped, axis=-1)], axis=-2)
        south = jnp.concatenate([jnp.take(values[..., -1:, :], mapped, axis=-1), values[..., :-1, :]], axis=-2)
        blank = jnp.zeros_like(values[..., :1])
        east = jnp.concatenate([values[..., 1:], blank], axis=-1)
        west = jnp.concatenate([blank, values[..., :-1]], axis=-1)
        return [north, south, east, west]
    wet_near = shifts(wet)

    def forward(start, mix_h, mix_v):
        weights = [0.5 * (mix_h + near) * wet * wet_n for near, wet_n in zip(shifts(mix_h), wet_near)]
        bonds = 0.5 * (mix_v[:-1] + mix_v[1:]) * wet[:-1] * wet[1:]
        state = start
        for turn in range(2):
            mixed = state
            for near, weight in zip(shifts(state), weights):
                mixed = mixed + weight * (near - state)
            state = vertical_solve(mixed, bonds)
        return state
    unused, pull = jax.vjp(forward, tracers, mixing_h, mixing_v)
    tracer_adjoint, grad_mixing_h, grad_mixing_v = pull(costate)
    return (tracer_adjoint, grad_mixing_h, grad_mixing_v)
```

```python
import jax
import jax.numpy as jnp
from jax import lax
from jax.experimental import pallas as pl
from jax.experimental.pallas import tpu as pltpu
from jax.sharding import PartitionSpec as P

LANES = 128
ROWS = 16
GROUP = 16
PER_TILE = LANES // GROUP


FILLER = 3


def in_vmem(array):
    return pltpu.with_memory_space_constraint(array, pltpu.VMEM)


def in_hbm(array):
    return pltpu.with_memory_space_constraint(array, pltpu.HBM)


def vmem_out(*shape):
    return pltpu.VMEM(shape, jnp.float32)


def iota(rows, dim):
    return lax.broadcasted_iota(jnp.int32, (rows, LANES), dim)


def roll(value, shift, axis):
    return pltpu.roll(value, shift % value.shape[axis], axis)


def fold(value):
    return jnp.where(iota(8, 0) < 4, value[:8], value[8:])


def east(value, halo):
    lane = iota(value.shape[0], 1)
    return roll(jnp.where(lane == 0, halo, value), -1, 1)


def west(value, halo):
    lane = iota(value.shape[0], 1)
    return roll(jnp.where(lane == LANES - 1, halo, value), 1, 1)


def rim(tile, base):
    return roll(tile, LANES - 2 - base, 1)


def north(value, beyond):
    sub = iota(8, 0)
    low, high = roll(value[:8], -1, 0), roll(value[8:], -1, 0)
    return jnp.concatenate([jnp.where(sub == 7, high, low), jnp.where(sub == 7, beyond, high)], axis=0)


def south(value, beyond):
    sub = iota(8, 0)
    low, high = roll(value[:8], 1, 0), roll(value[8:], 1, 0)
    return jnp.concatenate([jnp.where(sub == 0, beyond, low), jnp.where(sub == 0, low, high)], axis=0)


def bond(mix_v, level, k, depth):
    under = jnp.minimum(k + 1, depth - 1)
    return jnp.where(level > k + 1, 0.5 * (mix_v[k] + mix_v[under]), 0.0)


def prepare(
    seam,
    tracers,
    costate,
    mix_h_in,
    mix_v_in,
    levels_in,
    fields,
    factors,
    message,
    mix_h,
    mix_v,
    levels,
    sems,
):
    depth = mix_h.shape[0]
    copies = [
        pltpu.make_async_copy(source, target, sems.at[n])
        for n, (source, target) in enumerate(
            (
                (levels_in, levels),
                (mix_v_in, mix_v),
                (costate.at[0], fields.at[:, 2]),
                (costate.at[1], fields.at[:, 3]),
                (tracers.at[0], fields.at[:, 0]),
                (tracers.at[1], fields.at[:, 1]),
                (mix_h_in, mix_h),
            )
        )
    ]
    for copy in copies:
        copy.start()
    for copy in copies[:4]:
        copy.wait()
    level = levels[...]
    lane = iota(ROWS, 1)
    zero = jnp.zeros((ROWS, LANES), jnp.float32)

    def down(k, carry):
        bond_above, inverse, *values = carry
        bond_here = bond(mix_v, level, k, depth)
        inverse = 1.0 / (1.0 + bond_above + bond_here - bond_above * (bond_above * inverse))
        factor = bond_above * inverse
        factors[0, k] = inverse
        factors[1, k] = factor
        factors[2, k] = bond_here * inverse
        for t in range(2):
            values[t] = fields[k, 2 + t] * inverse + factor * values[t]
            fields[k, 2 + t] = values[t]
        return (bond_here, inverse, *values)

    lax.fori_loop(0, depth, down, (zero, zero, zero, zero))
    for copy in copies[4:]:
        copy.wait()
    level_f = level.astype(jnp.float32)
    code = zero + seam[0].astype(jnp.float32)

    def up(n, carry):
        k = depth - 1 - n
        bond_here, inverse, *values = carry
        for t in range(2):
            values[t] = fields[k, 2 + t] + factors[2, k] * values[t]
            fields[k, 2 + t] = values[t]
        bond_above = jnp.where(k > 0, bond(mix_v, level, jnp.maximum(k - 1, 0), depth), 0.0)
        inverse = 1.0 / (1.0 + bond_above + bond_here - bond_here * (bond_here * inverse))
        factors[3, k] = inverse
        factors[4, k] = bond_here * inverse
        factors[5, k] = bond_above * inverse
        tile, base = k // PER_TILE, GROUP * (k % PER_TILE)
        place = lane // 4 - base // 4
        first = message[tile]
        for q, value in enumerate((fields[k, 0], fields[k, 1], values[0], values[1])):
            first = jnp.where(place == q, pltpu.roll(value, (base + 4 * q + 2) % LANES, 1), first)
        message[tile] = first
        second = message[depth // PER_TILE + tile]
        for q, value in enumerate((mix_h[k], mix_v[k], level_f)):
            second = jnp.where(place == q, pltpu.roll(value, (base + 4 * q + 2) % LANES, 1), second)
        message[depth // PER_TILE + tile] = jnp.where(place == FILLER, code, second)
        return (bond_above, inverse, *values)

    lax.fori_loop(0, depth, up, (zero, zero, zero, zero))


def pack_rows(near, far, fields, mix_h, mix_v, levels, lower, upper, merged):
    depth = mix_h.shape[0]
    tiles = depth // PER_TILE
    place = lax.axis_index("ty")
    last = lax.axis_size("ty") - 1
    even = place % 2 == 0
    column = iota(ROWS, 1) % 4
    from_west = column < 2
    missing = ((place == 0) & from_west) | ((place == last) & jnp.logical_not(from_west))
    base_level = 10 * depth
    corners = []
    for j in range(2 * tiles):
        west_tile = jnp.where(even, far[j], near[j])
        east_tile = jnp.where(even, near[j], far[j])
        tile = jnp.where(from_west, west_tile, east_tile)
        if j >= tiles:
            tile = jnp.where(missing, 0.0, tile)
        merged[j] = tile
        other = jnp.where(
            column == 0, roll(west_tile, -2, 1), jnp.where(column == 3, roll(east_tile, 2, 1), tile)
        )
        corners.append(fold(other))
    sub = iota(8, 0)
    level_all = levels[...].astype(jnp.float32)
    level = fold(level_all)
    for target, row in ((lower, 0), (upper, 7)):
        block = jnp.zeros((8, LANES), jnp.float32)
        for n, value in enumerate([level, *corners]):
            block = jnp.where(sub == n, roll(value, n - row, 0), block)
        target[base_level : base_level + 8] = block

    def inner(value):
        return jnp.where(sub < 4, roll(value, -1, 0), roll(value, 1, 0))

    level_rim = rim(fold(merged[tiles]), 8)
    shallow = [
        jnp.minimum(level, near_level)
        for near_level in (east(level, level_rim), west(level, level_rim), inner(level))
    ]

    def row(k, _):
        tile, base = k // PER_TILE, GROUP * (k % PER_TILE)
        coefs = fold(merged[tiles + tile])
        mix = fold(mix_h[k])
        mix_rim = rim(coefs, base)
        mixes = (east(mix, mix_rim), west(mix, mix_rim), inner(mix))
        weights = [
            jnp.where(open_to > k.astype(jnp.float32), 0.5 * (mix + near_mix), 0.0)
            for open_to, near_mix in zip(shallow, mixes)
        ]
        packed = fold(merged[tile])
        low = jnp.zeros((8, LANES), jnp.float32)
        high = low
        for q in range(4):
            value = fold(fields[k, q])
            halo = rim(packed, base + 4 * q)
            part = value
            for near_value, weight in zip(
                (east(value, halo), west(value, halo), inner(value)), weights
            ):
                part = part + weight * (near_value - value)
            for n, thing in ((q, value), (4 + q, part)):
                low = jnp.where(sub == n, roll(thing, n, 0), low)
                high = jnp.where(sub == n, roll(thing, n - 7, 0), high)
        at = pl.ds(pl.multiple_of(8 * k, 8), 8)
        lower[at] = low
        upper[at] = high
        for n, array in enumerate((mix_h, mix_v)):
            at = pl.ds((8 + n) * depth + k, 1)
            lower[at] = array[k, :1]
            upper[at] = array[k, ROWS - 1 :]
        return 0

    lax.fori_loop(0, depth, row, 0)


def finish(
    seam,
    from_below,
    from_above,
    lower,
    upper,
    merged,
    own,
    fields,
    factors,
    mix_h,
    levels,
    adjoint_out,
    grad_h_out,
    grad_v_out,
    below,
    above,
    rows,
    columns,
    packed,
    weights,
    inside,
    later,
    adjoint,
    grad_h,
    grad_v,
    sems,
):
    depth = mix_h.shape[0]
    tiles = depth // PER_TILE
    sub = iota(8, 0)
    lane = iota(ROWS, 1)
    place = lax.axis_index("tx")
    last = lax.axis_size("tx") - 1
    base_mix, base_v, base_level, base_corner = 8 * depth, 9 * depth, 10 * depth, 10 * depth + 1
    zero = jnp.zeros((ROWS, LANES), jnp.float32)
    zero_rows = jnp.zeros((8, LANES), jnp.float32)

    for source, target, edge in ((from_below, below, 0), (from_above, above, last)):
        turn = (seam[0] == 1) & (place == edge)

        @pl.when(turn)
        def _():
            back = LANES - 1 - iota(8, 1)
            for r in range(0, base_level, 8):
                target[r : r + 8] = jnp.take_along_axis(source[r : r + 8], back, axis=1)
            block = source[base_level : base_level + 8]
            target[base_level : base_level + 8] = jnp.where(
                sub < 1, jnp.take_along_axis(block, back, axis=1), block
            )

        @pl.when(jnp.logical_not(turn))
        def _():
            for r in range(0, base_level + 8, 8):
                target[r : r + 8] = source[r : r + 8]

    def both(a, b):
        return jnp.where(sub < 4, a, b)

    column = lane % 4

    def coefficient(value, n):
        kept = iota(value.shape[0], 1) % GROUP // 4 == n
        value = roll(jnp.where(kept, value, 0.0), -4 * n, 1)
        value = value + roll(value, 4, 1)
        return value + roll(value, 8, 1)

    def around(value, mine, below_row, above_row):
        return (
            jnp.where(column == 1, roll(mine, -1, 1), roll(mine, 1, 1)),
            jnp.where(column == 1, roll(value, 1, 1), roll(value, -1, 1)),
            north(value, above_row),
            south(value, below_row),
        )

    turned = coefficient(merged[tiles, :8], FILLER)
    spot = iota(8, 1) % 4
    corner_rows = []
    for target, edge in ((below, 0), (above, last)):
        block = target[base_level : base_level + 8]
        swap = (place == edge) & (turned > 0.5)
        swapped = jnp.where(spot == 1, roll(block, 1, 1), roll(block, -1, 1))
        corner_rows.append(jnp.where(swap, swapped, block))
    for j in range(tiles):
        corner = [block[1 + j : 2 + j] for block in corner_rows]
        corner_coef = [block[1 + tiles + j : 2 + tiles + j] for block in corner_rows]
        level_k = (lane // GROUP + j * PER_TILE).astype(jnp.float32)
        (mix, mixes), (level, level_near) = [
            (
                coefficient(merged[tiles + j], n),
                around(
                    coefficient(merged[tiles + j], n),
                    coefficient(own[tiles + j], n),
                    *(coefficient(c, n) for c in corner_coef),
                ),
            )
            for n in (0, 2)
        ]
        value = merged[j]
        mixed = value
        for near_value, near_mix, near_level in zip(
            around(value, own[j], *corner), mixes, level_near
        ):
            weight = jnp.where(
                jnp.minimum(level, near_level) > level_k, 0.5 * (mix + near_mix), 0.0
            )
            mixed = mixed + weight * (near_value - value)
        packed[0, j] = mixed
        packed[1, j] = coefficient(merged[tiles + j], 1)
        if j == 0:
            level_columns = level

    def unpacked(n, k):
        return roll(packed[n, k // PER_TILE], LANES - GROUP * (k % PER_TILE), 1)

    level_out = both(below[base_level : base_level + 1], above[base_level : base_level + 1])
    level_in = both(lower[base_level : base_level + 1], upper[base_level : base_level + 1])
    level_face = jnp.minimum(level_out, level_in)
    level = levels[...].astype(jnp.float32)

    def near_all(value, halo, below_row, above_row):
        return (
            north(value, above_row),
            south(value, below_row),
            east(value, halo),
            west(value, halo),
        )

    shallow = [
        jnp.minimum(level, near_level)
        for near_level in near_all(
            level,
            rim(merged[tiles], 8),
            below[base_level : base_level + 1],
            above[base_level : base_level + 1],
        )
    ]

    def pivot_step(bond_above, bond_here, inverse):
        return 1.0 / (1.0 + bond_above + bond_here - bond_above * (bond_above * inverse))

    def row_at(ref, start, k):
        return ref[pl.ds(start + k, 1)]

    def mix_v_rows(k):
        return both(row_at(below, base_v, k), row_at(above, base_v, k))

    def steps_of(k, q, below_block, above_block):
        value = fields[k, q]
        halo = rim(merged[k // PER_TILE], GROUP * (k % PER_TILE) + 4 * q)
        nears = near_all(value, halo, below_block[q : q + 1], above_block[q : q + 1])
        return value, [n - value for n in nears]

    def first(k, carry):
        (row_bond, row_inverse, row_value), (col_bond, col_inverse, col_value), values = carry
        kf = k.astype(jnp.float32)
        block = pl.ds(pl.multiple_of(8 * k, 8), 8)
        below_block, above_block = below[block], above[block]
        under = jnp.minimum(k + 1, depth - 1)
        bond_here = jnp.where(
            level_out > kf + 1.0, 0.5 * (mix_v_rows(k) + mix_v_rows(under)), 0.0
        )
        row_inverse = pivot_step(row_bond, bond_here, row_inverse)
        out = both(below_block, roll(above_block, 4, 0))
        part = both(roll(below_block, 4, 0), above_block)
        inn = both(lower[block], roll(upper[block], 4, 0))
        weight = 0.5 * (
            both(row_at(below, base_mix, k), row_at(above, base_mix, k))
            + both(row_at(lower, base_mix, k), row_at(upper, base_mix, k))
        )
        rhs = part + jnp.where(level_face > kf, weight, 0.0) * (inn - out)
        row_value = rhs * row_inverse + row_bond * row_inverse * row_value
        rows[0, k] = row_value
        rows[1, k] = bond_here * row_inverse
        row_carry = (bond_here, row_inverse, row_value)
        bond_here = jnp.where(
            level_columns > kf + 1.0, 0.5 * (unpacked(1, k) + unpacked(1, under)), 0.0
        )
        col_inverse = pivot_step(col_bond, bond_here, col_inverse)
        col_value = unpacked(0, k) * col_inverse + col_bond * col_inverse * col_value
        columns[0, k] = col_value
        columns[1, k] = bond_here * col_inverse
        col_carry = (bond_here, col_inverse, col_value)
        mix = mix_h[k]
        mix_rim = rim(merged[tiles + k // PER_TILE], GROUP * (k % PER_TILE))
        near_mixes = near_all(mix, mix_rim, row_at(below, base_mix, k), row_at(above, base_mix, k))
        weight = [
            jnp.where(open_to > kf, 0.5 * (mix + near_mix), 0.0)
            for open_to, near_mix in zip(shallow, near_mixes)
        ]
        for n in range(4):
            weights[k, n] = weight[n]
        inverse, factor = factors[0, k], factors[1, k]
        values = list(values)
        for q in range(4):
            value, steps = steps_of(k, q, below_block, above_block)
            for n in range(4):
                value = value + weight[n] * steps[n]
            values[q] = value * inverse + factor * values[q]
            inside[k, q] = values[q]
        return (row_carry, col_carry, tuple(values))

    lax.fori_loop(
        0, depth, first, ((zero_rows,) * 3, (zero,) * 3, (zero,) * 4)
    )

    def second(n, carry):
        row_value, col_value, values, later_values = carry
        k = depth - 1 - n
        kf = k.astype(jnp.float32)
        block = pl.ds(pl.multiple_of(8 * k, 8), 8)
        below_block, above_block = below[block], above[block]
        row_value = rows[0, k] + rows[1, k] * row_value
        col_value = columns[0, k] + columns[1, k] * col_value
        values, later_values = list(values), list(later_values)
        factor = factors[2, k]
        first_steps, later_steps = [], []
        weight = [weights[k, n] for n in range(4)]
        for q in range(4):
            value = inside[k, q] + factor * values[q]
            inside[k, q] = value
            values[q] = value
            nears = near_all(
                value, rim(col_value, 4 * q), row_value[q : q + 1], row_value[4 + q : 5 + q]
            )
            steps = [near_value - value for near_value in nears]
            later_steps.append(steps)
            first_steps.append(steps_of(k, q, below_block, above_block)[1])
            for n in range(4):
                value = value + weight[n] * steps[n]
            if q < 2:
                later_values[q] = value * factors[3, k] + factors[4, k] * later_values[q]
                later[k, q] = later_values[q]
            else:
                adjoint[q - 2, k] = value
        total = zero
        for n in range(4):
            face = zero
            for t in range(2):
                face = face + first_steps[t][n] * later_steps[2 + t][n]
                face = face + later_steps[t][n] * first_steps[2 + t][n]
            total = total + jnp.where(shallow[n] > kf, face, 0.0)
        grad_h[k] = -0.5 * total
        return (row_value, col_value, tuple(values), tuple(later_values))

    lax.fori_loop(0, depth, second, (zero_rows, zero, (zero,) * 4, (zero,) * 2))
    copies = [
        pltpu.make_async_copy(source, target, sems.at[n])
        for n, (source, target) in enumerate(
            ((adjoint, adjoint_out), (grad_h, grad_h_out), (grad_v, grad_v_out))
        )
    ]
    copies[0].start()
    copies[1].start()

    def third(k, carry):
        face_above, later_above, inside_above, fields_above = carry
        inside_here = [inside[k, q] for q in range(4)]
        fields_here = [fields[k, 2 + t] for t in range(2)]
        later_here = [later[k, t] + factors[5, k] * later_above[t] for t in range(2)]
        total = zero
        for t in range(2):
            total = total + (inside_above[2 + t] - inside_here[2 + t]) * (
                inside_above[t] - inside_here[t]
            )
            total = total + (fields_above[t] - fields_here[t]) * (later_above[t] - later_here[t])
        face = jnp.where((k > 0) & (level > k.astype(jnp.float32)), total, 0.0)
        grad_v[jnp.maximum(k - 1, 0)] = -0.5 * (face + face_above)
        return face, tuple(later_here), tuple(inside_here), tuple(fields_here)

    face = lax.fori_loop(0, depth, third, (zero, (zero,) * 2, (zero,) * 4, (zero,) * 2))[0]
    grad_v[depth - 1] = -0.5 * face
    copies[2].start()
    for copy in copies:
        copy.wait()


def per_device(tracers, costate, mixing_h, mixing_v, levels, seam_code):
    depth = tracers.shape[1]
    tiles = depth // PER_TILE
    height = 10 * depth + 8
    params = pltpu.CompilerParams(vmem_limit_bytes=48 * 2**20)
    smem = pl.BlockSpec(memory_space=pltpu.SMEM)
    vmem = pl.BlockSpec(memory_space=pltpu.VMEM)
    hbm = pl.BlockSpec(memory_space=pltpu.HBM)
    tile = (ROWS, LANES)
    fields, factors, own, mix_h, mix_v, levels_here = pl.pallas_call(
        prepare,
        out_shape=(
            vmem_out(depth, 4, *tile),
            vmem_out(6, depth, *tile),
            vmem_out(2 * tiles, *tile),
            vmem_out(depth, *tile),
            vmem_out(depth, *tile),
            pltpu.VMEM(tile, jnp.int32),
        ),
        in_specs=[smem] + [hbm] * 5,
        scratch_shapes=[pltpu.SemaphoreType.DMA((7,))],
        compiler_params=params,
        name="prepare",
    )(seam_code, *(in_hbm(a) for a in (tracers, costate, mixing_h, mixing_v, levels)))

    count = lax.axis_size("ty")
    near_pairs = [(i, i ^ 1) for i in range(count)]
    far_pairs = [(i, (i + 1 if i % 2 else i - 1) % count) for i in range(count)]
    far = lax.ppermute(own, "ty", far_pairs)
    near = lax.ppermute(own, "ty", near_pairs)
    lower, upper, merged = pl.pallas_call(
        pack_rows,
        out_shape=(
            vmem_out(height, LANES),
            vmem_out(height, LANES),
            vmem_out(2 * tiles, *tile),
        ),
        compiler_params=params,
        name="pack_rows",
    )(*(in_vmem(a) for a in (near, far, fields, mix_h, mix_v, levels_here)))

    count = lax.axis_size("tx")
    from_below = lax.ppermute(upper, "tx", [(i, (i + 1) % count) for i in range(count)])
    from_above = lax.ppermute(lower, "tx", [(i, (i - 1) % count) for i in range(count)])
    block = jax.ShapeDtypeStruct(mixing_h.shape, jnp.float32)
    return pl.pallas_call(
        finish,
        out_shape=(jax.ShapeDtypeStruct(tracers.shape, jnp.float32), block, block),
        in_specs=[smem] + [vmem] * 10,
        out_specs=(hbm, hbm, hbm),
        scratch_shapes=[
            vmem_out(height, LANES),
            vmem_out(height, LANES),
            vmem_out(2, depth, 8, LANES),
            vmem_out(2, depth, *tile),
            vmem_out(2, tiles, *tile),
            vmem_out(depth, 4, *tile),
            vmem_out(depth, 4, *tile),
            vmem_out(depth, 2, *tile),
            vmem_out(2, depth, *tile),
            vmem_out(depth, *tile),
            vmem_out(depth, *tile),
            pltpu.SemaphoreType.DMA((3,)),
        ],
        compiler_params=params,
        name="finish",
    )(
        seam_code,
        *(
            in_vmem(a)
            for a in (
                from_below,
                from_above,
                lower,
                upper,
                merged,
                own,
                fields,
                factors,
                mix_h,
                levels_here,
            )
        ),
    )


def solution(mesh):
    placed = (
        P("members", None, "tx", "ty"),
        P("members", None, "tx", "ty"),
        P("members", "tx", "ty"),
        P("members", "tx", "ty"),
        P("tx", "ty"),
        P("ty"),
    )
    return jax.shard_map(
        per_device,
        mesh=mesh,
        in_specs=placed,
        out_specs=(
            P("members", None, "tx", "ty"),
            P("members", "tx", "ty"),
            P("members", "tx", "ty"),
        ),
        check_vma=False,
    )
```

```python
import jax
import jax.numpy as jnp
from jax import lax
from jax.experimental import pallas as pl
from jax.experimental.pallas import tpu as pltpu
from jax.sharding import PartitionSpec as P

LANES = 128
ROWS = 16
GROUP = 16
PER_TILE = LANES // GROUP


FILLER = 3


def in_vmem(array):
    return pltpu.with_memory_space_constraint(array, pltpu.VMEM)


def in_hbm(array):
    return pltpu.with_memory_space_constraint(array, pltpu.HBM)


def vmem_out(*shape):
    return pltpu.VMEM(shape, jnp.float32)


def iota(rows, dim):
    return lax.broadcasted_iota(jnp.int32, (rows, LANES), dim)


def roll(value, shift, axis):
    return pltpu.roll(value, shift % value.shape[axis], axis)


def fold(value):
    return jnp.where(iota(8, 0) < 4, value[:8], value[8:])


def east(value, halo):
    return jnp.where(iota(value.shape[0], 1) == LANES - 1, halo, roll(value, -1, 1))


def west(value, halo):
    return jnp.where(iota(value.shape[0], 1) == 0, halo, roll(value, 1, 1))


def rim(tile, base):
    return roll(tile, LANES - 2 - base, 1)


def crossed(tile):
    column = iota(tile.shape[0], 1) % 4
    return jnp.where(
        column == 1, roll(tile, -1, 1), jnp.where(column == 2, roll(tile, 1, 1), tile)
    )


def loop(count, body, carry, together=1):
    def several(n, carry):
        for m in range(together):
            carry = body(n * together + m, carry)
        return carry

    return lax.fori_loop(0, count // together, several, carry)


def north(value, beyond):
    sub = iota(8, 0)
    low, high = roll(value[:8], -1, 0), roll(value[8:], -1, 0)
    return jnp.concatenate([jnp.where(sub == 7, high, low), jnp.where(sub == 7, beyond, high)], axis=0)


def south(value, beyond):
    sub = iota(8, 0)
    low, high = roll(value[:8], 1, 0), roll(value[8:], 1, 0)
    return jnp.concatenate([jnp.where(sub == 0, beyond, low), jnp.where(sub == 0, low, high)], axis=0)


def bond(mix_v, level, k, depth):
    under = jnp.minimum(k + 1, depth - 1)
    return jnp.where(level > k + 1, 0.5 * (mix_v[k] + mix_v[under]), 0.0)


def prepare(
    seam,
    tracers,
    costate,
    mix_h_in,
    mix_v_in,
    levels_in,
    fields,
    factors,
    message,
    mix_h,
    mix_v,
    levels,
    sems,
):
    depth = mix_h.shape[0]
    copies = [
        pltpu.make_async_copy(source, target, sems.at[n])
        for n, (source, target) in enumerate(
            (
                (levels_in, levels),
                (mix_v_in, mix_v),
                (costate.at[0], fields.at[:, 2]),
                (costate.at[1], fields.at[:, 3]),
                (tracers.at[0], fields.at[:, 0]),
                (tracers.at[1], fields.at[:, 1]),
                (mix_h_in, mix_h),
            )
        )
    ]
    for copy in copies:
        copy.start()
    for copy in copies[:4]:
        copy.wait()
    level = levels[...]
    lane = iota(ROWS, 1)
    zero = jnp.zeros((ROWS, LANES), jnp.float32)

    def down(k, carry):
        bond_above, inverse, *values = carry
        bond_here = bond(mix_v, level, k, depth)
        inverse = 1.0 / (1.0 + bond_above + bond_here - bond_above * (bond_above * inverse))
        factor = bond_above * inverse
        factors[0, k] = inverse
        factors[1, k] = factor
        factors[2, k] = bond_here * inverse
        for t in range(2):
            values[t] = fields[k, 2 + t] * inverse + factor * values[t]
            fields[k, 2 + t] = values[t]
        return (bond_here, inverse, *values)

    loop(depth, down, (zero, zero, zero, zero), 4)
    for copy in copies[4:]:
        copy.wait()
    level_f = level.astype(jnp.float32)
    code = zero + seam[0].astype(jnp.float32)

    def up(n, carry):
        k = depth - 1 - n
        bond_here, inverse, *values = carry
        for t in range(2):
            values[t] = fields[k, 2 + t] + factors[2, k] * values[t]
            fields[k, 2 + t] = values[t]
        bond_above = jnp.where(k > 0, bond(mix_v, level, jnp.maximum(k - 1, 0), depth), 0.0)
        inverse = 1.0 / (1.0 + bond_above + bond_here - bond_here * (bond_here * inverse))
        factors[3, k] = inverse
        factors[4, k] = bond_here * inverse
        factors[5, k] = bond_above * inverse
        tile, base = k // PER_TILE, GROUP * (k % PER_TILE)
        place = lane // 4 - base // 4
        first = message[tile]
        for q, value in enumerate((fields[k, 0], fields[k, 1], values[0], values[1])):
            first = jnp.where(place == q, pltpu.roll(value, (base + 4 * q + 2) % LANES, 1), first)
        message[tile] = first
        second = message[depth // PER_TILE + tile]
        for q, value in enumerate((mix_h[k], mix_v[k], level_f)):
            second = jnp.where(place == q, pltpu.roll(value, (base + 4 * q + 2) % LANES, 1), second)
        message[depth // PER_TILE + tile] = jnp.where(place == FILLER, code, second)
        return (bond_above, inverse, *values)

    loop(depth, up, (zero, zero, zero, zero), 4)


def pack_rows(near, far, fields, mix_h, mix_v, levels, lower, upper, merged):
    depth = mix_h.shape[0]
    tiles = depth // PER_TILE
    place = lax.axis_index("ty")
    last = lax.axis_size("ty") - 1
    even = place % 2 == 0
    column = iota(ROWS, 1) % 4
    from_west = column < 2
    missing = ((place == 0) & from_west) | ((place == last) & jnp.logical_not(from_west))
    base_level = 10 * depth
    corners = []
    for j in range(2 * tiles):
        west_tile = jnp.where(even, far[j], near[j])
        east_tile = jnp.where(even, near[j], far[j])
        tile = jnp.where(from_west, west_tile, east_tile)
        if j >= tiles:
            tile = jnp.where(missing, 0.0, tile)
        merged[j] = crossed(tile)
        other = jnp.where(
            column == 0, roll(west_tile, -2, 1), jnp.where(column == 3, roll(east_tile, 2, 1), tile)
        )
        corners.append(crossed(fold(other)))
    sub = iota(8, 0)
    level_all = levels[...].astype(jnp.float32)
    level = fold(level_all)
    for target, row in ((lower, 0), (upper, 7)):
        block = jnp.zeros((8, LANES), jnp.float32)
        for n, value in enumerate([level, *corners]):
            block = jnp.where(sub == n, roll(value, n - row, 0), block)
        target[base_level : base_level + 8] = block

    def inner(value):
        return jnp.where(sub < 4, roll(value, -1, 0), roll(value, 1, 0))

    level_rim = rim(fold(merged[tiles]), 8)
    shallow = [
        jnp.minimum(level, near_level)
        for near_level in (east(level, level_rim), west(level, level_rim), inner(level))
    ]

    def row(k, _):
        tile, base = k // PER_TILE, GROUP * (k % PER_TILE)
        coefs = fold(merged[tiles + tile])
        mix = fold(mix_h[k])
        mix_rim = rim(coefs, base)
        mixes = (east(mix, mix_rim), west(mix, mix_rim), inner(mix))
        weights = [
            jnp.where(open_to > k.astype(jnp.float32), 0.5 * (mix + near_mix), 0.0)
            for open_to, near_mix in zip(shallow, mixes)
        ]
        packed = fold(merged[tile])
        low = jnp.zeros((8, LANES), jnp.float32)
        high = low
        for q in range(4):
            value = fold(fields[k, q])
            halo = rim(packed, base + 4 * q)
            part = value
            for near_value, weight in zip(
                (east(value, halo), west(value, halo), inner(value)), weights
            ):
                part = part + weight * (near_value - value)
            for n, thing in ((q, value), (4 + q, part)):
                low = jnp.where(sub == n, roll(thing, n, 0), low)
                high = jnp.where(sub == n, roll(thing, n - 7, 0), high)
        at = pl.ds(pl.multiple_of(8 * k, 8), 8)
        lower[at] = low
        upper[at] = high
        for n, array in enumerate((mix_h, mix_v)):
            at = pl.ds((8 + n) * depth + k, 1)
            lower[at] = array[k, :1]
            upper[at] = array[k, ROWS - 1 :]
        return 0

    loop(depth, row, 0, 4)


def finish(
    seam,
    from_below,
    from_above,
    lower,
    upper,
    merged,
    own,
    fields,
    factors,
    mix_h,
    levels,
    adjoint_out,
    grad_h_out,
    grad_v_out,
    below,
    above,
    rows,
    columns,
    packed,
    weights,
    inside,
    later,
    adjoint,
    grad_h,
    grad_v,
    sems,
):
    depth = mix_h.shape[0]
    tiles = depth // PER_TILE
    sub = iota(8, 0)
    lane = iota(ROWS, 1)
    place = lax.axis_index("tx")
    last = lax.axis_size("tx") - 1
    base_mix, base_v, base_level, base_corner = 8 * depth, 9 * depth, 10 * depth, 10 * depth + 1
    zero = jnp.zeros((ROWS, LANES), jnp.float32)
    zero_rows = jnp.zeros((8, LANES), jnp.float32)

    for source, target, edge in ((from_below, below, 0), (from_above, above, last)):
        turn = (seam[0] == 1) & (place == edge)

        @pl.when(turn)
        def _():
            back = LANES - 1 - iota(8, 1)
            for r in range(0, base_level, 8):
                target[r : r + 8] = jnp.take_along_axis(source[r : r + 8], back, axis=1)
            block = source[base_level : base_level + 8]
            target[base_level : base_level + 8] = jnp.where(
                sub < 1, jnp.take_along_axis(block, back, axis=1), block
            )

        @pl.when(jnp.logical_not(turn))
        def _():
            for r in range(0, base_level + 8, 8):
                target[r : r + 8] = source[r : r + 8]

    def both(a, b):
        return jnp.where(sub < 4, a, b)

    column = lane % 4

    def coefficient(value, n):
        kept = iota(value.shape[0], 1) % GROUP // 4 == n
        value = roll(jnp.where(kept, value, 0.0), -4 * n, 1)
        value = value + roll(value, 4, 1)
        return value + roll(value, 8, 1)

    def around(value, mine, below_row, above_row):
        return (
            mine,
            jnp.where(column == 1, roll(value, -2, 1), roll(value, 2, 1)),
            north(value, above_row),
            south(value, below_row),
        )

    turned = coefficient(merged[tiles, :8], FILLER)
    spot = iota(8, 1) % 4
    corner_rows = []
    for target, edge in ((below, 0), (above, last)):
        block = target[base_level : base_level + 8]
        swap = (place == edge) & (turned > 0.5)
        swapped = jnp.where(spot == 1, roll(block, -2, 1), roll(block, 2, 1))
        corner_rows.append(jnp.where(swap, swapped, block))
    for j in range(tiles):
        corner = [block[1 + j : 2 + j] for block in corner_rows]
        corner_coef = [block[1 + tiles + j : 2 + tiles + j] for block in corner_rows]
        level_k = (lane // GROUP + j * PER_TILE).astype(jnp.float32)
        (mix, mixes), (level, level_near) = [
            (
                coefficient(merged[tiles + j], n),
                around(
                    coefficient(merged[tiles + j], n),
                    coefficient(own[tiles + j], n),
                    *(coefficient(c, n) for c in corner_coef),
                ),
            )
            for n in (0, 2)
        ]
        value = merged[j]
        mixed = value
        for near_value, near_mix, near_level in zip(
            around(value, own[j], *corner), mixes, level_near
        ):
            weight = jnp.where(
                jnp.minimum(level, near_level) > level_k, 0.5 * (mix + near_mix), 0.0
            )
            mixed = mixed + weight * (near_value - value)
        packed[0, j] = mixed
        packed[1, j] = coefficient(merged[tiles + j], 1)
        if j == 0:
            level_columns = level

    def unpacked(n, k):
        return roll(packed[n, k // PER_TILE], LANES - GROUP * (k % PER_TILE), 1)

    level_out = both(below[base_level : base_level + 1], above[base_level : base_level + 1])
    level_in = both(lower[base_level : base_level + 1], upper[base_level : base_level + 1])
    level_face = jnp.minimum(level_out, level_in)
    level = levels[...].astype(jnp.float32)

    def near_all(value, halo, below_row, above_row):
        return (
            north(value, above_row),
            south(value, below_row),
            east(value, halo),
            west(value, halo),
        )

    shallow = [
        jnp.minimum(level, near_level)
        for near_level in near_all(
            level,
            rim(merged[tiles], 8),
            below[base_level : base_level + 1],
            above[base_level : base_level + 1],
        )
    ]

    def pivot_step(bond_above, bond_here, inverse):
        return 1.0 / (1.0 + bond_above + bond_here - bond_above * (bond_above * inverse))

    def row_at(ref, start, k):
        return ref[pl.ds(start + k, 1)]

    def mix_v_rows(k):
        return both(row_at(below, base_v, k), row_at(above, base_v, k))

    def steps_of(k, q, below_block, above_block):
        value = fields[k, q]
        halo = rim(merged[k // PER_TILE], GROUP * (k % PER_TILE) + 4 * q)
        nears = near_all(value, halo, below_block[q : q + 1], above_block[q : q + 1])
        return value, [n - value for n in nears]

    def first(k, carry):
        (row_bond, row_inverse, row_value), (col_bond, col_inverse, col_value), values = carry
        kf = k.astype(jnp.float32)
        block = pl.ds(pl.multiple_of(8 * k, 8), 8)
        below_block, above_block = below[block], above[block]
        under = jnp.minimum(k + 1, depth - 1)
        bond_here = jnp.where(
            level_out > kf + 1.0, 0.5 * (mix_v_rows(k) + mix_v_rows(under)), 0.0
        )
        row_inverse = pivot_step(row_bond, bond_here, row_inverse)
        out = both(below_block, roll(above_block, 4, 0))
        part = both(roll(below_block, 4, 0), above_block)
        inn = both(lower[block], roll(upper[block], 4, 0))
        weight = 0.5 * (
            both(row_at(below, base_mix, k), row_at(above, base_mix, k))
            + both(row_at(lower, base_mix, k), row_at(upper, base_mix, k))
        )
        rhs = part + jnp.where(level_face > kf, weight, 0.0) * (inn - out)
        row_value = rhs * row_inverse + row_bond * row_inverse * row_value
        rows[0, k] = row_value
        rows[1, k] = bond_here * row_inverse
        row_carry = (bond_here, row_inverse, row_value)
        bond_here = jnp.where(
            level_columns > kf + 1.0, 0.5 * (unpacked(1, k) + unpacked(1, under)), 0.0
        )
        col_inverse = pivot_step(col_bond, bond_here, col_inverse)
        col_value = unpacked(0, k) * col_inverse + col_bond * col_inverse * col_value
        columns[0, k] = col_value
        columns[1, k] = bond_here * col_inverse
        col_carry = (bond_here, col_inverse, col_value)
        mix = mix_h[k]
        mix_rim = rim(merged[tiles + k // PER_TILE], GROUP * (k % PER_TILE))
        near_mixes = near_all(mix, mix_rim, row_at(below, base_mix, k), row_at(above, base_mix, k))
        weight = [
            jnp.where(open_to > kf, 0.5 * (mix + near_mix), 0.0)
            for open_to, near_mix in zip(shallow, near_mixes)
        ]
        for n in range(4):
            weights[k, n] = weight[n]
        inverse, factor = factors[0, k], factors[1, k]
        values = list(values)
        for q in range(4):
            value, steps = steps_of(k, q, below_block, above_block)
            for n in range(4):
                value = value + weight[n] * steps[n]
            values[q] = value * inverse + factor * values[q]
            inside[k, q] = values[q]
        return (row_carry, col_carry, tuple(values))

    loop(depth, first, ((zero_rows,) * 3, (zero,) * 3, (zero,) * 4), 4)

    def second(n, carry):
        row_value, col_value, values, later_values = carry
        k = depth - 1 - n
        kf = k.astype(jnp.float32)
        block = pl.ds(pl.multiple_of(8 * k, 8), 8)
        below_block, above_block = below[block], above[block]
        row_value = rows[0, k] + rows[1, k] * row_value
        col_value = columns[0, k] + columns[1, k] * col_value
        values, later_values = list(values), list(later_values)
        factor = factors[2, k]
        first_steps, later_steps = [], []
        weight = [weights[k, n] for n in range(4)]
        for q in range(4):
            value = inside[k, q] + factor * values[q]
            inside[k, q] = value
            values[q] = value
            nears = near_all(
                value, rim(col_value, 4 * q), row_value[q : q + 1], row_value[4 + q : 5 + q]
            )
            steps = [near_value - value for near_value in nears]
            later_steps.append(steps)
            first_steps.append(steps_of(k, q, below_block, above_block)[1])
            for n in range(4):
                value = value + weight[n] * steps[n]
            if q < 2:
                later_values[q] = value * factors[3, k] + factors[4, k] * later_values[q]
                later[k, q] = later_values[q]
            else:
                adjoint[q - 2, k] = value
        total = zero
        for n in range(4):
            face = zero
            for t in range(2):
                face = face + first_steps[t][n] * later_steps[2 + t][n]
                face = face + later_steps[t][n] * first_steps[2 + t][n]
            total = total + jnp.where(shallow[n] > kf, face, 0.0)
        grad_h[k] = -0.5 * total
        return (row_value, col_value, tuple(values), tuple(later_values))

    loop(depth, second, (zero_rows, zero, (zero,) * 4, (zero,) * 2), 4)
    copies = [
        pltpu.make_async_copy(source, target, sems.at[n])
        for n, (source, target) in enumerate(
            ((adjoint, adjoint_out), (grad_h, grad_h_out), (grad_v, grad_v_out))
        )
    ]
    copies[0].start()
    copies[1].start()

    def third(k, carry):
        face_above, later_above, inside_above, fields_above = carry
        inside_here = [inside[k, q] for q in range(4)]
        fields_here = [fields[k, 2 + t] for t in range(2)]
        later_here = [later[k, t] + factors[5, k] * later_above[t] for t in range(2)]
        total = zero
        for t in range(2):
            total = total + (inside_above[2 + t] - inside_here[2 + t]) * (
                inside_above[t] - inside_here[t]
            )
            total = total + (fields_above[t] - fields_here[t]) * (later_above[t] - later_here[t])
        face = jnp.where((k > 0) & (level > k.astype(jnp.float32)), total, 0.0)
        grad_v[jnp.maximum(k - 1, 0)] = -0.5 * (face + face_above)
        return face, tuple(later_here), tuple(inside_here), tuple(fields_here)

    face = loop(depth, third, (zero, (zero,) * 2, (zero,) * 4, (zero,) * 2), 4)[0]
    grad_v[depth - 1] = -0.5 * face
    copies[2].start()
    for copy in copies:
        copy.wait()


def per_device(tracers, costate, mixing_h, mixing_v, levels, seam_code):
    depth = tracers.shape[1]
    tiles = depth // PER_TILE
    height = 10 * depth + 8
    params = pltpu.CompilerParams(vmem_limit_bytes=48 * 2**20)
    smem = pl.BlockSpec(memory_space=pltpu.SMEM)
    vmem = pl.BlockSpec(memory_space=pltpu.VMEM)
    hbm = pl.BlockSpec(memory_space=pltpu.HBM)
    tile = (ROWS, LANES)
    fields, factors, own, mix_h, mix_v, levels_here = pl.pallas_call(
        prepare,
        out_shape=(
            vmem_out(depth, 4, *tile),
            vmem_out(6, depth, *tile),
            vmem_out(2 * tiles, *tile),
            vmem_out(depth, *tile),
            vmem_out(depth, *tile),
            pltpu.VMEM(tile, jnp.int32),
        ),
        in_specs=[smem] + [hbm] * 5,
        scratch_shapes=[pltpu.SemaphoreType.DMA((7,))],
        compiler_params=params,
        name="prepare",
    )(seam_code, *(in_hbm(a) for a in (tracers, costate, mixing_h, mixing_v, levels)))

    count = lax.axis_size("ty")
    near_pairs = [(i, i ^ 1) for i in range(count)]
    far_pairs = [(i, (i + 1 if i % 2 else i - 1) % count) for i in range(count)]
    far = lax.ppermute(own, "ty", far_pairs)
    near = lax.ppermute(own, "ty", near_pairs)
    lower, upper, merged = pl.pallas_call(
        pack_rows,
        out_shape=(
            vmem_out(height, LANES),
            vmem_out(height, LANES),
            vmem_out(2 * tiles, *tile),
        ),
        compiler_params=params,
        name="pack_rows",
    )(*(in_vmem(a) for a in (near, far, fields, mix_h, mix_v, levels_here)))

    count = lax.axis_size("tx")
    from_below = lax.ppermute(upper, "tx", [(i, (i + 1) % count) for i in range(count)])
    from_above = lax.ppermute(lower, "tx", [(i, (i - 1) % count) for i in range(count)])
    block = jax.ShapeDtypeStruct(mixing_h.shape, jnp.float32)
    return pl.pallas_call(
        finish,
        out_shape=(jax.ShapeDtypeStruct(tracers.shape, jnp.float32), block, block),
        in_specs=[smem] + [vmem] * 10,
        out_specs=(hbm, hbm, hbm),
        scratch_shapes=[
            vmem_out(height, LANES),
            vmem_out(height, LANES),
            vmem_out(2, depth, 8, LANES),
            vmem_out(2, depth, *tile),
            vmem_out(2, tiles, *tile),
            vmem_out(depth, 4, *tile),
            vmem_out(depth, 4, *tile),
            vmem_out(depth, 2, *tile),
            vmem_out(2, depth, *tile),
            vmem_out(depth, *tile),
            vmem_out(depth, *tile),
            pltpu.SemaphoreType.DMA((3,)),
        ],
        compiler_params=params,
        name="finish",
    )(
        seam_code,
        *(
            in_vmem(a)
            for a in (
                from_below,
                from_above,
                lower,
                upper,
                merged,
                own,
                fields,
                factors,
                mix_h,
                levels_here,
            )
        ),
    )


def solution(mesh):
    placed = (
        P("members", None, "tx", "ty"),
        P("members", None, "tx", "ty"),
        P("members", "tx", "ty"),
        P("members", "tx", "ty"),
        P("tx", "ty"),
        P("ty"),
    )
    return jax.shard_map(
        per_device,
        mesh=mesh,
        in_specs=placed,
        out_specs=(
            P("members", None, "tx", "ty"),
            P("members", "tx", "ty"),
            P("members", "tx", "ty"),
        ),
        check_vma=False,
    )
```

```python
import jax
import jax.numpy as jnp
from jax import lax
from jax.experimental import pallas as pl
from jax.experimental.pallas import tpu as pltpu
from jax.sharding import PartitionSpec as P

LANES = 128
ROWS = 16
GROUP = 16
PER_TILE = LANES // GROUP


FILLER = 3


def in_vmem(array):
    return pltpu.with_memory_space_constraint(array, pltpu.VMEM)


def in_hbm(array):
    return pltpu.with_memory_space_constraint(array, pltpu.HBM)


def vmem_out(*shape):
    return pltpu.VMEM(shape, jnp.float32)


def iota(rows, dim):
    return lax.broadcasted_iota(jnp.int32, (rows, LANES), dim)


def roll(value, shift, axis):
    return pltpu.roll(value, shift % value.shape[axis], axis)


def fold(value):
    return jnp.where(iota(8, 0) < 4, value[:8], value[8:])


def east(value, halo):
    return jnp.where(iota(value.shape[0], 1) == LANES - 1, halo, roll(value, -1, 1))


def west(value, halo):
    return jnp.where(iota(value.shape[0], 1) == 0, halo, roll(value, 1, 1))


def rim(tile, base):
    return roll(tile, LANES - 2 - base, 1)


def crossed(tile):
    column = iota(tile.shape[0], 1) % 4
    return jnp.where(
        column == 1, roll(tile, -1, 1), jnp.where(column == 2, roll(tile, 1, 1), tile)
    )


def loop(count, body, carry):
    for n in range(count):
        carry = body(n, carry)
    return carry


def north(value, beyond):
    sub = iota(8, 0)
    low, high = roll(value[:8], -1, 0), roll(value[8:], -1, 0)
    return jnp.concatenate([jnp.where(sub == 7, high, low), jnp.where(sub == 7, beyond, high)], axis=0)


def south(value, beyond):
    sub = iota(8, 0)
    low, high = roll(value[:8], 1, 0), roll(value[8:], 1, 0)
    return jnp.concatenate([jnp.where(sub == 0, beyond, low), jnp.where(sub == 0, low, high)], axis=0)


def bond(mix_v, level, k, depth):
    if k in (-1, depth - 1):
        return jnp.zeros(level.shape, jnp.float32)
    return jnp.where(level > k + 1, 0.5 * (mix_v[k] + mix_v[k + 1]), 0.0)


def prepare(
    seam,
    tracers,
    costate,
    mix_h_in,
    mix_v_in,
    levels_in,
    fields,
    factors,
    message,
    mix_h,
    mix_v,
    levels,
    sems,
):
    depth = mix_h.shape[0]
    copies = [
        pltpu.make_async_copy(source, target, sems.at[n])
        for n, (source, target) in enumerate(
            (
                (levels_in, levels),
                (mix_v_in, mix_v),
                (costate.at[0], fields.at[:, 2]),
                (costate.at[1], fields.at[:, 3]),
                (tracers.at[0], fields.at[:, 0]),
                (tracers.at[1], fields.at[:, 1]),
                (mix_h_in, mix_h),
            )
        )
    ]
    for copy in copies:
        copy.start()
    for copy in copies[:4]:
        copy.wait()
    level = levels[...]
    lane = iota(ROWS, 1)
    zero = jnp.zeros((ROWS, LANES), jnp.float32)

    def down(k, carry):
        bond_above, inverse, *values = carry
        bond_here = bond(mix_v, level, k, depth)
        inverse = 1.0 / (1.0 + bond_above + bond_here - bond_above * (bond_above * inverse))
        factor = bond_above * inverse
        factors[0, k] = inverse
        factors[1, k] = factor
        factors[2, k] = bond_here * inverse
        for t in range(2):
            values[t] = fields[k, 2 + t] * inverse + factor * values[t]
            fields[k, 2 + t] = values[t]
        return (bond_here, inverse, *values)

    loop(depth, down, (zero, zero, zero, zero))
    for copy in copies[4:]:
        copy.wait()
    level_f = level.astype(jnp.float32)
    code = zero + seam[0].astype(jnp.float32)

    def up(n, carry):
        k = depth - 1 - n
        bond_here, inverse, *values = carry
        for t in range(2):
            values[t] = fields[k, 2 + t] + factors[2, k] * values[t]
            fields[k, 2 + t] = values[t]
        bond_above = bond(mix_v, level, k - 1, depth)
        inverse = 1.0 / (1.0 + bond_above + bond_here - bond_here * (bond_here * inverse))
        factors[3, k] = inverse
        factors[4, k] = bond_here * inverse
        factors[5, k] = bond_above * inverse
        tile, base = k // PER_TILE, GROUP * (k % PER_TILE)
        place = lane // 4 - base // 4
        first = message[tile]
        for q, value in enumerate((fields[k, 0], fields[k, 1], values[0], values[1])):
            first = jnp.where(place == q, roll(value, base + 4 * q + 2, 1), first)
        message[tile] = first
        second = message[depth // PER_TILE + tile]
        for q, value in enumerate((mix_h[k], mix_v[k], level_f)):
            second = jnp.where(place == q, roll(value, base + 4 * q + 2, 1), second)
        message[depth // PER_TILE + tile] = jnp.where(place == FILLER, code, second)
        return (bond_above, inverse, *values)

    loop(depth, up, (zero, zero, zero, zero))


def pack_rows(near, far, fields, mix_h, mix_v, levels, lower, upper, merged):
    depth = mix_h.shape[0]
    tiles = depth // PER_TILE
    place = lax.axis_index("ty")
    last = lax.axis_size("ty") - 1
    even = place % 2 == 0
    column = iota(ROWS, 1) % 4
    from_west = column < 2
    missing = ((place == 0) & from_west) | ((place == last) & jnp.logical_not(from_west))
    base_level = 10 * depth
    corners = []
    for j in range(2 * tiles):
        west_tile = jnp.where(even, far[j], near[j])
        east_tile = jnp.where(even, near[j], far[j])
        tile = jnp.where(from_west, west_tile, east_tile)
        if j >= tiles:
            tile = jnp.where(missing, 0.0, tile)
        merged[j] = crossed(tile)
        other = jnp.where(
            column == 0, roll(west_tile, -2, 1), jnp.where(column == 3, roll(east_tile, 2, 1), tile)
        )
        corners.append(crossed(fold(other)))
    sub = iota(8, 0)
    level_all = levels[...].astype(jnp.float32)
    level = fold(level_all)
    for target, row in ((lower, 0), (upper, 7)):
        block = jnp.zeros((8, LANES), jnp.float32)
        for n, value in enumerate([level, *corners]):
            block = jnp.where(sub == n, roll(value, n - row, 0), block)
        target[base_level : base_level + 8] = block

    def inner(value):
        return jnp.where(sub < 4, roll(value, -1, 0), roll(value, 1, 0))

    level_rim = rim(fold(merged[tiles]), 8)
    shallow = [
        jnp.minimum(level, near_level)
        for near_level in (east(level, level_rim), west(level, level_rim), inner(level))
    ]

    def row(k, _):
        tile, base = k // PER_TILE, GROUP * (k % PER_TILE)
        coefs = fold(merged[tiles + tile])
        mix = fold(mix_h[k])
        mix_rim = rim(coefs, base)
        mixes = (east(mix, mix_rim), west(mix, mix_rim), inner(mix))
        weights = [
            jnp.where(open_to > float(k), 0.5 * (mix + near_mix), 0.0)
            for open_to, near_mix in zip(shallow, mixes)
        ]
        packed = fold(merged[tile])
        low = jnp.zeros((8, LANES), jnp.float32)
        high = low
        for q in range(4):
            value = fold(fields[k, q])
            halo = rim(packed, base + 4 * q)
            part = value
            for near_value, weight in zip(
                (east(value, halo), west(value, halo), inner(value)), weights
            ):
                part = part + weight * (near_value - value)
            for n, thing in ((q, value), (4 + q, part)):
                low = jnp.where(sub == n, roll(thing, n, 0), low)
                high = jnp.where(sub == n, roll(thing, n - 7, 0), high)
        at = slice(8 * k, 8 * k + 8)
        lower[at] = low
        upper[at] = high
        for n, array in enumerate((mix_h, mix_v)):
            at = slice((8 + n) * depth + k, (8 + n) * depth + k + 1)
            lower[at] = array[k, :1]
            upper[at] = array[k, ROWS - 1 :]
        return 0

    loop(depth, row, 0)


def both(low, high):
    return jnp.where(iota(8, 0) < 4, low, high)


def coefficient(value, n):
    kept = iota(value.shape[0], 1) % GROUP // 4 == n
    value = roll(jnp.where(kept, value, 0.0), -4 * n, 1)
    value = value + roll(value, 4, 1)
    return value + roll(value, 8, 1)


def pivot(bond_above, bond_here, inverse):
    return 1.0 / (1.0 + bond_above + bond_here - bond_above * (bond_above * inverse))


def near_all(value, halo, below_row=0.0, above_row=0.0):
    return (
        north(value, above_row),
        south(value, below_row),
        east(value, halo),
        west(value, halo),
    )


def steps_of(fields, merged, k, q):
    value = fields[k, q]
    halo = rim(merged[k // PER_TILE], GROUP * (k % PER_TILE) + 4 * q)
    return value, [near - value for near in near_all(value, halo)]


def interior(
    merged,
    own,
    fields,
    factors,
    mix_h,
    levels,
    inside,
    columns,
    column_factors,
    weights,
    adjoint,
    grad_h,
    grad_v,
    packed,
    later,
):
    depth = mix_h.shape[0]
    tiles = depth // PER_TILE
    lane = iota(ROWS, 1)
    zero = jnp.zeros((ROWS, LANES), jnp.float32)

    column = lane % 4

    def around(value, mine):
        return (
            mine,
            jnp.where(column == 1, roll(value, -2, 1), roll(value, 2, 1)),
            north(value, 0.0),
            south(value, 0.0),
        )

    for j in range(tiles):
        level_k = (lane // GROUP + j * PER_TILE).astype(jnp.float32)
        here = [coefficient(merged[tiles + j], n) for n in range(3)]
        (mix, mixes), (level, level_near) = [
            (here[n], around(here[n], coefficient(own[tiles + j], n))) for n in (0, 2)
        ]
        value = merged[j]
        mixed = value
        for near, near_mix, near_level in zip(around(value, own[j]), mixes, level_near):
            weight = jnp.where(
                jnp.minimum(level, near_level) > level_k, 0.5 * (mix + near_mix), 0.0
            )
            mixed = mixed + weight * (near - value)
        packed[0, j] = mixed
        packed[1, j] = here[1]
        if j == 0:
            level_columns = level

    def unpacked(n, k):
        return roll(packed[n, k // PER_TILE], -GROUP * (k % PER_TILE), 1)

    level = levels[...].astype(jnp.float32)
    shallow = [jnp.minimum(level, near) for near in near_all(level, rim(merged[tiles], 8))]

    def first(k, carry):
        (col_bond, col_inverse, col_value), values = carry
        under = min(k + 1, depth - 1)
        bond_here = jnp.where(
            level_columns > k + 1.0, 0.5 * (unpacked(1, k) + unpacked(1, under)), 0.0
        )
        col_inverse = pivot(col_bond, bond_here, col_inverse)
        col_factor = col_bond * col_inverse
        col_value = unpacked(0, k) * col_inverse + col_factor * col_value
        columns[k] = col_value
        column_factors[0, k] = col_inverse
        column_factors[1, k] = col_factor
        column_factors[2, k] = bond_here * col_inverse
        mix = mix_h[k]
        mix_rim = rim(merged[tiles + k // PER_TILE], GROUP * (k % PER_TILE))
        weight = [
            jnp.where(open_to > float(k), 0.5 * (mix + near), 0.0)
            for open_to, near in zip(shallow, near_all(mix, mix_rim))
        ]
        for n in range(4):
            weights[k, n] = weight[n]
        inverse, factor = factors[0, k], factors[1, k]
        values = list(values)
        for q in range(4):
            value, steps = steps_of(fields, merged, k, q)
            for n in range(4):
                value = value + weight[n] * steps[n]
            values[q] = value * inverse + factor * values[q]
            inside[k, q] = values[q]
        return (bond_here, col_inverse, col_value), tuple(values)

    loop(depth, first, ((zero,) * 3, (zero,) * 4))

    def second(n, carry):
        col_value, values, later_values = carry
        k = depth - 1 - n
        col_value = columns[k] + column_factors[2, k] * col_value
        columns[k] = col_value
        values, later_values = list(values), list(later_values)
        first_steps, later_steps = [], []
        for q in range(4):
            value = inside[k, q] + factors[2, k] * values[q]
            inside[k, q] = value
            values[q] = value
            steps = [near - value for near in near_all(value, rim(col_value, 4 * q))]
            later_steps.append(steps)
            first_steps.append(steps_of(fields, merged, k, q)[1])
            for n in range(4):
                value = value + weights[k, n] * steps[n]
            if q < 2:
                later_values[q] = value * factors[3, k] + factors[4, k] * later_values[q]
                later[k, q] = later_values[q]
            else:
                adjoint[q - 2, k] = value
        total = zero
        for n in range(4):
            face = zero
            for t in range(2):
                face = face + first_steps[t][n] * later_steps[2 + t][n]
                face = face + later_steps[t][n] * first_steps[2 + t][n]
            total = total + jnp.where(shallow[n] > float(k), face, 0.0)
        grad_h[k] = -0.5 * total
        return col_value, tuple(values), tuple(later_values)

    loop(depth, second, (zero, (zero,) * 4, (zero,) * 2))
    vertical_gradient(
        depth,
        level,
        lambda i: factors[5, i],
        lambda k, q: inside[k, q],
        lambda k, t: fields[k, 2 + t],
        lambda k, t: later[k, t],
        grad_v,
    )


def vertical_gradient(depth, level, factor, inside, ahead, later, put):
    zero = jnp.zeros(level.shape, jnp.float32)
    face_above = zero
    later_above = inside_above = ahead_above = None
    for k in range(depth):
        inside_here = [inside(k, q) for q in range(4)]
        ahead_here = [ahead(k, t) for t in range(2)]
        later_here = [later(k, t) for t in range(2)]
        if k > 0:
            later_here = [later_here[t] + factor(k) * later_above[t] for t in range(2)]
            total = zero
            for t in range(2):
                total = total + (inside_above[2 + t] - inside_here[2 + t]) * (
                    inside_above[t] - inside_here[t]
                )
                total = total + (ahead_above[t] - ahead_here[t]) * (
                    later_above[t] - later_here[t]
                )
            face = jnp.where(level > float(k), total, 0.0)
            put[k - 1] = -0.5 * (face + face_above)
            face_above = face
        later_above, inside_above, ahead_above = later_here, inside_here, ahead_here
    put[depth - 1] = -0.5 * face_above


def finish(
    seam,
    from_below,
    from_above,
    lower,
    upper,
    merged,
    fields,
    factors,
    levels,
    inside,
    columns,
    column_factors,
    weights,
    adjoint_in,
    grad_h_in,
    grad_v_in,
    adjoint_out,
    grad_h_out,
    grad_v_out,
    below,
    above,
    out_rows,
    in_rows,
    corners,
    faces,
    later,
    edge_v,
    adjoint,
    grad_h,
    grad_v,
    sems,
):
    depth = fields.shape[0]
    tiles = depth // PER_TILE
    sub = iota(8, 0)
    lane = iota(8, 1)
    place = lax.axis_index("tx")
    last = lax.axis_size("tx") - 1
    base_mix, base_v, base_level = 8 * depth, 9 * depth, 10 * depth
    zero = jnp.zeros((8, LANES), jnp.float32)

    for source, target, edge in ((from_below, below, 0), (from_above, above, last)):
        turn = (seam[0] == 1) & (place == edge)

        @pl.when(turn)
        def _():
            back = LANES - 1 - lane
            for r in range(0, base_level, 8):
                target[r : r + 8] = jnp.take_along_axis(source[r : r + 8], back, axis=1)
            block = source[base_level : base_level + 8]
            target[base_level : base_level + 8] = jnp.where(
                sub < 1, jnp.take_along_axis(block, back, axis=1), block
            )

        @pl.when(jnp.logical_not(turn))
        def _():
            for r in range(0, base_level + 8, 8):
                target[r : r + 8] = source[r : r + 8]

    def ends(low, high, between=0.0):
        return jnp.where(sub == 0, low, jnp.where(sub == 7, high, between))

    folded = [fold(merged[j]) for j in range(2 * tiles)]
    turned = coefficient(folded[tiles], FILLER)
    corner_rows = []
    for target, edge in ((below, 0), (above, last)):
        block = target[base_level : base_level + 8]
        swap = (place == edge) & (turned[:1] > 0.5)
        swapped = jnp.where(lane % 4 == 1, roll(block, -2, 1), roll(block, 2, 1))
        corner_rows.append(jnp.where(swap, swapped, block))
    corner_flow = []
    for j in range(tiles):
        value, coefs = [
            ends(corner_rows[0][r : r + 1], corner_rows[1][r : r + 1])
            for r in (1 + j, 1 + tiles + j)
        ]
        level_k = (lane // GROUP + j * PER_TILE).astype(jnp.float32)
        mix, level = [
            (coefficient(coefs, n), coefficient(folded[tiles + j], n)) for n in (0, 2)
        ]
        weight = jnp.where(jnp.minimum(*level) > level_k, 0.5 * (mix[0] + mix[1]), 0.0)
        corner_flow.append(ends(1.0, 1.0) * weight * (value - folded[j]))

    def level_row(ref):
        return ref[base_level : base_level + 1]

    level_out = both(level_row(below), level_row(above))
    level_face = jnp.minimum(level_out, both(level_row(lower), level_row(upper)))

    def row_at(ref, start, k):
        return ref[start + k : start + k + 1]

    def mix_v_out(k):
        return both(row_at(below, base_v, k), row_at(above, base_v, k))

    def first(k, carry):
        bond_above, inverse, out_value, in_value, corner_value = carry
        block = slice(8 * k, 8 * k + 8)
        below_block, above_block = below[block], above[block]
        bond_here = jnp.where(
            level_out > k + 1.0, 0.5 * (mix_v_out(k) + mix_v_out(min(k + 1, depth - 1))), 0.0
        )
        inverse = pivot(bond_above, bond_here, inverse)
        out = both(below_block, roll(above_block, 4, 0))
        part = both(roll(below_block, 4, 0), above_block)
        inn = both(lower[block], roll(upper[block], 4, 0))
        mixes = 0.5 * (
            both(row_at(below, base_mix, k), row_at(above, base_mix, k))
            + both(row_at(lower, base_mix, k), row_at(upper, base_mix, k))
        )
        weight = jnp.where(level_face > float(k), mixes, 0.0)
        faces[k] = weight
        flow = weight * (inn - out)
        out_value = (part + flow) * inverse + bond_above * inverse * out_value
        out_rows[0, k] = out_value
        out_rows[1, k] = bond_here * inverse
        own = [both(factors[n, k, :1], factors[n, k, ROWS - 1 :]) for n in range(2)]
        in_value = own[1] * in_value - flow * own[0]
        in_rows[k] = in_value
        added = roll(corner_flow[k // PER_TILE], -GROUP * (k % PER_TILE), 1)
        corner_value = added * fold(column_factors[0, k]) + fold(column_factors[1, k]) * corner_value
        corners[k] = corner_value
        return bond_here, inverse, out_value, in_value, corner_value

    loop(depth, first, (zero,) * 5)

    level = fold(levels[...].astype(jnp.float32))
    level_rim = rim(folded[tiles], 8)

    def near_ends(value, halo, below_row, above_row):
        return (
            jnp.where(sub == 7, above_row, roll(value, -1, 0)),
            jnp.where(sub == 0, below_row, roll(value, 1, 0)),
            east(value, halo),
            west(value, halo),
        )

    shallow = [
        jnp.minimum(level, near)
        for near in near_ends(level, level_rim, level_row(below), level_row(above))
    ]

    def second(n, carry):
        out_value, in_value, corner_value, later_values = carry
        k = depth - 1 - n
        block = slice(8 * k, 8 * k + 8)
        below_block, above_block = below[block], above[block]
        out_value = out_rows[0, k] + out_rows[1, k] * out_value
        in_value = in_rows[k] + both(factors[2, k, :1], factors[2, k, ROWS - 1 :]) * in_value
        corner_value = corners[k] + fold(column_factors[2, k]) * corner_value
        column = fold(columns[k]) + corner_value
        face = faces[k]
        weight = [fold(weights[k, n]) for n in range(4)]
        weight[0] = jnp.where(sub == 7, face[4:5], weight[0])
        weight[1] = jnp.where(sub == 0, face[:1], weight[1])
        later_values = list(later_values)
        first_steps, later_steps = [], []
        for q in range(4):
            value = fold(fields[k, q])
            halo = rim(folded[k // PER_TILE], GROUP * (k % PER_TILE) + 4 * q)
            nears = near_ends(value, halo, below_block[q : q + 1], above_block[q : q + 1])
            first_steps.append([near - value for near in nears])
            value = fold(inside[k, q]) + ends(in_value[q : q + 1], in_value[4 + q : 5 + q])
            edge_v[k, q] = value
            nears = near_ends(
                value, rim(column, 4 * q), out_value[q : q + 1], out_value[4 + q : 5 + q]
            )
            steps = [near - value for near in nears]
            later_steps.append(steps)
            for n in range(4):
                value = value + weight[n] * steps[n]
            if q < 2:
                later_values[q] = (
                    value * fold(factors[3, k]) + fold(factors[4, k]) * later_values[q]
                )
                later[k, q] = later_values[q]
            else:
                merge_ends(adjoint, adjoint_in, (q - 2, k), value)
        total = zero
        for n in range(4):
            product = zero
            for t in range(2):
                product = product + first_steps[t][n] * later_steps[2 + t][n]
                product = product + later_steps[t][n] * first_steps[2 + t][n]
            total = total + jnp.where(shallow[n] > float(k), product, 0.0)
        merge_ends(grad_h, grad_h_in, (k,), -0.5 * total)
        return out_value, in_value, corner_value, tuple(later_values)

    def merge_ends(target, source, at, value):
        target[(*at, slice(0, 8))] = jnp.where(sub < 2, value, source[(*at, slice(0, 8))])
        target[(*at, slice(8, 16))] = jnp.where(sub < 6, source[(*at, slice(8, 16))], value)

    loop(depth, second, (zero, zero, zero, (zero, zero)))
    copies = [
        pltpu.make_async_copy(source, target, sems.at[n])
        for n, (source, target) in enumerate(
            ((adjoint, adjoint_out), (grad_h, grad_h_out), (grad_v, grad_v_out))
        )
    ]
    copies[0].start()
    copies[1].start()

    class Merged:
        def __setitem__(self, k, value):
            merge_ends(grad_v, grad_v_in, (k,), value)

    vertical_gradient(
        depth,
        level,
        lambda i: fold(factors[5, i]),
        lambda k, q: edge_v[k, q],
        lambda k, t: fold(fields[k, 2 + t]),
        lambda k, t: later[k, t],
        Merged(),
    )
    copies[2].start()
    for copy in copies:
        copy.wait()


def per_device(tracers, costate, mixing_h, mixing_v, levels, seam_code):
    depth = tracers.shape[1]
    tiles = depth // PER_TILE
    height = 10 * depth + 8
    params = pltpu.CompilerParams(vmem_limit_bytes=48 * 2**20)
    smem = pl.BlockSpec(memory_space=pltpu.SMEM)
    vmem = pl.BlockSpec(memory_space=pltpu.VMEM)
    hbm = pl.BlockSpec(memory_space=pltpu.HBM)
    tile = (ROWS, LANES)
    fields, factors, own, mix_h, mix_v, levels_here = pl.pallas_call(
        prepare,
        out_shape=(
            vmem_out(depth, 4, *tile),
            vmem_out(6, depth, *tile),
            vmem_out(2 * tiles, *tile),
            vmem_out(depth, *tile),
            vmem_out(depth, *tile),
            pltpu.VMEM(tile, jnp.int32),
        ),
        in_specs=[smem] + [hbm] * 5,
        scratch_shapes=[pltpu.SemaphoreType.DMA((7,))],
        compiler_params=params,
        name="prepare",
    )(seam_code, *(in_hbm(a) for a in (tracers, costate, mixing_h, mixing_v, levels)))

    count = lax.axis_size("ty")
    near_pairs = [(i, i ^ 1) for i in range(count)]
    far_pairs = [(i, (i + 1 if i % 2 else i - 1) % count) for i in range(count)]
    far = lax.ppermute(own, "ty", far_pairs)
    near = lax.ppermute(own, "ty", near_pairs)
    lower, upper, merged = pl.pallas_call(
        pack_rows,
        out_shape=(
            vmem_out(height, LANES),
            vmem_out(height, LANES),
            vmem_out(2 * tiles, *tile),
        ),
        compiler_params=params,
        name="pack_rows",
    )(*(in_vmem(a) for a in (near, far, fields, mix_h, mix_v, levels_here)))

    count = lax.axis_size("tx")
    from_below = lax.ppermute(upper, "tx", [(i, (i + 1) % count) for i in range(count)])
    from_above = lax.ppermute(lower, "tx", [(i, (i - 1) % count) for i in range(count)])
    inside = pl.pallas_call(
        interior,
        out_shape=(
            vmem_out(depth, 4, *tile),
            vmem_out(depth, *tile),
            vmem_out(3, depth, *tile),
            vmem_out(depth, 4, *tile),
            vmem_out(2, depth, *tile),
            vmem_out(depth, *tile),
            vmem_out(depth, *tile),
        ),
        scratch_shapes=[vmem_out(2, tiles, *tile), vmem_out(depth, 2, *tile)],
        compiler_params=params,
        cost_estimate=pl.CostEstimate(flops=20_000_000, bytes_accessed=8_000_000, transcendentals=0),
        name="interior",
    )(*(in_vmem(a) for a in (merged, own, fields, factors, mix_h, levels_here)))
    block = jax.ShapeDtypeStruct(mixing_h.shape, jnp.float32)
    row_block = (depth, 8, LANES)
    return pl.pallas_call(
        finish,
        out_shape=(jax.ShapeDtypeStruct(tracers.shape, jnp.float32), block, block),
        in_specs=[smem] + [vmem] * 15,
        out_specs=(hbm, hbm, hbm),
        scratch_shapes=[
            vmem_out(height, LANES),
            vmem_out(height, LANES),
            vmem_out(2, *row_block),
            vmem_out(*row_block),
            vmem_out(*row_block),
            vmem_out(*row_block),
            vmem_out(depth, 2, 8, LANES),
            vmem_out(depth, 4, 8, LANES),
            vmem_out(2, depth, *tile),
            vmem_out(depth, *tile),
            vmem_out(depth, *tile),
            pltpu.SemaphoreType.DMA((3,)),
        ],
        compiler_params=params,
        name="finish",
    )(
        seam_code,
        *(
            in_vmem(a)
            for a in (
                from_below,
                from_above,
                lower,
                upper,
                merged,
                fields,
                factors,
                levels_here,
                *inside,
            )
        ),
    )


def solution(mesh):
    placed = (
        P("members", None, "tx", "ty"),
        P("members", None, "tx", "ty"),
        P("members", "tx", "ty"),
        P("members", "tx", "ty"),
        P("tx", "ty"),
        P("ty"),
    )
    return jax.shard_map(
        per_device,
        mesh=mesh,
        in_specs=placed,
        out_specs=(
            P("members", None, "tx", "ty"),
            P("members", "tx", "ty"),
            P("members", "tx", "ty"),
        ),
        check_vma=False,
    )
```

```python
import jax
import jax.numpy as jnp
from jax import lax
from jax.experimental import pallas as pl
from jax.experimental.pallas import tpu as pltpu
from jax.sharding import PartitionSpec as P

LANES = 128
ROWS = 16
GROUP = 16
PER_TILE = LANES // GROUP


FILLER = 3


def in_vmem(array):
    return pltpu.with_memory_space_constraint(array, pltpu.VMEM)


def in_hbm(array):
    return pltpu.with_memory_space_constraint(array, pltpu.HBM)


def vmem_out(*shape):
    return pltpu.VMEM(shape, jnp.float32)


def iota(rows, dim):
    return lax.broadcasted_iota(jnp.int32, (rows, LANES), dim)


def roll(value, shift, axis):
    return pltpu.roll(value, shift % value.shape[axis], axis)


def fold(value):
    return jnp.where(iota(8, 0) < 4, value[:8], value[8:])


def east(value, halo):
    return jnp.where(iota(value.shape[0], 1) == LANES - 1, halo, roll(value, -1, 1))


def west(value, halo):
    return jnp.where(iota(value.shape[0], 1) == 0, halo, roll(value, 1, 1))


def rim(tile, base):
    return roll(tile, LANES - 2 - base, 1)


def crossed(tile):
    column = iota(tile.shape[0], 1) % 4
    return jnp.where(
        column == 1, roll(tile, -1, 1), jnp.where(column == 2, roll(tile, 1, 1), tile)
    )


def loop(count, body, carry):
    for n in range(count):
        carry = body(n, carry)
    return carry


def north(value, beyond):
    sub = iota(8, 0)
    low, high = roll(value[:8], -1, 0), roll(value[8:], -1, 0)
    return jnp.concatenate([jnp.where(sub == 7, high, low), jnp.where(sub == 7, beyond, high)], axis=0)


def south(value, beyond):
    sub = iota(8, 0)
    low, high = roll(value[:8], 1, 0), roll(value[8:], 1, 0)
    return jnp.concatenate([jnp.where(sub == 0, beyond, low), jnp.where(sub == 0, low, high)], axis=0)


def bond(mix_v, level, k, depth):
    if k in (-1, depth - 1):
        return jnp.zeros(level.shape, jnp.float32)
    return jnp.where(level > k + 1, 0.5 * (mix_v[k] + mix_v[k + 1]), 0.0)


def factorize(depth, level, mix_v, put):
    bond_above = jnp.zeros(level.shape, jnp.float32)
    inverse = bond_above
    for k in range(depth):
        bond_here = bond(mix_v, level, k, depth)
        inverse = pivot(bond_above, bond_here, inverse)
        put(k, inverse, bond_above * inverse, bond_here * inverse)
        bond_above = bond_here


def pivot(bond_above, bond_here, inverse):
    return 1.0 / (1.0 + bond_above + bond_here - bond_above * (bond_above * inverse))


def prepare(
    seam,
    tracers,
    costate,
    mix_h_in,
    mix_v_in,
    levels_in,
    fields,
    factors,
    message,
    mix_h,
    mix_v,
    levels,
    sems,
):
    depth = mix_h.shape[0]
    tiles = depth // PER_TILE
    copies = [
        pltpu.make_async_copy(source, target, sems.at[n])
        for n, (source, target) in enumerate(
            (
                (levels_in, levels),
                (mix_v_in, mix_v),
                (costate, fields.at[2:]),
                (tracers, fields.at[:2]),
                (mix_h_in, mix_h),
            )
        )
    ]
    for copy in copies:
        copy.start()
    for copy in copies[:2]:
        copy.wait()
    level = levels[...]
    place = iota(ROWS, 1) // 4
    zero = jnp.zeros((ROWS, LANES), jnp.float32)

    def put(k, *three):
        for n in range(3):
            factors[n, k] = three[n]

    factorize(depth, level, mix_v, put)
    seconds = [jnp.where(place % 4 == FILLER, seam[0].astype(jnp.float32), zero)] * tiles
    level_f = level.astype(jnp.float32)
    for k in range(depth):
        tile, base = k // PER_TILE, GROUP * (k % PER_TILE)
        for n, value in ((1, mix_v[k]), (2, level_f)):
            seconds[tile] = jnp.where(
                place == base // 4 + n, roll(value, base + 4 * n + 2, 1), seconds[tile]
            )
    for copy in copies[2:]:
        copy.wait()
    values = [zero, zero]
    for k in range(depth):
        for t in range(2):
            values[t] = fields[2 + t, k] * factors[0, k] + factors[1, k] * values[t]
            fields[2 + t, k] = values[t]
    firsts = [zero] * tiles
    values = [zero, zero]
    for k in range(depth - 1, -1, -1):
        tile, base = k // PER_TILE, GROUP * (k % PER_TILE)
        for t in range(2):
            values[t] = fields[2 + t, k] + factors[2, k] * values[t]
            fields[2 + t, k] = values[t]
        for q, value in enumerate((fields[0, k], fields[1, k], *values)):
            firsts[tile] = jnp.where(
                place == base // 4 + q, roll(value, base + 4 * q + 2, 1), firsts[tile]
            )
        seconds[tile] = jnp.where(
            place == base // 4, roll(mix_h[k], base + 2, 1), seconds[tile]
        )
    for tile in range(tiles):
        message[tile] = firsts[tile]
        message[tiles + tile] = seconds[tile]


def pack_rows(near, far, fields, mix_h, mix_v, levels, lower, upper, merged):
    depth = mix_h.shape[0]
    tiles = depth // PER_TILE
    place = lax.axis_index("ty")
    last = lax.axis_size("ty") - 1
    even = place % 2 == 0
    column = iota(ROWS, 1) % 4
    from_west = column < 2
    missing = ((place == 0) & from_west) | ((place == last) & jnp.logical_not(from_west))
    base_level = 10 * depth
    corners = []
    for j in range(2 * tiles):
        west_tile = jnp.where(even, far[j], near[j])
        east_tile = jnp.where(even, near[j], far[j])
        tile = jnp.where(from_west, west_tile, east_tile)
        if j >= tiles:
            tile = jnp.where(missing, 0.0, tile)
        merged[j] = crossed(tile)
        other = jnp.where(
            column == 0, roll(west_tile, -2, 1), jnp.where(column == 3, roll(east_tile, 2, 1), tile)
        )
        corners.append(crossed(fold(other)))
    sub = iota(8, 0)
    level_all = levels[...].astype(jnp.float32)
    level = fold(level_all)
    for target, row in ((lower, 0), (upper, 7)):
        block = jnp.zeros((8, LANES), jnp.float32)
        for n, value in enumerate([level, *corners]):
            block = jnp.where(sub == n, roll(value, n - row, 0), block)
        target[base_level : base_level + 8] = block

    def inner(value):
        return jnp.where(sub < 4, roll(value, -1, 0), roll(value, 1, 0))

    level_rim = rim(fold(merged[tiles]), 8)
    shallow = [
        jnp.minimum(level, near_level)
        for near_level in (east(level, level_rim), west(level, level_rim), inner(level))
    ]

    def row(k, _):
        tile, base = k // PER_TILE, GROUP * (k % PER_TILE)
        coefs = fold(merged[tiles + tile])
        mix = fold(mix_h[k])
        mix_rim = rim(coefs, base)
        mixes = (east(mix, mix_rim), west(mix, mix_rim), inner(mix))
        weights = [
            jnp.where(open_to > float(k), 0.5 * (mix + near_mix), 0.0)
            for open_to, near_mix in zip(shallow, mixes)
        ]
        packed = fold(merged[tile])
        low = jnp.zeros((8, LANES), jnp.float32)
        high = low
        for q in range(4):
            value = fold(fields[q, k])
            halo = rim(packed, base + 4 * q)
            part = value
            for near_value, weight in zip(
                (east(value, halo), west(value, halo), inner(value)), weights
            ):
                part = part + weight * (near_value - value)
            for n, thing in ((q, value), (4 + q, part)):
                low = jnp.where(sub == n, roll(thing, n, 0), low)
                high = jnp.where(sub == n, roll(thing, n - 7, 0), high)
        at = slice(8 * k, 8 * k + 8)
        lower[at] = low
        upper[at] = high
        for n, array in enumerate((mix_h, mix_v)):
            at = slice((8 + n) * depth + k, (8 + n) * depth + k + 1)
            lower[at] = array[k, :1]
            upper[at] = array[k, ROWS - 1 :]
        return 0

    loop(depth, row, 0)


def both(low, high):
    return jnp.where(iota(8, 0) < 4, low, high)


def coefficient(value, n):
    kept = iota(value.shape[0], 1) % GROUP // 4 == n
    value = roll(jnp.where(kept, value, 0.0), -4 * n, 1)
    value = value + roll(value, 4, 1)
    return value + roll(value, 8, 1)


def near_all(value, halo, below_row=0.0, above_row=0.0):
    return (
        north(value, above_row),
        south(value, below_row),
        east(value, halo),
        west(value, halo),
    )


def steps_of(fields, merged, k, q):
    value = fields[q, k]
    halo = rim(merged[k // PER_TILE], GROUP * (k % PER_TILE) + 4 * q)
    return value, [near - value for near in near_all(value, halo)]


EDGES = (
    "field",
    "mix",
    "inv_down",
    "up_down",
    "down_down",
    "inv_up",
    "up_up",
    "down_up",
    "inv_up_1",
    "up_up_1",
    "down_up_1",
    "to_east",
    "to_west",
    "to_inner",
    "cross_east",
    "cross_west",
    "cross_inner",
    "inside",
    "adjoint",
    "adjoint_1",
    "later",
    "ahead",
    "ahead_1",
    "grad_h",
    "grad_h_1",
    "grad_v_1",
    "column",
    "mix_column",
    "inv_column",
    "up_column",
    "down_column",
)
EDGE_LEVELS = ("own", "own_1", "east", "west", "inner", "column")


def exchange(value):
    return jnp.where(iota(8, 0) % 4 < 2, roll(value, -2, 0), roll(value, 2, 0))


def at_edges(rows, shift):
    sub = iota(8, 0) % 4
    out = roll(rows, LANES - 2 - shift, 1)
    for q in range(1, 4):
        out = jnp.where(sub == q, roll(rows, LANES - 2 - shift - 4 * q, 1), out)
    return out


def stacked(*rows):
    sub = iota(8, 0)
    out = jnp.zeros((8, LANES), jnp.float32)
    for n, row in enumerate(rows):
        if row is not None:
            out = jnp.where(sub == n, row, out)
    return out


def interior(
    merged,
    own,
    fields,
    factors,
    mix_h,
    mix_v,
    levels,
    lower,
    upper,
    edges,
    edge_levels,
    adjoint,
    grad_h,
    grad_v,
    inside,
    columns,
    column_factors,
    weights,
    packed,
    later,
    up_factors,
):
    depth = mix_h.shape[0]
    face_below = jnp.zeros((ROWS, LANES), jnp.float32)
    inverse = face_below
    level_int = levels[...]
    for k in range(depth - 1, -1, -1):
        face_above = bond(mix_v, level_int, k - 1, depth)
        inverse = pivot(face_below, face_above, inverse)
        up_factors[0, k] = inverse
        up_factors[1, k] = face_below * inverse
        up_factors[2, k] = face_above * inverse
        face_below = face_above
    tiles = depth // PER_TILE
    lane = iota(ROWS, 1)
    zero = jnp.zeros((ROWS, LANES), jnp.float32)

    column = lane % 4

    def around(value, mine):
        return (
            mine,
            jnp.where(column == 1, roll(value, -2, 1), roll(value, 2, 1)),
            north(value, 0.0),
            south(value, 0.0),
        )

    for j in range(tiles):
        level_k = (lane // GROUP + j * PER_TILE).astype(jnp.float32)
        here = [coefficient(merged[tiles + j], n) for n in range(3)]
        (mix, mixes), (level, level_near) = [
            (here[n], around(here[n], coefficient(own[tiles + j], n))) for n in (0, 2)
        ]
        value = merged[j]
        mixed = value
        for near, near_mix, near_level in zip(around(value, own[j]), mixes, level_near):
            weight = jnp.where(
                jnp.minimum(level, near_level) > level_k, 0.5 * (mix + near_mix), 0.0
            )
            mixed = mixed + weight * (near - value)
        packed[0, j] = mixed
        packed[1, j] = here[1]
        if j == 0:
            level_columns = level

    def unpacked(n, k):
        return roll(packed[n, k // PER_TILE], -GROUP * (k % PER_TILE), 1)

    level = levels[...].astype(jnp.float32)
    shallow = [jnp.minimum(level, near) for near in near_all(level, rim(merged[tiles], 8))]

    def first(k, carry):
        (col_bond, col_inverse, col_value), values = carry
        under = min(k + 1, depth - 1)
        bond_here = jnp.where(
            level_columns > k + 1.0, 0.5 * (unpacked(1, k) + unpacked(1, under)), 0.0
        )
        col_inverse = pivot(col_bond, bond_here, col_inverse)
        col_factor = col_bond * col_inverse
        col_value = unpacked(0, k) * col_inverse + col_factor * col_value
        columns[k] = col_value
        column_factors[0, k] = col_inverse
        column_factors[1, k] = col_factor
        column_factors[2, k] = bond_here * col_inverse
        mix = mix_h[k]
        mix_rim = rim(merged[tiles + k // PER_TILE], GROUP * (k % PER_TILE))
        weight = [
            jnp.where(open_to > float(k), 0.5 * (mix + near), 0.0)
            for open_to, near in zip(shallow, near_all(mix, mix_rim))
        ]
        for n in range(4):
            weights[k, n] = weight[n]
        inverse, factor = factors[0, k], factors[1, k]
        values = list(values)
        for q in range(4):
            value, steps = steps_of(fields, merged, k, q)
            for n in range(4):
                value = value + weight[n] * steps[n]
            values[q] = value * inverse + factor * values[q]
            inside[k, q] = values[q]
        return (bond_here, col_inverse, col_value), tuple(values)

    loop(depth, first, ((zero,) * 3, (zero,) * 4))

    def second(n, carry):
        col_value, values, later_values = carry
        k = depth - 1 - n
        col_value = columns[k] + column_factors[2, k] * col_value
        columns[k] = col_value
        values, later_values = list(values), list(later_values)
        first_steps, later_steps = [], []
        for q in range(4):
            value = inside[k, q] + factors[2, k] * values[q]
            inside[k, q] = value
            values[q] = value
            steps = [near - value for near in near_all(value, rim(col_value, 4 * q))]
            later_steps.append(steps)
            first_steps.append(steps_of(fields, merged, k, q)[1])
            for n in range(4):
                value = value + weights[k, n] * steps[n]
            if q < 2:
                later_values[q] = value * up_factors[0, k] + up_factors[1, k] * later_values[q]
                later[k, q] = later_values[q]
            else:
                adjoint[q - 2, k] = value
        total = zero
        for n in range(4):
            face = zero
            for t in range(2):
                face = face + first_steps[t][n] * later_steps[2 + t][n]
                face = face + later_steps[t][n] * first_steps[2 + t][n]
            total = total + jnp.where(shallow[n] > float(k), face, 0.0)
        grad_h[k] = -0.5 * total
        return col_value, tuple(values), tuple(later_values)

    loop(depth, second, (zero, (zero,) * 4, (zero,) * 2))

    face_above = zero
    for k in range(depth):
        if k > 0:
            total = zero
            for t in range(2):
                later[k, t] = later[k, t] + up_factors[2, k] * later[k - 1, t]
                total = total + (inside[k - 1, 2 + t] - inside[k, 2 + t]) * (
                    inside[k - 1, t] - inside[k, t]
                )
                total = total + (fields[2 + t, k - 1] - fields[2 + t, k]) * (
                    later[k - 1, t] - later[k, t]
                )
            face = jnp.where(level > float(k), total, 0.0)
            grad_v[k - 1] = -0.5 * (face + face_above)
            face_above = face
    grad_v[depth - 1] = -0.5 * face_above

    def ends(value, depth_in=0):
        return both(value[depth_in : depth_in + 1], value[ROWS - 1 - depth_in : ROWS - depth_in])

    coef_rows = ends(merged[tiles])
    for n, value in enumerate(
        (
            ends(level),
            ends(level, 1),
            ends(shallow[2]),
            ends(shallow[3]),
            both(shallow[0][:1], shallow[1][ROWS - 1 :]),
            rim(coef_rows, 8),
        )
    ):
        edge_levels[n] = value
    last_lane, first_lane = iota(8, 1) == LANES - 1, iota(8, 1) == 0

    def four(row, depth_in):
        low, high = depth_in, ROWS - 1 - depth_in
        return stacked(
            *(row(q, slice(low, low + 1)) for q in range(4)),
            *(row(q, slice(high, high + 1)) for q in range(4)),
        )

    for k in range(depth):
        j, i = divmod(k, PER_TILE)
        block = slice(8 * k, 8 * k + 8)
        field = both(lower[block], roll(upper[block], 4, 0))
        field_1 = four(lambda q, r: fields[q, k, r], 1)
        column = at_edges(ends(merged[j]), GROUP * i)
        steps = (
            jnp.where(last_lane, column, roll(field, -1, 1)) - field,
            jnp.where(first_lane, column, roll(field, 1, 1)) - field,
            field_1 - field,
        )

        def tracer(ref):
            return lambda q, r: ref[k, q, r] if q < 2 else None

        def result(q, r):
            return adjoint[q - 2, k, r] if q > 1 else None

        things = dict(
            field=field,
            mix=ends(mix_h[k]),
            to_east=ends(weights[k, 2]),
            to_west=ends(weights[k, 3]),
            to_inner=both(weights[k, 0, :1], weights[k, 1, ROWS - 1 :]),
            cross_east=exchange(steps[0]),
            cross_west=exchange(steps[1]),
            cross_inner=exchange(steps[2]),
            inside=four(lambda q, r: inside[k, q, r], 0),
            adjoint=four(result, 0),
            adjoint_1=four(result, 1),
            later=four(tracer(later), 0),
            ahead=roll(field, -2, 0),
            ahead_1=roll(field_1, -2, 0),
            grad_h=ends(grad_h[k]),
            grad_h_1=ends(grad_h[k], 1),
            grad_v_1=ends(grad_v[k], 1),
            column=column,
            mix_column=rim(ends(merged[tiles + j]), GROUP * i),
        )
        for n, name in enumerate(("inv", "up", "down")):
            things[name + "_down"] = ends(factors[n, k])
            things[name + "_up"] = ends(up_factors[n, k])
            things[name + "_up_1"] = ends(up_factors[n, k], 1)
            things[name + "_column"] = rim(ends(column_factors[n, k]), 0)
        for name, value in things.items():
            edges[EDGES.index(name), k] = value


def finish(
    seam,
    from_below,
    from_above,
    merged,
    edges,
    edge_levels,
    adjoint_in,
    grad_h_in,
    grad_v_in,
    adjoint_out,
    grad_h_out,
    grad_v_out,
    below,
    above,
    rows,
    later,
    adjoint,
    grad_h,
    grad_v,
    sems,
):
    depth, tiles = grad_h.shape[0], grad_h.shape[0] // PER_TILE
    sub = iota(8, 0)
    lane = iota(8, 1)
    place = lax.axis_index("tx")
    last = lax.axis_size("tx") - 1
    base_mix, base_v, base_level = 8 * depth, 9 * depth, 10 * depth
    zero = jnp.zeros((8, LANES), jnp.float32)

    def edge(name, k):
        return edges[EDGES.index(name), k]

    def edge_level(name):
        return edge_levels[EDGE_LEVELS.index(name)]

    for source, target, border in ((from_below, below, 0), (from_above, above, last)):
        turn = (seam[0] == 1) & (place == border)

        @pl.when(turn)
        def _():
            back = LANES - 1 - lane
            for r in range(0, base_level, 8):
                target[r : r + 8] = jnp.take_along_axis(source[r : r + 8], back, axis=1)
            block = source[base_level : base_level + 8]
            target[base_level : base_level + 8] = jnp.where(
                sub < 1, jnp.take_along_axis(block, back, axis=1), block
            )

        @pl.when(jnp.logical_not(turn))
        def _():
            for r in range(0, base_level + 8, 8):
                target[r : r + 8] = source[r : r + 8]

    for k in range(depth):
        for t in range(2):
            adjoint[t, k] = adjoint_in[t, k]
        grad_h[k] = grad_h_in[k]
        grad_v[k] = grad_v_in[k]

    turned = coefficient(merged[tiles, :8], FILLER)[:1]
    corners = []
    for target, border in ((below, 0), (above, last)):
        block = target[base_level : base_level + 8]
        swapped = jnp.where(lane % 4 == 1, roll(block, -2, 1), roll(block, 2, 1))
        corners.append(jnp.where((place == border) & (turned > 0.5), swapped, block))

    def corner(r):
        return both(corners[0][r : r + 1], corners[1][r : r + 1])

    def outer(start, k=0):
        at = slice(start + k, start + k + 1)
        return both(below[at], above[at])

    level_out = outer(base_level)
    level_face = jnp.minimum(level_out, edge_level("own"))
    level_corner = jnp.minimum(rim(corner(1 + tiles), 8), edge_level("column"))

    bond_above = inverse = out_value = added = column_added = zero
    flows = []
    for k in range(depth):
        j, i = divmod(k, PER_TILE)
        block = slice(8 * k, 8 * k + 8)
        below_block, above_block = below[block], above[block]
        bond_here = jnp.where(
            level_out > k + 1.0,
            0.5 * (outer(base_v, k) + outer(base_v, min(k + 1, depth - 1))),
            0.0,
        )
        inverse = pivot(bond_above, bond_here, inverse)
        out = both(below_block, roll(above_block, 4, 0))
        part = both(roll(below_block, 4, 0), above_block)
        step = out - edge("field", k)
        weight = jnp.where(level_face > float(k), 0.5 * (outer(base_mix, k) + edge("mix", k)), 0.0)
        flow = weight * step
        out_value = (part - flow) * inverse + bond_above * inverse * out_value
        added = flow * edge("inv_down", k) + edge("up_down", k) * added
        weight_corner = jnp.where(
            level_corner > float(k),
            0.5 * (rim(corner(1 + tiles + j), GROUP * i) + edge("mix_column", k)),
            0.0,
        )
        step_corner = at_edges(corner(1 + j), GROUP * i) - edge("column", k)
        column_added = (
            weight_corner * step_corner * edge("inv_column", k)
            + edge("up_column", k) * column_added
        )
        rows[0, k] = out_value
        rows[1, k] = bond_here * inverse
        rows[2, k] = added
        rows[3, k] = column_added
        rows[4, k] = weight
        rows[5, k] = exchange(step)
        bond_above = bond_here

    out_value = added = column_added = later_0 = later_1 = zero
    for k in range(depth - 1, -1, -1):
        out_value = rows[0, k] + rows[1, k] * out_value
        added = rows[2, k] + edge("down_down", k) * added
        column_added = rows[3, k] + edge("down_column", k) * column_added
        value = edge("inside", k) + added
        rows[0, k] = value
        east_step = jnp.where(lane == LANES - 1, column_added, roll(added, -1, 1)) - added
        west_step = jnp.where(lane == 0, column_added, roll(added, 1, 1)) - added
        out_step = out_value - value
        inner_flow = edge("to_inner", k) * added
        change = (
            added
            + edge("to_east", k) * east_step
            + edge("to_west", k) * west_step
            - inner_flow
            + rows[4, k] * out_step
        )
        later_0 = change * edge("inv_up", k) + edge("up_up", k) * later_0
        later_1 = inner_flow * edge("inv_up_1", k) + edge("up_up_1", k) * later_1
        later[0, k] = later_0
        later[1, k] = later_1
        result = edge("adjoint", k) + change
        result_1 = edge("adjoint_1", k) + inner_flow
        for t in range(2):
            for at, source, row in (
                (0, result, 2),
                (ROWS - 1, result, 6),
                (1, result_1, 2),
                (ROWS - 2, result_1, 6),
            ):
                adjoint[t, k, at : at + 1] = source[row + t : row + t + 1]
        product_1 = jnp.where(
            edge_level("inner") > float(k), -edge("cross_inner", k) * added, 0.0
        )
        product = (
            product_1
            + jnp.where(edge_level("east") > float(k), edge("cross_east", k) * east_step, 0.0)
            + jnp.where(edge_level("west") > float(k), edge("cross_west", k) * west_step, 0.0)
            + jnp.where(level_face > float(k), rows[5, k] * out_step, 0.0)
        )
        for name, inset, value in (("grad_h", 0, product), ("grad_h_1", 1, product_1)):
            value = value + roll(value, -1, 0)
            value = edge(name, k) - 0.5 * (value + roll(value, -2, 0))
            grad_h[k, inset : inset + 1] = value[:1]
            grad_h[k, ROWS - 1 - inset : ROWS - inset] = value[4:5]

    copies = [
        pltpu.make_async_copy(source, target, sems.at[n])
        for n, (source, target) in enumerate(
            ((adjoint, adjoint_out), (grad_h, grad_h_out), (grad_v, grad_v_out))
        )
    ]
    copies[0].start()
    copies[1].start()

    face_0 = face_1 = later_0 = later_1 = zero
    for k in range(depth + 1):
        if k < depth:
            above_0, above_1 = later_0, later_1
            later_0 = later[0, k] + edge("down_up", k) * later_0
            later_1 = later[1, k] + edge("down_up_1", k) * later_1
        if k == 0:
            continue
        next_0 = next_1 = zero
        if k < depth:
            step = rows[0, k - 1] - rows[0, k]
            next_0 = step * roll(step, -2, 0) + (edge("ahead", k - 1) - edge("ahead", k)) * (
                edge("later", k - 1) + above_0 - edge("later", k) - later_0
            )
            next_1 = (edge("ahead_1", k - 1) - edge("ahead_1", k)) * (above_1 - later_1)
            next_0 = jnp.where(
                edge_level("own") > float(k), next_0 + roll(next_0, -1, 0), 0.0
            )
            next_1 = jnp.where(
                edge_level("own_1") > float(k), next_1 + roll(next_1, -1, 0), 0.0
            )
        value_0 = -0.5 * (face_0 + next_0)
        value_1 = edge("grad_v_1", k - 1) - 0.5 * (face_1 + next_1)
        for inset, value in ((0, value_0), (1, value_1)):
            grad_v[k - 1, inset : inset + 1] = value[:1]
            grad_v[k - 1, ROWS - 1 - inset : ROWS - inset] = value[4:5]
        face_0, face_1 = next_0, next_1
    copies[2].start()
    for copy in copies:
        copy.wait()


def per_device(tracers, costate, mixing_h, mixing_v, levels, seam_code):
    depth = tracers.shape[1]
    tiles = depth // PER_TILE
    height = 10 * depth + 8
    params = pltpu.CompilerParams(vmem_limit_bytes=48 * 2**20)
    smem = pl.BlockSpec(memory_space=pltpu.SMEM)
    vmem = pl.BlockSpec(memory_space=pltpu.VMEM)
    hbm = pl.BlockSpec(memory_space=pltpu.HBM)
    tile = (ROWS, LANES)
    fields, factors, own, mix_h, mix_v, levels_here = pl.pallas_call(
        prepare,
        out_shape=(
            vmem_out(4, depth, *tile),
            vmem_out(3, depth, *tile),
            vmem_out(2 * tiles, *tile),
            vmem_out(depth, *tile),
            vmem_out(depth, *tile),
            pltpu.VMEM(tile, jnp.int32),
        ),
        in_specs=[smem] + [hbm] * 5,
        scratch_shapes=[pltpu.SemaphoreType.DMA((5,))],
        compiler_params=params,
        name="prepare",
    )(seam_code, *(in_hbm(a) for a in (tracers, costate, mixing_h, mixing_v, levels)))

    count = lax.axis_size("ty")
    near_pairs = [(i, i ^ 1) for i in range(count)]
    far_pairs = [(i, (i + 1 if i % 2 else i - 1) % count) for i in range(count)]
    far = lax.ppermute(own, "ty", far_pairs)
    near = lax.ppermute(own, "ty", near_pairs)
    lower, upper, merged = pl.pallas_call(
        pack_rows,
        out_shape=(
            vmem_out(height, LANES),
            vmem_out(height, LANES),
            vmem_out(2 * tiles, *tile),
        ),
        compiler_params=params,
        name="pack_rows",
    )(*(in_vmem(a) for a in (near, far, fields, mix_h, mix_v, levels_here)))

    count = lax.axis_size("tx")
    from_below = lax.ppermute(upper, "tx", [(i, (i + 1) % count) for i in range(count)])
    from_above = lax.ppermute(lower, "tx", [(i, (i - 1) % count) for i in range(count)])
    row_block = (depth, 8, LANES)
    inner = pl.pallas_call(
        interior,
        out_shape=(
            vmem_out(len(EDGES), *row_block),
            vmem_out(len(EDGE_LEVELS), 8, LANES),
            vmem_out(2, depth, *tile),
            vmem_out(depth, *tile),
            vmem_out(depth, *tile),
        ),
        scratch_shapes=[
            vmem_out(depth, 4, *tile),
            vmem_out(depth, *tile),
            vmem_out(3, depth, *tile),
            vmem_out(depth, 4, *tile),
            vmem_out(2, tiles, *tile),
            vmem_out(depth, 2, *tile),
            vmem_out(3, depth, *tile),
        ],
        compiler_params=params,
        cost_estimate=pl.CostEstimate(flops=20_000_000, bytes_accessed=8_000_000, transcendentals=0),
        name="interior",
    )(
        *(
            in_vmem(a)
            for a in (merged, own, fields, factors, mix_h, mix_v, levels_here, lower, upper)
        )
    )
    block = jax.ShapeDtypeStruct(mixing_h.shape, jnp.float32)
    return pl.pallas_call(
        finish,
        out_shape=(jax.ShapeDtypeStruct(tracers.shape, jnp.float32), block, block),
        in_specs=[smem] + [vmem] * 8,
        out_specs=(hbm, hbm, hbm),
        scratch_shapes=[
            vmem_out(height, LANES),
            vmem_out(height, LANES),
            vmem_out(6, *row_block),
            vmem_out(2, *row_block),
            vmem_out(2, depth, *tile),
            vmem_out(depth, *tile),
            vmem_out(depth, *tile),
            pltpu.SemaphoreType.DMA((3,)),
        ],
        compiler_params=params,
        name="finish",
    )(seam_code, *(in_vmem(a) for a in (from_below, from_above, merged, *inner)))


def solution(mesh):
    placed = (
        P("members", None, "tx", "ty"),
        P("members", None, "tx", "ty"),
        P("members", "tx", "ty"),
        P("members", "tx", "ty"),
        P("tx", "ty"),
        P("ty"),
    )
    return jax.shard_map(
        per_device,
        mesh=mesh,
        in_specs=placed,
        out_specs=(
            P("members", None, "tx", "ty"),
            P("members", "tx", "ty"),
            P("members", "tx", "ty"),
        ),
        check_vma=False,
    )
```

```python
import jax
import jax.numpy as jnp
from jax import lax
from jax.experimental import pallas as pl
from jax.experimental.pallas import tpu as pltpu
from jax.sharding import PartitionSpec as P

LANES = 128
ROWS = 16
GROUP = 16
PER_TILE = LANES // GROUP


FILLER = 3


def in_vmem(array):
    return pltpu.with_memory_space_constraint(array, pltpu.VMEM)


def in_hbm(array):
    return pltpu.with_memory_space_constraint(array, pltpu.HBM)


def vmem_out(*shape):
    return pltpu.VMEM(shape, jnp.float32)


def iota(rows, dim):
    return lax.broadcasted_iota(jnp.int32, (rows, LANES), dim)


def roll(value, shift, axis):
    return pltpu.roll(value, shift % value.shape[axis], axis)


def fold(value):
    return jnp.where(iota(8, 0) < 4, value[:8], value[8:])


def east(value, halo):
    return jnp.where(iota(value.shape[0], 1) == LANES - 1, halo, roll(value, -1, 1))


def west(value, halo):
    return jnp.where(iota(value.shape[0], 1) == 0, halo, roll(value, 1, 1))


def rim(tile, base):
    return roll(tile, LANES - 2 - base, 1)


def crossed(tile):
    column = iota(tile.shape[0], 1) % 4
    return jnp.where(
        column == 1, roll(tile, -1, 1), jnp.where(column == 2, roll(tile, 1, 1), tile)
    )


def loop(count, body, carry):
    for n in range(count):
        carry = body(n, carry)
    return carry


def north(value, beyond):
    sub = iota(8, 0)
    low, high = roll(value[:8], -1, 0), roll(value[8:], -1, 0)
    return jnp.concatenate([jnp.where(sub == 7, high, low), jnp.where(sub == 7, beyond, high)], axis=0)


def south(value, beyond):
    sub = iota(8, 0)
    low, high = roll(value[:8], 1, 0), roll(value[8:], 1, 0)
    return jnp.concatenate([jnp.where(sub == 0, beyond, low), jnp.where(sub == 0, low, high)], axis=0)


def bond(mix_v, level, k, depth):
    if k in (-1, depth - 1):
        return jnp.zeros(level.shape, jnp.float32)
    return jnp.where(level > k + 1, 0.5 * (mix_v[k] + mix_v[k + 1]), 0.0)


def factorize(depth, level, mix_v, put):
    bond_above = jnp.zeros(level.shape, jnp.float32)
    inverse = bond_above
    for k in range(depth):
        bond_here = bond(mix_v, level, k, depth)
        inverse = pivot(bond_above, bond_here, inverse)
        put(k, inverse, bond_above * inverse, bond_here * inverse)
        bond_above = bond_here


def pivot(bond_above, bond_here, inverse):
    return 1.0 / (1.0 + bond_above + bond_here - bond_above * (bond_above * inverse))


def prepare(
    seam,
    tracers,
    costate,
    mix_h_in,
    mix_v_in,
    levels_in,
    fields,
    factors,
    message,
    mix_h,
    mix_v,
    levels,
    sems,
):
    depth = mix_h.shape[0]
    tiles = depth // PER_TILE
    copies = [
        pltpu.make_async_copy(source, target, sems.at[n])
        for n, (source, target) in enumerate(
            (
                (levels_in, levels),
                (mix_v_in, mix_v),
                (costate, fields.at[2:]),
                (tracers, fields.at[:2]),
                (mix_h_in, mix_h),
            )
        )
    ]
    for copy in copies:
        copy.start()
    for copy in copies[:2]:
        copy.wait()
    level = levels[...]
    place = iota(ROWS, 1) // 4
    zero = jnp.zeros((ROWS, LANES), jnp.float32)

    def put(k, *three):
        for n in range(3):
            factors[n, k] = three[n]

    factorize(depth, level, mix_v, put)
    seconds = [jnp.where(place % 4 == FILLER, seam[0].astype(jnp.float32), zero)] * tiles
    level_f = level.astype(jnp.float32)
    for k in range(depth):
        tile, base = k // PER_TILE, GROUP * (k % PER_TILE)
        for n, value in ((1, mix_v[k]), (2, level_f)):
            seconds[tile] = jnp.where(
                place == base // 4 + n, roll(value, base + 4 * n + 2, 1), seconds[tile]
            )
    for copy in copies[2:]:
        copy.wait()
    values = [zero, zero]
    for k in range(depth):
        for t in range(2):
            values[t] = fields[2 + t, k] * factors[0, k] + factors[1, k] * values[t]
            fields[2 + t, k] = values[t]
    firsts = [zero] * tiles
    values = [zero, zero]
    for k in range(depth - 1, -1, -1):
        tile, base = k // PER_TILE, GROUP * (k % PER_TILE)
        for t in range(2):
            values[t] = fields[2 + t, k] + factors[2, k] * values[t]
            fields[2 + t, k] = values[t]
        for q, value in enumerate((fields[0, k], fields[1, k], *values)):
            firsts[tile] = jnp.where(
                place == base // 4 + q, roll(value, base + 4 * q + 2, 1), firsts[tile]
            )
        seconds[tile] = jnp.where(
            place == base // 4, roll(mix_h[k], base + 2, 1), seconds[tile]
        )
    for tile in range(tiles):
        message[tile] = firsts[tile]
        message[tiles + tile] = seconds[tile]


def row_blocks(depth, row, half, weights_of, halo_of, inner_shift, fields, mix_h, mix_v, target):
    sub = iota(8, 0)
    at = row % 8
    for k in range(depth):
        weights = weights_of(k)
        block = jnp.zeros((8, LANES), jnp.float32)
        for q in range(4):
            value = fields[q, k, half]
            halo = halo_of(k, q)
            part = value
            for near, weight in zip(
                (east(value, halo), west(value, halo), roll(value, inner_shift, 0)), weights
            ):
                part = part + weight * (near - value)
            for n, thing in ((q, value), (4 + q, part)):
                block = jnp.where(sub == n, roll(thing, n - at, 0), block)
        target[8 * k : 8 * k + 8] = block
        for n, array in enumerate((mix_h, mix_v)):
            start = (8 + n) * depth + k
            target[start : start + 1] = array[k, row : row + 1]


def pack_up(fields, mix_h, mix_v, levels, upper):
    depth = mix_h.shape[0]
    half = slice(8, 16)
    level = levels[half].astype(jnp.float32)
    shallow = [
        jnp.minimum(level, near)
        for near in (east(level, 0.0), west(level, 0.0), roll(level, 1, 0))
    ]

    def weights_of(k):
        mix = mix_h[k, half]
        return [
            jnp.where(open_to > float(k), 0.5 * (mix + near), 0.0)
            for open_to, near in zip(shallow, (east(mix, 0.0), west(mix, 0.0), roll(mix, 1, 0)))
        ]

    row_blocks(depth, 15, half, weights_of, lambda k, q: 0.0, 1, fields, mix_h, mix_v, upper)
    upper[10 * depth : 10 * depth + 8] = stacked(level[7:])


def pack_sides(near, far, own, merged, corner, rest):
    tiles = near.shape[0] // 2
    place = lax.axis_index("ty")
    last = lax.axis_size("ty") - 1
    even = place % 2 == 0
    column = iota(ROWS, 1) % 4
    from_west = column < 2
    missing = ((place == 0) & from_west) | ((place == last) & jnp.logical_not(from_west))
    corners = []
    for j in range(2 * tiles):
        west_tile = jnp.where(even, far[j], near[j])
        east_tile = jnp.where(even, near[j], far[j])
        tile = jnp.where(from_west, west_tile, east_tile)
        if j >= tiles:
            tile = jnp.where(missing, 0.0, tile)
        merged[j] = crossed(tile)
        corners.append(
            crossed(
                fold(
                    jnp.where(
                        column == 0,
                        roll(west_tile, -2, 1),
                        jnp.where(column == 3, roll(east_tile, 2, 1), tile),
                    )
                )
            )
        )
    flows = []
    lane = iota(1, 1)
    for j in range(tiles):
        level_k = (lane // GROUP + j * PER_TILE).astype(jnp.float32)
        mix, level = [
            [coefficient(ref[tiles + j, ROWS - 1 :], n) for ref in (merged, own)] for n in (0, 2)
        ]
        weight = jnp.where(jnp.minimum(*level) > level_k, 0.5 * (mix[0] + mix[1]), 0.0)
        flows.append(weight * (merged[j, ROWS - 1 :] - own[j, ROWS - 1 :]))
    corner[...] = stacked(*(value[7:] for value in corners), *flows)
    rest[...] = stacked(*(value[:1] for value in corners))


def pack_down(merged, rest, fields, mix_h, mix_v, levels, lower):
    depth = mix_h.shape[0]
    tiles = depth // PER_TILE
    half = slice(0, 8)
    level = levels[half].astype(jnp.float32)
    halo = rim(merged[tiles, half], 8)
    shallow = [
        jnp.minimum(level, near)
        for near in (east(level, halo), west(level, halo), roll(level, -1, 0))
    ]

    def weights_of(k):
        mix = mix_h[k, half]
        halo = rim(merged[tiles + k // PER_TILE, half], GROUP * (k % PER_TILE))
        return [
            jnp.where(open_to > float(k), 0.5 * (mix + near), 0.0)
            for open_to, near in zip(shallow, (east(mix, halo), west(mix, halo), roll(mix, -1, 0)))
        ]

    def halo_of(k, q):
        return rim(merged[k // PER_TILE, half], GROUP * (k % PER_TILE) + 4 * q)

    row_blocks(depth, 0, half, weights_of, halo_of, -1, fields, mix_h, mix_v, lower)
    lower[10 * depth : 10 * depth + 8] = jnp.where(
        iota(8, 0) == 0, level[:1], roll(rest[...], 1, 0)
    )


def both(low, high):
    return jnp.where(iota(8, 0) < 4, low, high)


def coefficient(value, n):
    kept = iota(value.shape[0], 1) % GROUP // 4 == n
    value = roll(jnp.where(kept, value, 0.0), -4 * n, 1)
    value = value + roll(value, 4, 1)
    return value + roll(value, 8, 1)


def near_all(value, halo, below_row=0.0, above_row=0.0):
    return (
        north(value, above_row),
        south(value, below_row),
        east(value, halo),
        west(value, halo),
    )


def steps_of(fields, merged, k, q):
    value = fields[q, k]
    halo = rim(merged[k // PER_TILE], GROUP * (k % PER_TILE) + 4 * q)
    return value, [near - value for near in near_all(value, halo)]


EDGES = (
    "field",
    "mix",
    "inv_down",
    "up_down",
    "down_down",
    "inv_up",
    "up_up",
    "down_up",
    "inv_up_1",
    "up_up_1",
    "down_up_1",
    "to_east",
    "to_west",
    "to_inner",
    "cross_east",
    "cross_west",
    "cross_inner",
    "inside",
    "adjoint",
    "adjoint_1",
    "later",
    "ahead",
    "ahead_1",
    "grad_h",
    "grad_h_1",
    "grad_v_1",
    "column",
    "mix_column",
    "inv_column",
    "up_column",
    "down_column",
)
EDGE_LEVELS = ("own", "own_1", "east", "west", "inner", "column")


def exchange(value):
    return jnp.where(iota(8, 0) % 4 < 2, roll(value, -2, 0), roll(value, 2, 0))


def at_edges(rows, shift):
    sub = iota(8, 0) % 4
    out = roll(rows, LANES - 2 - shift, 1)
    for q in range(1, 4):
        out = jnp.where(sub == q, roll(rows, LANES - 2 - shift - 4 * q, 1), out)
    return jnp.broadcast_to(out, (8, LANES))


def stacked(*rows):
    sub = iota(8, 0)
    out = jnp.zeros((8, LANES), jnp.float32)
    for n, row in enumerate(rows):
        if row is not None:
            out = jnp.where(sub == n, row, out)
    return out


def interior(
    merged,
    own,
    fields,
    factors,
    mix_h,
    mix_v,
    levels,
    lower,
    upper,
    edges,
    edge_levels,
    adjoint,
    grad_h,
    grad_v,
    inside,
    columns,
    column_factors,
    weights,
    packed,
    later,
    up_factors,
):
    depth = mix_h.shape[0]
    face_below = jnp.zeros((ROWS, LANES), jnp.float32)
    inverse = face_below
    level_int = levels[...]
    for k in range(depth - 1, -1, -1):
        face_above = bond(mix_v, level_int, k - 1, depth)
        inverse = pivot(face_below, face_above, inverse)
        up_factors[0, k] = inverse
        up_factors[1, k] = face_below * inverse
        up_factors[2, k] = face_above * inverse
        face_below = face_above
    tiles = depth // PER_TILE
    lane = iota(ROWS, 1)
    zero = jnp.zeros((ROWS, LANES), jnp.float32)

    column = lane % 4

    def around(value, mine):
        return (
            mine,
            jnp.where(column == 1, roll(value, -2, 1), roll(value, 2, 1)),
            north(value, 0.0),
            south(value, 0.0),
        )

    for j in range(tiles):
        level_k = (lane // GROUP + j * PER_TILE).astype(jnp.float32)
        here = [coefficient(merged[tiles + j], n) for n in range(3)]
        (mix, mixes), (level, level_near) = [
            (here[n], around(here[n], coefficient(own[tiles + j], n))) for n in (0, 2)
        ]
        value = merged[j]
        mixed = value
        for near, near_mix, near_level in zip(around(value, own[j]), mixes, level_near):
            weight = jnp.where(
                jnp.minimum(level, near_level) > level_k, 0.5 * (mix + near_mix), 0.0
            )
            mixed = mixed + weight * (near - value)
        packed[0, j] = mixed
        packed[1, j] = here[1]
        if j == 0:
            level_columns = level

    def unpacked(n, k):
        return roll(packed[n, k // PER_TILE], -GROUP * (k % PER_TILE), 1)

    level = levels[...].astype(jnp.float32)
    shallow = [jnp.minimum(level, near) for near in near_all(level, rim(merged[tiles], 8))]

    def first(k, carry):
        (col_bond, col_inverse, col_value), values = carry
        under = min(k + 1, depth - 1)
        bond_here = jnp.where(
            level_columns > k + 1.0, 0.5 * (unpacked(1, k) + unpacked(1, under)), 0.0
        )
        col_inverse = pivot(col_bond, bond_here, col_inverse)
        col_factor = col_bond * col_inverse
        col_value = unpacked(0, k) * col_inverse + col_factor * col_value
        columns[k] = col_value
        column_factors[0, k] = col_inverse
        column_factors[1, k] = col_factor
        column_factors[2, k] = bond_here * col_inverse
        mix = mix_h[k]
        mix_rim = rim(merged[tiles + k // PER_TILE], GROUP * (k % PER_TILE))
        weight = [
            jnp.where(open_to > float(k), 0.5 * (mix + near), 0.0)
            for open_to, near in zip(shallow, near_all(mix, mix_rim))
        ]
        for n in range(4):
            weights[k, n] = weight[n]
        inverse, factor = factors[0, k], factors[1, k]
        values = list(values)
        for q in range(4):
            value, steps = steps_of(fields, merged, k, q)
            for n in range(4):
                value = value + weight[n] * steps[n]
            values[q] = value * inverse + factor * values[q]
            inside[k, q] = values[q]
        return (bond_here, col_inverse, col_value), tuple(values)

    loop(depth, first, ((zero,) * 3, (zero,) * 4))

    def second(n, carry):
        col_value, values, later_values = carry
        k = depth - 1 - n
        col_value = columns[k] + column_factors[2, k] * col_value
        columns[k] = col_value
        values, later_values = list(values), list(later_values)
        first_steps, later_steps = [], []
        for q in range(4):
            value = inside[k, q] + factors[2, k] * values[q]
            inside[k, q] = value
            values[q] = value
            steps = [near - value for near in near_all(value, rim(col_value, 4 * q))]
            later_steps.append(steps)
            first_steps.append(steps_of(fields, merged, k, q)[1])
            for n in range(4):
                value = value + weights[k, n] * steps[n]
            if q < 2:
                later_values[q] = value * up_factors[0, k] + up_factors[1, k] * later_values[q]
                later[k, q] = later_values[q]
            else:
                adjoint[q - 2, k] = value
        total = zero
        for n in range(4):
            face = zero
            for t in range(2):
                face = face + first_steps[t][n] * later_steps[2 + t][n]
                face = face + later_steps[t][n] * first_steps[2 + t][n]
            total = total + jnp.where(shallow[n] > float(k), face, 0.0)
        grad_h[k] = -0.5 * total
        return col_value, tuple(values), tuple(later_values)

    loop(depth, second, (zero, (zero,) * 4, (zero,) * 2))

    face_above = zero
    for k in range(depth):
        if k > 0:
            total = zero
            for t in range(2):
                later[k, t] = later[k, t] + up_factors[2, k] * later[k - 1, t]
                total = total + (inside[k - 1, 2 + t] - inside[k, 2 + t]) * (
                    inside[k - 1, t] - inside[k, t]
                )
                total = total + (fields[2 + t, k - 1] - fields[2 + t, k]) * (
                    later[k - 1, t] - later[k, t]
                )
            face = jnp.where(level > float(k), total, 0.0)
            grad_v[k - 1] = -0.5 * (face + face_above)
            face_above = face
    grad_v[depth - 1] = -0.5 * face_above

    def ends(value, depth_in=0):
        return both(value[depth_in : depth_in + 1], value[ROWS - 1 - depth_in : ROWS - depth_in])

    coef_rows = ends(merged[tiles])
    for n, value in enumerate(
        (
            ends(level),
            ends(level, 1),
            ends(shallow[2]),
            ends(shallow[3]),
            both(shallow[0][:1], shallow[1][ROWS - 1 :]),
            rim(coef_rows, 8),
        )
    ):
        edge_levels[n] = value
    last_lane, first_lane = iota(8, 1) == LANES - 1, iota(8, 1) == 0

    def four(row, depth_in):
        low, high = depth_in, ROWS - 1 - depth_in
        return stacked(
            *(row(q, slice(low, low + 1)) for q in range(4)),
            *(row(q, slice(high, high + 1)) for q in range(4)),
        )

    for k in range(depth):
        j, i = divmod(k, PER_TILE)
        block = slice(8 * k, 8 * k + 8)
        field = both(lower[block], roll(upper[block], 4, 0))
        field_1 = four(lambda q, r: fields[q, k, r], 1)
        column = at_edges(ends(merged[j]), GROUP * i)
        steps = (
            jnp.where(last_lane, column, roll(field, -1, 1)) - field,
            jnp.where(first_lane, column, roll(field, 1, 1)) - field,
            field_1 - field,
        )

        def tracer(ref):
            return lambda q, r: ref[k, q, r] if q < 2 else None

        def result(q, r):
            return adjoint[q - 2, k, r] if q > 1 else None

        things = dict(
            field=field,
            mix=ends(mix_h[k]),
            to_east=ends(weights[k, 2]),
            to_west=ends(weights[k, 3]),
            to_inner=both(weights[k, 0, :1], weights[k, 1, ROWS - 1 :]),
            cross_east=exchange(steps[0]),
            cross_west=exchange(steps[1]),
            cross_inner=exchange(steps[2]),
            inside=four(lambda q, r: inside[k, q, r], 0),
            adjoint=four(result, 0),
            adjoint_1=four(result, 1),
            later=four(tracer(later), 0),
            ahead=roll(field, -2, 0),
            ahead_1=roll(field_1, -2, 0),
            grad_h=ends(grad_h[k]),
            grad_h_1=ends(grad_h[k], 1),
            grad_v_1=ends(grad_v[k], 1),
            column=column,
            mix_column=rim(ends(merged[tiles + j]), GROUP * i),
        )
        for n, name in enumerate(("inv", "up", "down")):
            things[name + "_down"] = ends(factors[n, k])
            things[name + "_up"] = ends(up_factors[n, k])
            things[name + "_up_1"] = ends(up_factors[n, k], 1)
            things[name + "_column"] = rim(ends(column_factors[n, k]), 0)
        for name, value in things.items():
            edges[EDGES.index(name), k] = value


def turned_corner(block, merged, tiles, border):
    code = coefficient(merged[tiles, :8], FILLER)[:1]
    swapped = jnp.where(iota(8, 1) % 4 == 1, roll(block, -2, 1), roll(block, 2, 1))
    return jnp.where((lax.axis_index("tx") == border) & (code > 0.5), swapped, block)


def open_below(seam, corner, merged, edges, edge_levels, opened):
    depth = opened.shape[1]
    tiles = depth // PER_TILE
    turn = (seam[0] == 1) & (lax.axis_index("tx") == 0)
    block = corner[...]
    flows = jnp.where(turn, crossed(block), block)
    block = turned_corner(block, merged, tiles, 0)
    sub, lane = iota(8, 0), iota(8, 1)
    inside = (sub < 4) & ((lane == 0) | (lane == LANES - 1))
    level = jnp.minimum(
        rim(block[tiles : tiles + 1], 8), edge_levels[EDGE_LEVELS.index("column")]
    )
    for k in range(depth):
        j, i = divmod(k, PER_TILE)
        mix = rim(block[tiles + j : tiles + j + 1], GROUP * i)
        weight = 0.5 * (mix + edges[EDGES.index("mix_column"), k])
        opened[0, k] = at_edges(block[j : j + 1], GROUP * i) - edges[EDGES.index("column"), k]
        opened[1, k] = jnp.where(level > float(k), weight, 0.0)
        opened[2, k] = jnp.where(
            inside, at_edges(flows[2 * tiles + j : 2 * tiles + j + 1], GROUP * i), 0.0
        )


def finish(
    seam,
    from_below,
    from_above,
    opened,
    merged,
    edges,
    edge_levels,
    adjoint_in,
    grad_h_in,
    grad_v_in,
    adjoint_out,
    grad_h_out,
    grad_v_out,
    below,
    above,
    rows,
    later,
    adjoint,
    grad_h,
    grad_v,
    sems,
):
    depth, tiles = grad_h.shape[0], grad_h.shape[0] // PER_TILE
    sub = iota(8, 0)
    lane = iota(8, 1)
    place = lax.axis_index("tx")
    last = lax.axis_size("tx") - 1
    base_mix, base_v, base_level = 8 * depth, 9 * depth, 10 * depth
    zero = jnp.zeros((8, LANES), jnp.float32)

    def edge(name, k):
        return edges[EDGES.index(name), k]

    def edge_level(name):
        return edge_levels[EDGE_LEVELS.index(name)]

    for source, target, border in ((from_below, below, 0), (from_above, above, last)):
        turn = (seam[0] == 1) & (place == border)

        @pl.when(turn)
        def _():
            back = LANES - 1 - lane
            for r in range(0, base_level, 8):
                target[r : r + 8] = jnp.take_along_axis(source[r : r + 8], back, axis=1)
            block = source[base_level : base_level + 8]
            target[base_level : base_level + 8] = jnp.where(
                sub < 1, jnp.take_along_axis(block, back, axis=1), block
            )

        @pl.when(jnp.logical_not(turn))
        def _():
            for r in range(0, base_level + 8, 8):
                target[r : r + 8] = source[r : r + 8]

    for k in range(depth):
        for t in range(2):
            adjoint[t, k] = adjoint_in[t, k]
        grad_h[k] = grad_h_in[k]
        grad_v[k] = grad_v_in[k]

    corner = turned_corner(above[base_level : base_level + 8], merged, tiles, last)

    def outer(start, k=0):
        at = slice(start + k, start + k + 1)
        return both(below[at], above[at])

    level_out = outer(base_level)
    level_face = jnp.minimum(level_out, edge_level("own"))
    level_corner = jnp.minimum(rim(corner[1 + tiles : 2 + tiles], 8), edge_level("column"))

    bond_above = inverse = out_value = added = column_added = zero
    flows = []
    for k in range(depth):
        j, i = divmod(k, PER_TILE)
        block = slice(8 * k, 8 * k + 8)
        below_block, above_block = below[block], above[block]
        bond_here = jnp.where(
            level_out > k + 1.0,
            0.5 * (outer(base_v, k) + outer(base_v, min(k + 1, depth - 1))),
            0.0,
        )
        inverse = pivot(bond_above, bond_here, inverse)
        out = both(below_block, roll(above_block, 4, 0))
        part = both(roll(below_block, 4, 0), above_block) + opened[2, k]
        step = out - edge("field", k)
        weight = jnp.where(level_face > float(k), 0.5 * (outer(base_mix, k) + edge("mix", k)), 0.0)
        flow = weight * step
        out_value = (part - flow) * inverse + bond_above * inverse * out_value
        added = flow * edge("inv_down", k) + edge("up_down", k) * added
        mix_corner = rim(corner[1 + tiles + j : 2 + tiles + j], GROUP * i)
        weight_corner = both(
            opened[1, k],
            jnp.where(level_corner > float(k), 0.5 * (mix_corner + edge("mix_column", k)), 0.0),
        )
        step_corner = both(
            opened[0, k], at_edges(corner[1 + j : 2 + j], GROUP * i) - edge("column", k)
        )
        column_added = (
            weight_corner * step_corner * edge("inv_column", k)
            + edge("up_column", k) * column_added
        )
        rows[0, k] = out_value
        rows[1, k] = bond_here * inverse
        rows[2, k] = added
        rows[3, k] = column_added
        rows[4, k] = weight
        rows[5, k] = exchange(step)
        bond_above = bond_here

    out_value = added = column_added = later_0 = later_1 = zero
    for k in range(depth - 1, -1, -1):
        out_value = rows[0, k] + rows[1, k] * out_value
        added = rows[2, k] + edge("down_down", k) * added
        column_added = rows[3, k] + edge("down_column", k) * column_added
        value = edge("inside", k) + added
        rows[0, k] = value
        east_step = jnp.where(lane == LANES - 1, column_added, roll(added, -1, 1)) - added
        west_step = jnp.where(lane == 0, column_added, roll(added, 1, 1)) - added
        out_step = out_value - value
        inner_flow = edge("to_inner", k) * added
        change = (
            added
            + edge("to_east", k) * east_step
            + edge("to_west", k) * west_step
            - inner_flow
            + rows[4, k] * out_step
        )
        later_0 = change * edge("inv_up", k) + edge("up_up", k) * later_0
        later_1 = inner_flow * edge("inv_up_1", k) + edge("up_up_1", k) * later_1
        later[0, k] = later_0
        later[1, k] = later_1
        result = edge("adjoint", k) + change
        result_1 = edge("adjoint_1", k) + inner_flow
        for t in range(2):
            for at, source, row in (
                (0, result, 2),
                (ROWS - 1, result, 6),
                (1, result_1, 2),
                (ROWS - 2, result_1, 6),
            ):
                adjoint[t, k, at : at + 1] = source[row + t : row + t + 1]
        product_1 = jnp.where(
            edge_level("inner") > float(k), -edge("cross_inner", k) * added, 0.0
        )
        product = (
            product_1
            + jnp.where(edge_level("east") > float(k), edge("cross_east", k) * east_step, 0.0)
            + jnp.where(edge_level("west") > float(k), edge("cross_west", k) * west_step, 0.0)
            + jnp.where(level_face > float(k), rows[5, k] * out_step, 0.0)
        )
        for name, inset, value in (("grad_h", 0, product), ("grad_h_1", 1, product_1)):
            value = value + roll(value, -1, 0)
            value = edge(name, k) - 0.5 * (value + roll(value, -2, 0))
            grad_h[k, inset : inset + 1] = value[:1]
            grad_h[k, ROWS - 1 - inset : ROWS - inset] = value[4:5]

    copies = [
        pltpu.make_async_copy(source, target, sems.at[n])
        for n, (source, target) in enumerate(
            ((adjoint, adjoint_out), (grad_h, grad_h_out), (grad_v, grad_v_out))
        )
    ]
    copies[0].start()
    copies[1].start()

    face_0 = face_1 = later_0 = later_1 = zero
    for k in range(depth + 1):
        if k < depth:
            above_0, above_1 = later_0, later_1
            later_0 = later[0, k] + edge("down_up", k) * later_0
            later_1 = later[1, k] + edge("down_up_1", k) * later_1
        if k == 0:
            continue
        next_0 = next_1 = zero
        if k < depth:
            step = rows[0, k - 1] - rows[0, k]
            next_0 = step * roll(step, -2, 0) + (edge("ahead", k - 1) - edge("ahead", k)) * (
                edge("later", k - 1) + above_0 - edge("later", k) - later_0
            )
            next_1 = (edge("ahead_1", k - 1) - edge("ahead_1", k)) * (above_1 - later_1)
            next_0 = jnp.where(
                edge_level("own") > float(k), next_0 + roll(next_0, -1, 0), 0.0
            )
            next_1 = jnp.where(
                edge_level("own_1") > float(k), next_1 + roll(next_1, -1, 0), 0.0
            )
        value_0 = -0.5 * (face_0 + next_0)
        value_1 = edge("grad_v_1", k - 1) - 0.5 * (face_1 + next_1)
        for inset, value in ((0, value_0), (1, value_1)):
            grad_v[k - 1, inset : inset + 1] = value[:1]
            grad_v[k - 1, ROWS - 1 - inset : ROWS - inset] = value[4:5]
        face_0, face_1 = next_0, next_1
    copies[2].start()
    for copy in copies:
        copy.wait()


def per_device(tracers, costate, mixing_h, mixing_v, levels, seam_code):
    depth = tracers.shape[1]
    tiles = depth // PER_TILE
    height = 10 * depth + 8
    params = pltpu.CompilerParams(vmem_limit_bytes=48 * 2**20)
    smem = pl.BlockSpec(memory_space=pltpu.SMEM)
    vmem = pl.BlockSpec(memory_space=pltpu.VMEM)
    hbm = pl.BlockSpec(memory_space=pltpu.HBM)
    tile = (ROWS, LANES)
    fields, factors, own, mix_h, mix_v, levels_here = pl.pallas_call(
        prepare,
        out_shape=(
            vmem_out(4, depth, *tile),
            vmem_out(3, depth, *tile),
            vmem_out(2 * tiles, *tile),
            vmem_out(depth, *tile),
            vmem_out(depth, *tile),
            pltpu.VMEM(tile, jnp.int32),
        ),
        in_specs=[smem] + [hbm] * 5,
        scratch_shapes=[pltpu.SemaphoreType.DMA((5,))],
        compiler_params=params,
        name="prepare",
    )(seam_code, *(in_hbm(a) for a in (tracers, costate, mixing_h, mixing_v, levels)))

    count = lax.axis_size("ty")
    near_pairs = [(i, i ^ 1) for i in range(count)]
    far_pairs = [(i, (i + 1 if i % 2 else i - 1) % count) for i in range(count)]
    far = lax.ppermute(own, "ty", far_pairs)
    near = lax.ppermute(own, "ty", near_pairs)

    def call(body, outs, *operands, **options):
        return pl.pallas_call(
            body, out_shape=outs, compiler_params=params, name=body.__name__, **options
        )(*(in_vmem(a) for a in operands))

    count = lax.axis_size("tx")
    upward = [(i, (i + 1) % count) for i in range(count)]
    downward = [(i, (i - 1) % count) for i in range(count)]
    upper = call(pack_up, vmem_out(height, LANES), fields, mix_h, mix_v, levels_here)
    from_below = lax.ppermute(upper, "tx", upward)
    merged, corner, rest = call(
        pack_sides,
        (vmem_out(2 * tiles, *tile), vmem_out(8, LANES), vmem_out(8, LANES)),
        near,
        far,
        own,
    )
    corner_below = lax.ppermute(corner, "tx", upward)
    lower = call(
        pack_down, vmem_out(height, LANES), merged, rest, fields, mix_h, mix_v, levels_here
    )
    from_above = lax.ppermute(lower, "tx", downward)
    row_block = (depth, 8, LANES)
    inner = pl.pallas_call(
        interior,
        out_shape=(
            vmem_out(len(EDGES), *row_block),
            vmem_out(len(EDGE_LEVELS), 8, LANES),
            vmem_out(2, depth, *tile),
            vmem_out(depth, *tile),
            vmem_out(depth, *tile),
        ),
        scratch_shapes=[
            vmem_out(depth, 4, *tile),
            vmem_out(depth, *tile),
            vmem_out(3, depth, *tile),
            vmem_out(depth, 4, *tile),
            vmem_out(2, tiles, *tile),
            vmem_out(depth, 2, *tile),
            vmem_out(3, depth, *tile),
        ],
        compiler_params=params,
        cost_estimate=pl.CostEstimate(flops=100_000_000, bytes_accessed=100_000_000, transcendentals=0),
        name="interior",
    )(
        *(
            in_vmem(a)
            for a in (merged, own, fields, factors, mix_h, mix_v, levels_here, lower, upper)
        )
    )
    opened = pl.pallas_call(
        open_below,
        out_shape=vmem_out(3, *row_block),
        in_specs=[smem] + [vmem] * 4,
        compiler_params=params,
        cost_estimate=pl.CostEstimate(flops=900_000_000, bytes_accessed=900_000_000, transcendentals=0),
        name="open_below",
    )(seam_code, *(in_vmem(a) for a in (corner_below, merged, *inner[:2])))
    block = jax.ShapeDtypeStruct(mixing_h.shape, jnp.float32)
    return pl.pallas_call(
        finish,
        out_shape=(jax.ShapeDtypeStruct(tracers.shape, jnp.float32), block, block),
        in_specs=[smem] + [vmem] * 9,
        out_specs=(hbm, hbm, hbm),
        scratch_shapes=[
            vmem_out(height, LANES),
            vmem_out(height, LANES),
            vmem_out(6, *row_block),
            vmem_out(2, *row_block),
            vmem_out(2, depth, *tile),
            vmem_out(depth, *tile),
            vmem_out(depth, *tile),
            pltpu.SemaphoreType.DMA((3,)),
        ],
        compiler_params=params,
        name="finish",
    )(seam_code, *(in_vmem(a) for a in (from_below, from_above, opened, merged, *inner)))


def solution(mesh):
    placed = (
        P("members", None, "tx", "ty"),
        P("members", None, "tx", "ty"),
        P("members", "tx", "ty"),
        P("members", "tx", "ty"),
        P("tx", "ty"),
        P("ty"),
    )
    return jax.shard_map(
        per_device,
        mesh=mesh,
        in_specs=placed,
        out_specs=(
            P("members", None, "tx", "ty"),
            P("members", "tx", "ty"),
            P("members", "tx", "ty"),
        ),
        check_vma=False,
    )
```

```python
import jax
import jax.numpy as jnp
from jax import lax
from jax.experimental import pallas as pl
from jax.experimental.pallas import tpu as pltpu
from jax.sharding import PartitionSpec as P

LANES = 128
ROWS = 16
GROUP = 16
PER_TILE = LANES // GROUP


FILLER = 3


def in_vmem(array):
    return pltpu.with_memory_space_constraint(array, pltpu.VMEM)


def in_hbm(array):
    return pltpu.with_memory_space_constraint(array, pltpu.HBM)


def vmem_out(*shape):
    return pltpu.VMEM(shape, jnp.float32)


def iota(rows, dim):
    return lax.broadcasted_iota(jnp.int32, (rows, LANES), dim)


def roll(value, shift, axis):
    return pltpu.roll(value, shift % value.shape[axis], axis)


def fold(value):
    return jnp.where(iota(8, 0) < 4, value[:8], value[8:])


def east(value, halo):
    return jnp.where(iota(value.shape[0], 1) == LANES - 1, halo, roll(value, -1, 1))


def west(value, halo):
    return jnp.where(iota(value.shape[0], 1) == 0, halo, roll(value, 1, 1))


def rim(tile, base):
    return roll(tile, LANES - 2 - base, 1)


def crossed(tile):
    column = iota(tile.shape[0], 1) % 4
    return jnp.where(
        column == 1, roll(tile, -1, 1), jnp.where(column == 2, roll(tile, 1, 1), tile)
    )


def tile_of(q, k, depth):
    return slice((q * depth + k) * ROWS, (q * depth + k + 1) * ROWS)


def up(value):
    low, high = roll(value[:8], -1, 0), roll(value[8:], -1, 0)
    return jnp.concatenate([jnp.where(iota(8, 0) == 7, high, low), high], axis=0)


def down(value):
    low, high = roll(value[:8], 1, 0), roll(value[8:], 1, 0)
    return jnp.concatenate([low, jnp.where(iota(8, 0) == 0, low, high)], axis=0)


def bond(mix_v, level, k, depth):
    if k in (-1, depth - 1):
        return jnp.zeros(level.shape, jnp.float32)
    return jnp.where(level > k + 1, 0.5 * (mix_v[k] + mix_v[k + 1]), 0.0)


def factorize(depth, level, mix_v, put):
    bond_above = jnp.zeros(level.shape, jnp.float32)
    inverse = bond_above
    for k in range(depth):
        bond_here = bond(mix_v, level, k, depth)
        inverse = pivot(bond_above, bond_here, inverse)
        put(k, inverse, bond_above * inverse, bond_here * inverse)
        bond_above = bond_here


def pivot(bond_above, bond_here, inverse):
    return 1.0 / (1.0 + bond_above + bond_here - bond_above * (bond_above * inverse))


def prepare(
    seam,
    tracers,
    costate,
    mix_h_in,
    mix_v_in,
    levels_in,
    fields,
    factors,
    message,
    mix_h,
    mix_v,
    levels,
    sems,
):
    depth = mix_h.shape[0]
    tiles = depth // PER_TILE
    copies = [
        pltpu.make_async_copy(source, target, sems.at[n])
        for n, (source, target) in enumerate(
            (
                (levels_in, levels),
                (mix_v_in, mix_v),
                (costate, fields.at[2 * depth * ROWS :]),
                (tracers, fields.at[: 2 * depth * ROWS]),
                (mix_h_in, mix_h),
            )
        )
    ]
    for copy in copies:
        copy.start()
    for copy in copies[:2]:
        copy.wait()
    level = levels[...]
    place = iota(ROWS, 1) // 4
    zero = jnp.zeros((ROWS, LANES), jnp.float32)

    def put(k, *three):
        for n in range(3):
            factors[n, k] = three[n]

    factorize(depth, level, mix_v, put)
    seconds = [jnp.where(place % 4 == FILLER, seam[0].astype(jnp.float32), zero)] * tiles
    level_f = level.astype(jnp.float32)
    for k in range(depth):
        tile, base = k // PER_TILE, GROUP * (k % PER_TILE)
        for n, value in ((1, mix_v[k]), (2, level_f)):
            seconds[tile] = jnp.where(
                place == base // 4 + n, roll(value, base + 4 * n + 2, 1), seconds[tile]
            )
    for copy in copies[2:]:
        copy.wait()
    values = [zero, zero]
    for k in range(depth):
        for t in range(2):
            values[t] = fields[tile_of(2 + t, k, depth)] * factors[0, k] + factors[1, k] * values[t]
            fields[tile_of(2 + t, k, depth)] = values[t]
    firsts = [zero] * tiles
    values = [zero, zero]
    for k in range(depth - 1, -1, -1):
        tile, base = k // PER_TILE, GROUP * (k % PER_TILE)
        for t in range(2):
            values[t] = fields[tile_of(2 + t, k, depth)] + factors[2, k] * values[t]
            fields[tile_of(2 + t, k, depth)] = values[t]
        for q in range(4):
            value = fields[tile_of(q, k, depth)] if q < 2 else values[q - 2]
            firsts[tile] = jnp.where(
                place == base // 4 + q, roll(value, base + 4 * q + 2, 1), firsts[tile]
            )
        seconds[tile] = jnp.where(
            place == base // 4, roll(mix_h[k], base + 2, 1), seconds[tile]
        )
    for tile in range(tiles):
        message[tile] = firsts[tile]
        message[tiles + tile] = seconds[tile]


def row_blocks(depth, row, half, weights_of, halo_of, inner_shift, fields, mix_h, mix_v, target):
    sub = iota(8, 0)
    at = row % 8
    for k in range(depth):
        weights = weights_of(k)
        block = jnp.zeros((8, LANES), jnp.float32)
        for q in range(4):
            value = fields[tile_of(q, k, depth)][half]
            halo = halo_of(k, q)
            part = value
            for near, weight in zip(
                (east(value, halo), west(value, halo), roll(value, inner_shift, 0)), weights
            ):
                part = part + weight * (near - value)
            for n, thing in ((q, value), (4 + q, part)):
                block = jnp.where(sub == n, roll(thing, n - at, 0), block)
        target[8 * k : 8 * k + 8] = block
        for n, array in enumerate((mix_h, mix_v)):
            start = (8 + n) * depth + k
            target[start : start + 1] = array[k, row : row + 1]


def pack_up(fields, mix_h, mix_v, levels, upper):
    depth = mix_h.shape[0]
    half = slice(8, 16)
    level = levels[half].astype(jnp.float32)
    shallow = [
        jnp.minimum(level, near)
        for near in (east(level, 0.0), west(level, 0.0), roll(level, 1, 0))
    ]

    def weights_of(k):
        mix = mix_h[k, half]
        return [
            jnp.where(open_to > float(k), 0.5 * (mix + near), 0.0)
            for open_to, near in zip(shallow, (east(mix, 0.0), west(mix, 0.0), roll(mix, 1, 0)))
        ]

    row_blocks(depth, 15, half, weights_of, lambda k, q: 0.0, 1, fields, mix_h, mix_v, upper)
    upper[10 * depth : 10 * depth + 8] = stacked(level[7:])


def pack_sides(near, far, own, merged, corner, rest):
    tiles = near.shape[0] // 2
    place = lax.axis_index("ty")
    last = lax.axis_size("ty") - 1
    even = place % 2 == 0
    column = iota(ROWS, 1) % 4
    from_west = column < 2
    missing = ((place == 0) & from_west) | ((place == last) & jnp.logical_not(from_west))
    corners = []
    for j in range(2 * tiles):
        west_tile = jnp.where(even, far[j], near[j])
        east_tile = jnp.where(even, near[j], far[j])
        tile = jnp.where(from_west, west_tile, east_tile)
        if j >= tiles:
            tile = jnp.where(missing, 0.0, tile)
        merged[j] = crossed(tile)
        corners.append(
            crossed(
                fold(
                    jnp.where(
                        column == 0,
                        roll(west_tile, -2, 1),
                        jnp.where(column == 3, roll(east_tile, 2, 1), tile),
                    )
                )
            )
        )
    flows = []
    lane = iota(1, 1)
    for j in range(tiles):
        level_k = (lane // GROUP + j * PER_TILE).astype(jnp.float32)
        mix, level = [
            [coefficient(ref[tiles + j, ROWS - 1 :], n) for ref in (merged, own)] for n in (0, 2)
        ]
        weight = jnp.where(jnp.minimum(*level) > level_k, 0.5 * (mix[0] + mix[1]), 0.0)
        flows.append(weight * (merged[j, ROWS - 1 :] - own[j, ROWS - 1 :]))
    corner[...] = stacked(*(value[7:] for value in corners), *flows)
    rest[...] = stacked(*(value[:1] for value in corners))


def pack_down(merged, rest, fields, mix_h, mix_v, levels, lower):
    depth = mix_h.shape[0]
    tiles = depth // PER_TILE
    half = slice(0, 8)
    level = levels[half].astype(jnp.float32)
    halo = rim(merged[tiles, half], 8)
    shallow = [
        jnp.minimum(level, near)
        for near in (east(level, halo), west(level, halo), roll(level, -1, 0))
    ]

    def weights_of(k):
        mix = mix_h[k, half]
        halo = rim(merged[tiles + k // PER_TILE, half], GROUP * (k % PER_TILE))
        return [
            jnp.where(open_to > float(k), 0.5 * (mix + near), 0.0)
            for open_to, near in zip(shallow, (east(mix, halo), west(mix, halo), roll(mix, -1, 0)))
        ]

    def halo_of(k, q):
        return rim(merged[k // PER_TILE, half], GROUP * (k % PER_TILE) + 4 * q)

    row_blocks(depth, 0, half, weights_of, halo_of, -1, fields, mix_h, mix_v, lower)
    lower[10 * depth : 10 * depth + 8] = jnp.where(
        iota(8, 0) == 0, level[:1], roll(rest[...], 1, 0)
    )


def both(low, high):
    return jnp.where(iota(8, 0) < 4, low, high)


def coefficient(value, n):
    kept = iota(value.shape[0], 1) % GROUP // 4 == n
    value = roll(jnp.where(kept, value, 0.0), -4 * n, 1)
    value = value + roll(value, 4, 1)
    return value + roll(value, 8, 1)


EDGES = (
    "field",
    "mix",
    "inv_down",
    "up_down",
    "down_down",
    "inv_up",
    "up_up",
    "down_up",
    "inv_up_1",
    "up_up_1",
    "down_up_1",
    "to_east",
    "to_west",
    "to_inner",
    "cross_east",
    "cross_west",
    "cross_inner",
    "inside",
    "after",
    "after_1",
    "ahead",
    "ahead_1",
    "grad_h",
    "grad_h_1",
    "grad_v_1",
    "column",
    "mix_column",
    "inv_column",
    "up_column",
    "down_column",
)
EDGE_LEVELS = ("own", "own_1", "east", "west", "inner", "column")


def exchange(value):
    return jnp.where(iota(8, 0) % 4 < 2, roll(value, -2, 0), roll(value, 2, 0))


def at_edges(rows, shift):
    sub = iota(8, 0) % 4
    out = roll(rows, LANES - 2 - shift, 1)
    for q in range(1, 4):
        out = jnp.where(sub == q, roll(rows, LANES - 2 - shift - 4 * q, 1), out)
    return jnp.broadcast_to(out, (8, LANES))


def stacked(*rows):
    sub = iota(8, 0)
    out = jnp.zeros((8, LANES), jnp.float32)
    for n, row in enumerate(rows):
        if row is not None:
            out = jnp.where(sub == n, row, out)
    return out


def nears_of(value, halo):
    return east(value, halo), west(value, halo), up(value), down(value)


def at(q):
    return slice(q * ROWS, (q + 1) * ROWS)


def interior_down(
    merged,
    own,
    fields,
    factors,
    mix_h,
    mix_v,
    levels,
    sent,
    inside,
    steps,
    weights,
    columns,
    column_factors,
    up_factors,
    shallow_out,
    packed,
):
    depth = mix_h.shape[0]
    tiles = depth // PER_TILE
    lane = iota(ROWS, 1)
    zero = jnp.zeros((ROWS, LANES), jnp.float32)
    level = levels[...]
    face_below = inverse = zero
    for k in range(depth - 1, -1, -1):
        face_above = bond(mix_v, level, k - 1, depth)
        inverse = pivot(face_below, face_above, inverse)
        up_factors[0, k] = inverse
        up_factors[1, k] = face_below * inverse
        up_factors[2, k] = face_above * inverse
        face_below = face_above

    column = lane % 4
    last_row, first_row = iota(ROWS, 0) == ROWS - 1, iota(ROWS, 0) == 0
    for j in range(tiles):
        level_k = (lane // GROUP + j * PER_TILE).astype(jnp.float32)
        mix, bonds, depths = [coefficient(merged[tiles + j], n) for n in range(3)]
        own_mix, own_depths = [coefficient(own[tiles + j], n) for n in (0, 2)]
        value = merged[j]

        def outer(array):
            return jnp.where(column == 1, roll(array, -2, 1), roll(array, 2, 1))

        def weight(near_depths, near_mix):
            return jnp.where(
                jnp.minimum(depths, near_depths) > level_k, 0.5 * (mix + near_mix), 0.0
            )

        mixed = value + weight(own_depths, own_mix) * (own[j] - value)
        mixed = mixed + weight(outer(depths), outer(mix)) * (outer(value) - value)
        for border, shift in ((last_row, up), (first_row, down)):
            flow = weight(shift(depths), shift(mix)) * (shift(value) - value)
            mixed = mixed + jnp.where(border, 0.0, flow)
        packed[0, j] = mixed
        packed[1, j] = bonds
        if j == 0:
            level_columns = depths

    def unpacked(n, k):
        return roll(packed[n, k // PER_TILE], -GROUP * (k % PER_TILE), 1)

    level = level.astype(jnp.float32)
    shallow = [jnp.minimum(level, near) for near in nears_of(level, rim(merged[tiles], 8))]
    shallow[2] = jnp.where(last_row, 0.0, shallow[2])
    shallow[3] = jnp.where(first_row, 0.0, shallow[3])
    for n in range(4):
        shallow_out[n] = shallow[n]

    bond_above = col_inverse = col_value = zero
    values = [zero] * 4
    for k in range(depth):
        j, i = divmod(k, PER_TILE)
        under = min(k + 1, depth - 1)
        bond_here = jnp.where(
            level_columns > k + 1.0, 0.5 * (unpacked(1, k) + unpacked(1, under)), 0.0
        )
        col_inverse = pivot(bond_above, bond_here, col_inverse)
        col_factor = bond_above * col_inverse
        col_value = unpacked(0, k) * col_inverse + col_factor * col_value
        columns[k] = col_value
        column_factors[0, k] = col_inverse
        column_factors[1, k] = col_factor
        column_factors[2, k] = bond_here * col_inverse
        bond_above = bond_here
        mix = mix_h[k]
        weight = [
            jnp.where(open_to > float(k), 0.5 * (mix + near), 0.0)
            for open_to, near in zip(shallow, nears_of(mix, rim(merged[tiles + j], GROUP * i)))
        ]
        for n in range(4):
            weights[k, n] = weight[n]
        for q in range(4):
            value = fields[tile_of(q, k, depth)]
            step = [near - value for near in nears_of(value, rim(merged[j], GROUP * i + 4 * q))]
            for n in range(4):
                steps[k, q, n] = step[n]
                value = value + weight[n] * step[n]
            values[q] = value * factors[0, k] + factors[1, k] * values[q]
            inside[k, at(q)] = values[q]


def interior_up(
    inside_in,
    steps,
    weights,
    columns,
    column_factors,
    up_factors,
    shallow_in,
    factors,
    inside,
    after,
    adjoint,
    grad_h,
):
    depth = grad_h.shape[0]
    zero = jnp.zeros((ROWS, LANES), jnp.float32)
    shallow = [shallow_in[n] for n in range(4)]
    col_value = zero
    values = [zero] * 4
    later_values = [zero] * 2
    for k in range(depth - 1, -1, -1):
        col_value = columns[k] + column_factors[2, k] * col_value
        later_steps = []
        for q in range(4):
            value = inside_in[k, at(q)] + factors[2, k] * values[q]
            inside[k, at(q)] = value
            values[q] = value
            step = [near - value for near in nears_of(value, rim(col_value, 4 * q))]
            later_steps.append(step)
            for n in range(4):
                value = value + weights[k, n] * step[n]
            if q < 2:
                later_values[q] = value * up_factors[0, k] + up_factors[1, k] * later_values[q]
                value = later_values[q]
            else:
                adjoint[q - 2, k] = value
            after[k, at(q)] = value
        total = zero
        for n in range(4):
            face = zero
            for t in range(2):
                face = face + steps[k, t, n] * later_steps[2 + t][n]
                face = face + later_steps[t][n] * steps[k, 2 + t, n]
            total = total + jnp.where(shallow[n] > float(k), face, 0.0)
        grad_h[k] = -0.5 * total


def interior_edges(
    merged,
    fields,
    factors,
    mix_h,
    levels,
    inside,
    after,
    weights,
    column_factors,
    up_factors,
    shallow,
    grad_h,
    edges,
    edge_levels,
    grad_v,
    later,
):
    depth = mix_h.shape[0]
    tiles = depth // PER_TILE
    zero = jnp.zeros((ROWS, LANES), jnp.float32)
    level = levels[...].astype(jnp.float32)
    face_above = zero
    for t in range(2):
        later[0, at(t)] = after[0, at(t)]
    for k in range(depth):
        if k > 0:
            total = zero
            for t in range(2):
                later_here = after[k, at(t)] + up_factors[2, k] * later[k - 1, at(t)]
                later[k, at(t)] = later_here
                total = total + (inside[k - 1, at(2 + t)] - inside[k, at(2 + t)]) * (
                    inside[k - 1, at(t)] - inside[k, at(t)]
                )
                total = total + (
                    fields[tile_of(2 + t, k - 1, depth)] - fields[tile_of(2 + t, k, depth)]
                ) * (later[k - 1, at(t)] - later_here)
            face = jnp.where(level > float(k), total, 0.0)
            grad_v[k - 1] = -0.5 * (face + face_above)
            face_above = face
    grad_v[depth - 1] = -0.5 * face_above

    def ends(value, inset=0):
        return both(value[inset : inset + 1], value[ROWS - 1 - inset : ROWS - inset])

    def four(ref, start, stride, inset=0):
        low, high = start + inset, start + ROWS - 1 - inset
        return stacked(
            *(ref[row + q * stride : row + q * stride + 1] for row in (low, high) for q in range(4))
        )

    last_lane, first_lane = iota(8, 1) == LANES - 1, iota(8, 1) == 0

    coef_rows = ends(merged[tiles])
    for n, value in enumerate(
        (
            ends(level),
            ends(level, 1),
            ends(shallow[0]),
            ends(shallow[1]),
            both(shallow[2, :1], shallow[3, ROWS - 1 :]),
            rim(coef_rows, 8),
        )
    ):
        edge_levels[n] = value

    for k in range(depth):
        j, i = divmod(k, PER_TILE)
        field = four(fields, k * ROWS, depth * ROWS)
        field_1 = four(fields, k * ROWS, depth * ROWS, 1)
        column = at_edges(ends(merged[j]), GROUP * i)
        things = dict(
            field=field,
            mix=ends(mix_h[k]),
            to_east=ends(weights[k, 0]),
            to_west=ends(weights[k, 1]),
            to_inner=both(weights[k, 2, :1], weights[k, 3, ROWS - 1 :]),
            cross_east=exchange(jnp.where(last_lane, column, roll(field, -1, 1)) - field),
            cross_west=exchange(jnp.where(first_lane, column, roll(field, 1, 1)) - field),
            cross_inner=exchange(field_1 - field),
            inside=four(inside.at[k], 0, ROWS),
            after=stacked(
                *(
                    (later if q < 2 else after)[k, q * ROWS + row : q * ROWS + row + 1]
                    for row in (0, ROWS - 1)
                    for q in range(4)
                )
            ),
            after_1=four(after.at[k], 0, ROWS, 1),
            ahead=roll(field, -2, 0),
            ahead_1=roll(field_1, -2, 0),
            grad_h=ends(grad_h[k]),
            grad_h_1=ends(grad_h[k], 1),
            grad_v_1=ends(grad_v[k], 1),
            column=column,
            mix_column=rim(ends(merged[tiles + j]), GROUP * i),
        )
        for n, name in enumerate(("inv", "up", "down")):
            things[name + "_down"] = ends(factors[n, k])
            things[name + "_up"] = ends(up_factors[n, k])
            things[name + "_up_1"] = ends(up_factors[n, k], 1)
            things[name + "_column"] = rim(ends(column_factors[n, k]), 0)
        for name, value in things.items():
            edges[EDGES.index(name), k] = value


def turned_corner(block, merged, tiles, border):
    code = coefficient(merged[tiles, :8], FILLER)[:1]
    swapped = jnp.where(iota(8, 1) % 4 == 1, roll(block, -2, 1), roll(block, 2, 1))
    return jnp.where((lax.axis_index("tx") == border) & (code > 0.5), swapped, block)


def open_below(seam, corner, merged, edge_levels, opened):
    tiles = merged.shape[0] // 2
    turn = (seam[0] == 1) & (lax.axis_index("tx") == 0)
    block = corner[...]
    flows = jnp.where(turn, crossed(block), block)
    block = turned_corner(block, merged, tiles, 0)
    opened[0] = jnp.where(iota(8, 0) < 2 * tiles, block, flows)
    opened[1] = jnp.minimum(
        rim(block[tiles : tiles + 1], 8), edge_levels[EDGE_LEVELS.index("column")]
    )


def finish(
    seam,
    from_below,
    from_above,
    opened,
    merged,
    edges,
    edge_levels,
    adjoint_in,
    grad_h_in,
    grad_v_in,
    adjoint_out,
    grad_h_out,
    grad_v_out,
    below,
    above,
    rows,
    later,
    adjoint,
    grad_h,
    grad_v,
    sems,
):
    depth, tiles = grad_h.shape[0], grad_h.shape[0] // PER_TILE
    sub = iota(8, 0)
    lane = iota(8, 1)
    place = lax.axis_index("tx")
    last = lax.axis_size("tx") - 1
    base_mix, base_v, base_level = 8 * depth, 9 * depth, 10 * depth
    zero = jnp.zeros((8, LANES), jnp.float32)

    def edge(name, k):
        return edges[EDGES.index(name), k]

    def edge_level(name):
        return edge_levels[EDGE_LEVELS.index(name)]

    for source, target, border in ((from_below, below, 0), (from_above, above, last)):
        turn = (seam[0] == 1) & (place == border)

        @pl.when(turn)
        def _():
            back = LANES - 1 - lane
            for r in range(0, base_level, 8):
                target[r : r + 8] = jnp.take_along_axis(source[r : r + 8], back, axis=1)
            block = source[base_level : base_level + 8]
            target[base_level : base_level + 8] = jnp.where(
                sub < 1, jnp.take_along_axis(block, back, axis=1), block
            )

        @pl.when(jnp.logical_not(turn))
        def _():
            for r in range(0, base_level + 8, 8):
                target[r : r + 8] = source[r : r + 8]

    for k in range(depth):
        for t in range(2):
            adjoint[t, k] = adjoint_in[t, k]
        grad_h[k] = grad_h_in[k]
        grad_v[k] = grad_v_in[k]

    corner_above = turned_corner(above[base_level : base_level + 8], merged, tiles, last)

    def corner(r):
        return both(opened[0, r : r + 1], corner_above[1 + r : 2 + r])

    beside = (sub < 4) & ((lane == 0) | (lane == LANES - 1))

    def outer(start, k=0):
        at = slice(start + k, start + k + 1)
        return both(below[at], above[at])

    level_out = outer(base_level)
    level_face = jnp.minimum(level_out, edge_level("own"))
    level_corner = both(
        opened[1],
        jnp.minimum(rim(corner_above[1 + tiles : 2 + tiles], 8), edge_level("column")),
    )

    bond_above = inverse = out_value = added = column_added = zero
    flows = []
    for k in range(depth):
        j, i = divmod(k, PER_TILE)
        block = slice(8 * k, 8 * k + 8)
        below_block, above_block = below[block], above[block]
        bond_here = jnp.where(
            level_out > k + 1.0,
            0.5 * (outer(base_v, k) + outer(base_v, min(k + 1, depth - 1))),
            0.0,
        )
        inverse = pivot(bond_above, bond_here, inverse)
        out = both(below_block, roll(above_block, 4, 0))
        part = both(roll(below_block, 4, 0), above_block) + jnp.where(
            beside, at_edges(opened[0, 2 * tiles + j : 2 * tiles + j + 1], GROUP * i), 0.0
        )
        step = out - edge("field", k)
        weight = jnp.where(level_face > float(k), 0.5 * (outer(base_mix, k) + edge("mix", k)), 0.0)
        flow = weight * step
        out_value = (part - flow) * inverse + bond_above * inverse * out_value
        added = flow * edge("inv_down", k) + edge("up_down", k) * added
        mix_corner = rim(corner(tiles + j), GROUP * i)
        weight_corner = jnp.where(
            level_corner > float(k), 0.5 * (mix_corner + edge("mix_column", k)), 0.0
        )
        step_corner = at_edges(corner(j), GROUP * i) - edge("column", k)
        column_added = (
            weight_corner * step_corner * edge("inv_column", k)
            + edge("up_column", k) * column_added
        )
        rows[0, k] = out_value
        rows[1, k] = bond_here * inverse
        rows[2, k] = added
        rows[3, k] = column_added
        rows[4, k] = weight
        rows[5, k] = exchange(step)
        bond_above = bond_here

    out_value = added = column_added = later_0 = later_1 = zero
    for k in range(depth - 1, -1, -1):
        out_value = rows[0, k] + rows[1, k] * out_value
        added = rows[2, k] + edge("down_down", k) * added
        column_added = rows[3, k] + edge("down_column", k) * column_added
        value = edge("inside", k) + added
        rows[0, k] = value
        east_step = jnp.where(lane == LANES - 1, column_added, roll(added, -1, 1)) - added
        west_step = jnp.where(lane == 0, column_added, roll(added, 1, 1)) - added
        out_step = out_value - value
        inner_flow = edge("to_inner", k) * added
        change = (
            added
            + edge("to_east", k) * east_step
            + edge("to_west", k) * west_step
            - inner_flow
            + rows[4, k] * out_step
        )
        later_0 = change * edge("inv_up", k) + edge("up_up", k) * later_0
        later_1 = inner_flow * edge("inv_up_1", k) + edge("up_up_1", k) * later_1
        later[0, k] = later_0
        later[1, k] = later_1
        result = edge("after", k) + change
        result_1 = edge("after_1", k) + inner_flow
        for t in range(2):
            for at, source, row in (
                (0, result, 2),
                (ROWS - 1, result, 6),
                (1, result_1, 2),
                (ROWS - 2, result_1, 6),
            ):
                adjoint[t, k, at : at + 1] = source[row + t : row + t + 1]
        product_1 = jnp.where(
            edge_level("inner") > float(k), -edge("cross_inner", k) * added, 0.0
        )
        product = (
            product_1
            + jnp.where(edge_level("east") > float(k), edge("cross_east", k) * east_step, 0.0)
            + jnp.where(edge_level("west") > float(k), edge("cross_west", k) * west_step, 0.0)
            + jnp.where(level_face > float(k), rows[5, k] * out_step, 0.0)
        )
        for name, inset, value in (("grad_h", 0, product), ("grad_h_1", 1, product_1)):
            value = value + roll(value, -1, 0)
            value = edge(name, k) - 0.5 * (value + roll(value, -2, 0))
            grad_h[k, inset : inset + 1] = value[:1]
            grad_h[k, ROWS - 1 - inset : ROWS - inset] = value[4:5]

    copies = [
        pltpu.make_async_copy(source, target, sems.at[n])
        for n, (source, target) in enumerate(
            ((adjoint, adjoint_out), (grad_h, grad_h_out), (grad_v, grad_v_out))
        )
    ]
    copies[0].start()
    copies[1].start()

    face_0 = face_1 = later_0 = later_1 = zero
    for k in range(depth + 1):
        if k < depth:
            above_0, above_1 = later_0, later_1
            later_0 = later[0, k] + edge("down_up", k) * later_0
            later_1 = later[1, k] + edge("down_up_1", k) * later_1
        if k == 0:
            continue
        next_0 = next_1 = zero
        if k < depth:
            step = rows[0, k - 1] - rows[0, k]
            next_0 = step * roll(step, -2, 0) + (edge("ahead", k - 1) - edge("ahead", k)) * (
                edge("after", k - 1) + above_0 - edge("after", k) - later_0
            )
            next_1 = (edge("ahead_1", k - 1) - edge("ahead_1", k)) * (above_1 - later_1)
            next_0 = jnp.where(
                edge_level("own") > float(k), next_0 + roll(next_0, -1, 0), 0.0
            )
            next_1 = jnp.where(
                edge_level("own_1") > float(k), next_1 + roll(next_1, -1, 0), 0.0
            )
        value_0 = -0.5 * (face_0 + next_0)
        value_1 = edge("grad_v_1", k - 1) - 0.5 * (face_1 + next_1)
        for inset, value in ((0, value_0), (1, value_1)):
            grad_v[k - 1, inset : inset + 1] = value[:1]
            grad_v[k - 1, ROWS - 1 - inset : ROWS - inset] = value[4:5]
        face_0, face_1 = next_0, next_1
    copies[2].start()
    for copy in copies:
        copy.wait()


def per_device(tracers, costate, mixing_h, mixing_v, levels, seam_code):
    depth = tracers.shape[1]
    tiles = depth // PER_TILE
    height = 10 * depth + 8
    params = pltpu.CompilerParams(vmem_limit_bytes=48 * 2**20)
    smem = pl.BlockSpec(memory_space=pltpu.SMEM)
    vmem = pl.BlockSpec(memory_space=pltpu.VMEM)
    hbm = pl.BlockSpec(memory_space=pltpu.HBM)
    tile = (ROWS, LANES)

    def flat(array):
        return array.reshape(-1, LANES)

    fields, factors, own, mix_h, mix_v, levels_here = pl.pallas_call(
        prepare,
        out_shape=(
            vmem_out(4 * depth * ROWS, LANES),
            vmem_out(3, depth, *tile),
            vmem_out(2 * tiles, *tile),
            vmem_out(depth, *tile),
            vmem_out(depth, *tile),
            pltpu.VMEM(tile, jnp.int32),
        ),
        in_specs=[smem] + [hbm] * 5,
        scratch_shapes=[pltpu.SemaphoreType.DMA((5,))],
        compiler_params=params,
        name="prepare",
    )(seam_code, *(in_hbm(a) for a in (flat(tracers), flat(costate), mixing_h, mixing_v, levels)))

    count = lax.axis_size("ty")
    near_pairs = [(i, i ^ 1) for i in range(count)]
    far_pairs = [(i, (i + 1 if i % 2 else i - 1) % count) for i in range(count)]
    far = lax.ppermute(own, "ty", far_pairs)
    near = lax.ppermute(own, "ty", near_pairs)

    def cost(work):
        return pl.CostEstimate(flops=work, bytes_accessed=work, transcendentals=0)

    def call(body, outs, *operands, **options):
        return pl.pallas_call(
            body, out_shape=outs, compiler_params=params, name=body.__name__, **options
        )(*(in_vmem(a) for a in operands))

    count = lax.axis_size("tx")
    upward = [(i, (i + 1) % count) for i in range(count)]
    downward = [(i, (i - 1) % count) for i in range(count)]
    upper = call(pack_up, vmem_out(height, LANES), fields, mix_h, mix_v, levels_here)
    from_below = lax.ppermute(upper, "tx", upward)
    merged, corner, rest = call(
        pack_sides,
        (vmem_out(2 * tiles, *tile), vmem_out(8, LANES), vmem_out(8, LANES)),
        near,
        far,
        own,
    )
    corner_below = lax.ppermute(corner, "tx", upward)
    lower = call(
        pack_down, vmem_out(height, LANES), merged, rest, fields, mix_h, mix_v, levels_here
    )
    from_above = lax.ppermute(lower, "tx", downward)
    row_block = (depth, 8, LANES)
    inside, steps, weights, columns, column_factors, up_factors, shallow = call(
        interior_down,
        (
            vmem_out(depth, 4 * ROWS, LANES),
            vmem_out(depth, 4, 4, *tile),
            vmem_out(depth, 4, *tile),
            vmem_out(depth, *tile),
            vmem_out(3, depth, *tile),
            vmem_out(3, depth, *tile),
            vmem_out(4, *tile),
        ),
        *(merged, own, fields, factors, mix_h, mix_v, levels_here, lower),
        scratch_shapes=[vmem_out(2, tiles, *tile)],
        cost_estimate=cost(30_000_000),
    )
    inside, after, adjoint, grad_h = call(
        interior_up,
        (
            vmem_out(depth, 4 * ROWS, LANES),
            vmem_out(depth, 4 * ROWS, LANES),
            vmem_out(2, depth, *tile),
            vmem_out(depth, *tile),
        ),
        *(inside, steps, weights, columns, column_factors, up_factors, shallow, factors),
        cost_estimate=cost(30_000_000),
    )
    edges, edge_levels, grad_v = call(
        interior_edges,
        (
            vmem_out(len(EDGES), *row_block),
            vmem_out(len(EDGE_LEVELS), 8, LANES),
            vmem_out(depth, *tile),
        ),
        *(merged, fields, factors, mix_h, levels_here, inside, after),
        *(weights, column_factors, up_factors, shallow, grad_h),
        scratch_shapes=[vmem_out(depth, 2 * ROWS, LANES)],
        cost_estimate=cost(40_000_000),
    )
    inner = (edges, edge_levels, adjoint, grad_h, grad_v)
    opened = pl.pallas_call(
        open_below,
        out_shape=vmem_out(2, 8, LANES),
        in_specs=[smem] + [vmem] * 3,
        compiler_params=params,
        cost_estimate=cost(900_000_000),
        name="open_below",
    )(seam_code, *(in_vmem(a) for a in (corner_below, merged, inner[1])))
    block = jax.ShapeDtypeStruct(mixing_h.shape, jnp.float32)
    return pl.pallas_call(
        finish,
        out_shape=(jax.ShapeDtypeStruct(tracers.shape, jnp.float32), block, block),
        in_specs=[smem] + [vmem] * 9,
        out_specs=(hbm, hbm, hbm),
        scratch_shapes=[
            vmem_out(height, LANES),
            vmem_out(height, LANES),
            vmem_out(6, *row_block),
            vmem_out(2, *row_block),
            vmem_out(2, depth, *tile),
            vmem_out(depth, *tile),
            vmem_out(depth, *tile),
            pltpu.SemaphoreType.DMA((3,)),
        ],
        compiler_params=params,
        name="finish",
    )(seam_code, *(in_vmem(a) for a in (from_below, from_above, opened, merged, *inner)))


def solution(mesh):
    placed = (
        P("members", None, "tx", "ty"),
        P("members", None, "tx", "ty"),
        P("members", "tx", "ty"),
        P("members", "tx", "ty"),
        P("tx", "ty"),
        P("ty"),
    )
    return jax.shard_map(
        per_device,
        mesh=mesh,
        in_specs=placed,
        out_specs=(
            P("members", None, "tx", "ty"),
            P("members", "tx", "ty"),
            P("members", "tx", "ty"),
        ),
        check_vma=False,
    )
```

```python
import jax
import jax.numpy as jnp
from jax import lax
from jax.experimental import pallas as pl
from jax.experimental.pallas import tpu as pltpu
from jax.sharding import PartitionSpec as P

LANES = 128
ROWS = 16
GROUP = 16
PER_TILE = LANES // GROUP


FILLER = 3


def in_vmem(array):
    return pltpu.with_memory_space_constraint(array, pltpu.VMEM)


def in_hbm(array):
    return pltpu.with_memory_space_constraint(array, pltpu.HBM)


def vmem_out(*shape):
    return pltpu.VMEM(shape, jnp.float32)


def iota(rows, dim):
    return lax.broadcasted_iota(jnp.int32, (rows, LANES), dim)


def roll(value, shift, axis):
    return pltpu.roll(value, shift % value.shape[axis], axis)


def fold(value):
    return jnp.where(iota(8, 0) < 4, value[:8], value[8:])


def east(value, halo):
    return jnp.where(iota(value.shape[0], 1) == LANES - 1, halo, roll(value, -1, 1))


def west(value, halo):
    return jnp.where(iota(value.shape[0], 1) == 0, halo, roll(value, 1, 1))


def rim(tile, base):
    return roll(tile, LANES - 2 - base, 1)


def crossed(tile):
    column = iota(tile.shape[0], 1) % 4
    return jnp.where(
        column == 1, roll(tile, -1, 1), jnp.where(column == 2, roll(tile, 1, 1), tile)
    )


def tile_of(q, k, depth):
    return slice((q * depth + k) * ROWS, (q * depth + k + 1) * ROWS)


def up(value):
    low, high = roll(value[:8], -1, 0), roll(value[8:], -1, 0)
    return jnp.concatenate([jnp.where(iota(8, 0) == 7, high, low), high], axis=0)


def down(value):
    low, high = roll(value[:8], 1, 0), roll(value[8:], 1, 0)
    return jnp.concatenate([low, jnp.where(iota(8, 0) == 0, low, high)], axis=0)


def bond(mix_v, level, k, depth):
    if k in (-1, depth - 1):
        return jnp.zeros(level.shape, jnp.float32)
    return jnp.where(level > k + 1, 0.5 * (mix_v[k] + mix_v[k + 1]), 0.0)


def factorize(depth, level, mix_v, put):
    bond_above = jnp.zeros(level.shape, jnp.float32)
    inverse = bond_above
    for k in range(depth):
        bond_here = bond(mix_v, level, k, depth)
        inverse = pivot(bond_above, bond_here, inverse)
        put(k, inverse, bond_above * inverse, bond_here * inverse)
        bond_above = bond_here


def pivot(bond_above, bond_here, inverse):
    return 1.0 / (1.0 + bond_above + bond_here - bond_above * bond_above * inverse)


def prepare(
    seam,
    tracers,
    costate,
    mix_h_in,
    mix_v_in,
    levels_in,
    fields,
    factors,
    message,
    mix_h,
    mix_v,
    levels,
    sems,
):
    depth = mix_h.shape[0]
    tiles = depth // PER_TILE
    copies = []
    for n, (source, target, parts) in enumerate(
        (
            (levels_in, levels, 1),
            (mix_v_in, mix_v, 4),
            (costate, fields.at[2 * depth * ROWS :], 4),
            (tracers, fields.at[: 2 * depth * ROWS], 4),
            (mix_h_in, mix_h, 4),
        )
    ):
        size = source.shape[0] // parts
        for m in range(parts):
            cut = slice(m * size, (m + 1) * size)
            pltpu.make_async_copy(source.at[cut], target.at[cut], sems.at[n]).start()
        copies.append(pltpu.make_async_copy(source, target, sems.at[n]))
    for copy in copies[:2]:
        copy.wait()
    level = levels[...]
    place = iota(ROWS, 1) // 4
    zero = jnp.zeros((ROWS, LANES), jnp.float32)

    def put(k, *three):
        for n in range(3):
            factors[n, k] = three[n]

    factorize(depth, level, mix_v, put)
    seconds = [jnp.where(place % 4 == FILLER, seam[0].astype(jnp.float32), zero)] * tiles
    level_f = level.astype(jnp.float32)
    for k in range(depth):
        tile, base = k // PER_TILE, GROUP * (k % PER_TILE)
        for n, value in ((1, mix_v[k]), (2, level_f)):
            seconds[tile] = jnp.where(
                place == base // 4 + n, roll(value, base + 4 * n + 2, 1), seconds[tile]
            )
    copies[2].wait()
    values = [zero, zero]
    for k in range(depth):
        for t in range(2):
            values[t] = fields[tile_of(2 + t, k, depth)] * factors[0, k] + factors[1, k] * values[t]
            fields[tile_of(2 + t, k, depth)] = values[t]
    firsts = [zero] * tiles
    values = [zero, zero]

    def add(k, q, value):
        tile, base = k // PER_TILE, GROUP * (k % PER_TILE) + 4 * q
        firsts[tile] = jnp.where(place == base // 4, roll(value, base + 2, 1), firsts[tile])

    for k in range(depth - 1, -1, -1):
        for t in range(2):
            values[t] = fields[tile_of(2 + t, k, depth)] + factors[2, k] * values[t]
            fields[tile_of(2 + t, k, depth)] = values[t]
            add(k, 2 + t, values[t])
    for copy in copies[3:]:
        copy.wait()
    for k in range(depth):
        tile, base = k // PER_TILE, GROUP * (k % PER_TILE)
        for t in range(2):
            add(k, t, fields[tile_of(t, k, depth)])
        seconds[tile] = jnp.where(
            place == base // 4, roll(mix_h[k], base + 2, 1), seconds[tile]
        )
    for tile in range(tiles):
        message[tile] = firsts[tile]
        message[tiles + tile] = seconds[tile]


def pack_rows(fields, mix_h, mix_v, levels, lower, upper):
    depth = mix_h.shape[0]
    sub = iota(8, 0)

    def nears(value):
        inner = jnp.where(sub < 4, roll(value, -1, 0), roll(value, 1, 0))
        return east(value, 0.0), west(value, 0.0), inner

    level = fold(levels[...].astype(jnp.float32))
    shallow = [jnp.minimum(level, near) for near in nears(level)]
    for k in range(depth):
        mix = fold(mix_h[k])
        weights = [
            jnp.where(open_to > float(k), 0.5 * (mix + near), 0.0)
            for open_to, near in zip(shallow, nears(mix))
        ]
        low = jnp.zeros((8, LANES), jnp.float32)
        high = low
        for q in range(4):
            value = fold(fields[tile_of(q, k, depth)])
            part = value
            for near, weight in zip(nears(value), weights):
                part = part + weight * (near - value)
            for n, thing in ((q, value), (4 + q, part)):
                low = jnp.where(sub == n, roll(thing, n, 0), low)
                high = jnp.where(sub == n, roll(thing, n - 7, 0), high)
        lower[8 * k : 8 * k + 8] = low
        upper[8 * k : 8 * k + 8] = high
        for n, array in enumerate((mix_h, mix_v)):
            start = (8 + n) * depth + k
            lower[start : start + 1] = array[k, :1]
            upper[start : start + 1] = array[k, ROWS - 1 :]
    lower[10 * depth : 10 * depth + 8] = stacked(level[:1])
    upper[10 * depth : 10 * depth + 8] = stacked(level[7:])


def pack_sides(near, far, own, early, merged, corner, lower):
    tiles = near.shape[0] // 2
    place = lax.axis_index("ty")
    last = lax.axis_size("ty") - 1
    even = place % 2 == 0
    column = iota(ROWS, 1) % 4
    corners = []
    edge = iota(8, 1) % 4
    for j in range(2 * tiles):
        west_tile = jnp.where(even, far[j], near[j])
        east_tile = jnp.where(even, near[j], far[j])
        if j >= tiles:
            west_tile = jnp.where(place == 0, 0.0, west_tile)
            east_tile = jnp.where(place == last, 0.0, east_tile)
        middle = jnp.where(column == 1, roll(east_tile, -1, 1), roll(west_tile, 1, 1))
        merged[j] = jnp.where(
            column == 0, west_tile, jnp.where(column == 3, east_tile, middle)
        )
        west_rows, east_rows = fold(west_tile), fold(east_tile)
        middle = jnp.where(edge == 1, roll(east_rows, -1, 1), roll(west_rows, 1, 1))
        corners.append(
            jnp.where(
                edge == 0,
                roll(west_rows, -2, 1),
                jnp.where(edge == 3, roll(east_rows, 2, 1), middle),
            )
        )
    lane = iota(1, 1)

    def for_row(row, sub):
        flows = []
        for j in range(tiles):
            level_k = (lane // GROUP + j * PER_TILE).astype(jnp.float32)
            mix, level = [
                [coefficient(ref[tiles + j, row : row + 1], n) for ref in (merged, own)]
                for n in (0, 2)
            ]
            weight = jnp.where(jnp.minimum(*level) > level_k, 0.5 * (mix[0] + mix[1]), 0.0)
            flows.append(weight * (merged[j, row : row + 1] - own[j, row : row + 1]))
        return [value[sub : sub + 1] for value in corners] + flows

    corner[...] = stacked(*for_row(ROWS - 1, 7))
    last_block = early.shape[0] - 8
    for r in range(0, last_block, 8):
        lower[r : r + 8] = early[r : r + 8]
    lower[last_block:] = stacked(early[last_block : last_block + 1], *for_row(0, 0))


def both(low, high):
    return jnp.where(iota(8, 0) < 4, low, high)


def coefficient(value, n):
    kept = iota(value.shape[0], 1) % GROUP // 4 == n
    value = jnp.where(kept, value, 0.0)
    out = roll(value, -4 * n, 1)
    for q in range(1, 4):
        out = out + roll(value, 4 * (q - n), 1)
    return out


EDGES = (
    "field",
    "mix",
    "inv_down",
    "up_down",
    "down_down",
    "inv_up",
    "up_up",
    "down_up",
    "inv_up_1",
    "up_up_1",
    "down_up_1",
    "to_east",
    "to_west",
    "to_inner",
    "cross_east",
    "cross_west",
    "cross_inner",
    "inside",
    "after",
    "after_1",
    "ahead",
    "ahead_1",
    "grad_h",
    "grad_h_1",
    "grad_v_1",
    "column",
    "mix_column",
    "inv_column",
    "up_column",
    "down_column",
)
EDGE_LEVELS = ("own", "own_1", "east", "west", "inner", "column")


def exchange(value):
    return jnp.where(iota(8, 0) % 4 < 2, roll(value, -2, 0), roll(value, 2, 0))


def at_edges(rows, shift):
    sub = iota(8, 0) % 4
    out = roll(rows, LANES - 2 - shift, 1)
    for q in range(1, 4):
        out = jnp.where(sub == q, roll(rows, LANES - 2 - shift - 4 * q, 1), out)
    return jnp.broadcast_to(out, (8, LANES))


def stacked(*rows):
    sub = iota(8, 0)
    out = jnp.zeros((8, LANES), jnp.float32)
    for n, row in enumerate(rows):
        if row is not None:
            out = jnp.where(sub == n, row, out)
    return out


def nears_of(value, halo):
    return east(value, halo), west(value, halo), up(value), down(value)


def at(q):
    return slice(q * ROWS, (q + 1) * ROWS)


def interior_down(
    merged,
    own,
    fields,
    factors,
    mix_h,
    mix_v,
    levels,
    sent,
    inside,
    steps,
    weights,
    columns,
    column_factors,
    up_factors,
    shallow_out,
    packed,
):
    depth = mix_h.shape[0]
    tiles = depth // PER_TILE
    lane = iota(ROWS, 1)
    zero = jnp.zeros((ROWS, LANES), jnp.float32)
    level = levels[...]
    face_below = inverse = zero
    for k in range(depth - 1, -1, -1):
        face_above = bond(mix_v, level, k - 1, depth)
        inverse = pivot(face_below, face_above, inverse)
        up_factors[0, k] = inverse
        up_factors[1, k] = face_below * inverse
        up_factors[2, k] = face_above * inverse
        face_below = face_above

    column = lane % 4
    last_row, first_row = iota(ROWS, 0) == ROWS - 1, iota(ROWS, 0) == 0
    for j in range(tiles):
        level_k = (lane // GROUP + j * PER_TILE).astype(jnp.float32)
        mix, bonds, depths = [coefficient(merged[tiles + j], n) for n in range(3)]
        own_mix, own_depths = [coefficient(own[tiles + j], n) for n in (0, 2)]
        value = merged[j]

        def outer(array):
            return jnp.where(column == 1, roll(array, -2, 1), roll(array, 2, 1))

        def weight(near_depths, near_mix):
            return jnp.where(
                jnp.minimum(depths, near_depths) > level_k, 0.5 * (mix + near_mix), 0.0
            )

        mixed = value + weight(own_depths, own_mix) * (own[j] - value)
        mixed = mixed + weight(outer(depths), outer(mix)) * (outer(value) - value)
        for border, shift in ((last_row, up), (first_row, down)):
            flow = weight(shift(depths), shift(mix)) * (shift(value) - value)
            mixed = mixed + jnp.where(border, 0.0, flow)
        packed[0, j] = mixed
        packed[1, j] = bonds
        if j == 0:
            level_columns = depths

    def unpacked(n, k):
        return roll(packed[n, k // PER_TILE], -GROUP * (k % PER_TILE), 1)

    level = level.astype(jnp.float32)
    shallow = [jnp.minimum(level, near) for near in nears_of(level, rim(merged[tiles], 8))]
    shallow[2] = jnp.where(last_row, 0.0, shallow[2])
    shallow[3] = jnp.where(first_row, 0.0, shallow[3])
    for n in range(4):
        shallow_out[n] = shallow[n]

    bond_above = col_inverse = col_value = zero
    values = [zero] * 4
    for k in range(depth):
        j, i = divmod(k, PER_TILE)
        under = min(k + 1, depth - 1)
        bond_here = jnp.where(
            level_columns > k + 1.0, 0.5 * (unpacked(1, k) + unpacked(1, under)), 0.0
        )
        col_inverse = pivot(bond_above, bond_here, col_inverse)
        col_factor = bond_above * col_inverse
        col_value = unpacked(0, k) * col_inverse + col_factor * col_value
        columns[k] = col_value
        column_factors[0, k] = col_inverse
        column_factors[1, k] = col_factor
        column_factors[2, k] = bond_here * col_inverse
        bond_above = bond_here
        mix = mix_h[k]
        weight = [
            jnp.where(open_to > float(k), 0.5 * (mix + near), 0.0)
            for open_to, near in zip(shallow, nears_of(mix, rim(merged[tiles + j], GROUP * i)))
        ]
        for n in range(4):
            weights[k, n] = weight[n]
        for q in range(4):
            value = fields[tile_of(q, k, depth)]
            step = [near - value for near in nears_of(value, rim(merged[j], GROUP * i + 4 * q))]
            for n in range(4):
                steps[k, q, n] = step[n]
                value = value + weight[n] * step[n]
            values[q] = value * factors[0, k] + factors[1, k] * values[q]
            inside[k, at(q)] = values[q]


def interior_up(
    inside_in,
    steps,
    weights,
    columns,
    column_factors,
    up_factors,
    shallow_in,
    factors,
    inside,
    after,
    adjoint,
    grad_h,
):
    depth = grad_h.shape[0]
    zero = jnp.zeros((ROWS, LANES), jnp.float32)
    shallow = [shallow_in[n] for n in range(4)]
    col_value = zero
    values = [zero] * 4
    later_values = [zero] * 2
    for k in range(depth - 1, -1, -1):
        col_value = columns[k] + column_factors[2, k] * col_value
        later_steps = []
        for q in range(4):
            value = inside_in[k, at(q)] + factors[2, k] * values[q]
            inside[k, at(q)] = value
            values[q] = value
            step = [near - value for near in nears_of(value, rim(col_value, 4 * q))]
            later_steps.append(step)
            for n in range(4):
                value = value + weights[k, n] * step[n]
            if q < 2:
                later_values[q] = value * up_factors[0, k] + up_factors[1, k] * later_values[q]
                value = later_values[q]
            else:
                adjoint[q - 2, k] = value
            after[k, at(q)] = value
        total = zero
        for n in range(4):
            face = zero
            for t in range(2):
                face = face + steps[k, t, n] * later_steps[2 + t][n]
                face = face + later_steps[t][n] * steps[k, 2 + t, n]
            total = total + jnp.where(shallow[n] > float(k), face, 0.0)
        grad_h[k] = -0.5 * total


def interior_edges(
    merged,
    fields,
    factors,
    mix_h,
    levels,
    inside,
    after,
    weights,
    column_factors,
    up_factors,
    shallow,
    grad_h,
    edges,
    edge_levels,
    grad_v,
    later,
):
    depth = mix_h.shape[0]
    tiles = depth // PER_TILE
    zero = jnp.zeros((ROWS, LANES), jnp.float32)
    level = levels[...].astype(jnp.float32)
    face_above = zero
    for t in range(2):
        later[0, at(t)] = after[0, at(t)]
    for k in range(depth):
        if k > 0:
            total = zero
            for t in range(2):
                later_here = after[k, at(t)] + up_factors[2, k] * later[k - 1, at(t)]
                later[k, at(t)] = later_here
                total = total + (inside[k - 1, at(2 + t)] - inside[k, at(2 + t)]) * (
                    inside[k - 1, at(t)] - inside[k, at(t)]
                )
                total = total + (
                    fields[tile_of(2 + t, k - 1, depth)] - fields[tile_of(2 + t, k, depth)]
                ) * (later[k - 1, at(t)] - later_here)
            face = jnp.where(level > float(k), total, 0.0)
            grad_v[k - 1] = -0.5 * (face + face_above)
            face_above = face
    grad_v[depth - 1] = -0.5 * face_above

    def ends(value, inset=0):
        return both(value[inset : inset + 1], value[ROWS - 1 - inset : ROWS - inset])

    def four(ref, start, stride, inset=0):
        low, high = start + inset, start + ROWS - 1 - inset
        return stacked(
            *(ref[row + q * stride : row + q * stride + 1] for row in (low, high) for q in range(4))
        )

    last_lane, first_lane = iota(8, 1) == LANES - 1, iota(8, 1) == 0

    coef_rows = ends(merged[tiles])
    for n, value in enumerate(
        (
            ends(level),
            ends(level, 1),
            ends(shallow[0]),
            ends(shallow[1]),
            both(shallow[2, :1], shallow[3, ROWS - 1 :]),
            rim(coef_rows, 8),
        )
    ):
        edge_levels[n] = value

    for k in range(depth):
        j, i = divmod(k, PER_TILE)
        field = four(fields, k * ROWS, depth * ROWS)
        field_1 = four(fields, k * ROWS, depth * ROWS, 1)
        column = at_edges(ends(merged[j]), GROUP * i)
        things = dict(
            field=field,
            mix=ends(mix_h[k]),
            to_east=ends(weights[k, 0]),
            to_west=ends(weights[k, 1]),
            to_inner=both(weights[k, 2, :1], weights[k, 3, ROWS - 1 :]),
            cross_east=exchange(jnp.where(last_lane, column, roll(field, -1, 1)) - field),
            cross_west=exchange(jnp.where(first_lane, column, roll(field, 1, 1)) - field),
            cross_inner=exchange(field_1 - field),
            inside=four(inside.at[k], 0, ROWS),
            after=stacked(
                *(
                    (later if q < 2 else after)[k, q * ROWS + row : q * ROWS + row + 1]
                    for row in (0, ROWS - 1)
                    for q in range(4)
                )
            ),
            after_1=four(after.at[k], 0, ROWS, 1),
            ahead=roll(field, -2, 0),
            ahead_1=roll(field_1, -2, 0),
            grad_h=ends(grad_h[k]),
            grad_h_1=ends(grad_h[k], 1),
            grad_v_1=ends(grad_v[k], 1),
            column=column,
            mix_column=rim(ends(merged[tiles + j]), GROUP * i),
        )
        for n, name in enumerate(("inv", "up", "down")):
            things[name + "_down"] = ends(factors[n, k])
            things[name + "_up"] = ends(up_factors[n, k])
            things[name + "_up_1"] = ends(up_factors[n, k], 1)
            things[name + "_column"] = rim(ends(column_factors[n, k]), 0)
        for name, value in things.items():
            edges[EDGES.index(name), k] = value


def turned_corner(block, merged, tiles, border):
    code = coefficient(merged[tiles, :8], FILLER)[:1]
    swapped = jnp.where(iota(8, 1) % 4 == 1, roll(block, -2, 1), roll(block, 2, 1))
    return jnp.where((lax.axis_index("tx") == border) & (code > 0.5), swapped, block)


def open_below(seam, corner, merged, edge_levels, opened):
    tiles = merged.shape[0] // 2
    turn = (seam[0] == 1) & (lax.axis_index("tx") == 0)
    block = corner[...]
    flows = jnp.where(turn, crossed(block), block)
    block = turned_corner(block, merged, tiles, 0)
    opened[0] = jnp.where(iota(8, 0) < 2 * tiles, block, flows)
    opened[1] = jnp.minimum(
        rim(block[tiles : tiles + 1], 8), edge_levels[EDGE_LEVELS.index("column")]
    )


def finish(
    seam,
    from_below,
    from_above,
    opened,
    merged,
    edges,
    edge_levels,
    adjoint_in,
    grad_h_in,
    grad_v_in,
    adjoint_out,
    grad_h_out,
    grad_v_out,
    below,
    above,
    rows,
    later,
    adjoint,
    grad_h,
    grad_v,
    sems,
):
    depth, tiles = grad_h.shape[0], grad_h.shape[0] // PER_TILE
    sub = iota(8, 0)
    lane = iota(8, 1)
    place = lax.axis_index("tx")
    last = lax.axis_size("tx") - 1
    base_mix, base_v, base_level = 8 * depth, 9 * depth, 10 * depth
    zero = jnp.zeros((8, LANES), jnp.float32)

    def edge(name, k):
        return edges[EDGES.index(name), k]

    def edge_level(name):
        return edge_levels[EDGE_LEVELS.index(name)]

    for source, target, border in ((from_below, below, 0), (from_above, above, last)):
        turn = (seam[0] == 1) & (place == border)

        @pl.when(turn)
        def _():
            back = LANES - 1 - lane
            for r in range(0, base_level, 8):
                target[r : r + 8] = jnp.take_along_axis(source[r : r + 8], back, axis=1)
            block = source[base_level : base_level + 8]
            target[base_level : base_level + 8] = jnp.where(
                sub < 1, jnp.take_along_axis(block, back, axis=1), block
            )

        @pl.when(jnp.logical_not(turn))
        def _():
            for r in range(0, base_level + 8, 8):
                target[r : r + 8] = source[r : r + 8]

    for k in range(depth):
        for t in range(2):
            adjoint[t, k] = adjoint_in[t, k]
        grad_h[k] = grad_h_in[k]
        grad_v[k] = grad_v_in[k]

    last_block = above[base_level : base_level + 8]
    corner_above = turned_corner(last_block, merged, tiles, last)
    turn_above = (seam[0] == 1) & (place == last)
    flows_above = jnp.where(turn_above, crossed(last_block), last_block)

    def corner(r):
        return both(opened[0, r : r + 1], corner_above[1 + r : 2 + r])

    def flow_of(j):
        r = 2 * tiles + j
        return both(opened[0, r : r + 1], flows_above[1 + r : 2 + r])

    beside = (lane == 0) | (lane == LANES - 1)

    def outer(start, k=0):
        at = slice(start + k, start + k + 1)
        return both(below[at], above[at])

    level_out = outer(base_level)
    level_face = jnp.minimum(level_out, edge_level("own"))
    level_corner = both(
        opened[1],
        jnp.minimum(rim(corner_above[1 + tiles : 2 + tiles], 8), edge_level("column")),
    )

    bond_above = inverse = out_value = added = column_added = zero
    flows = []
    for k in range(depth):
        j, i = divmod(k, PER_TILE)
        block = slice(8 * k, 8 * k + 8)
        below_block, above_block = below[block], above[block]
        bond_here = jnp.where(
            level_out > k + 1.0,
            0.5 * (outer(base_v, k) + outer(base_v, min(k + 1, depth - 1))),
            0.0,
        )
        inverse = pivot(bond_above, bond_here, inverse)
        out = both(below_block, roll(above_block, 4, 0))
        part = both(roll(below_block, 4, 0), above_block) + jnp.where(
            beside, at_edges(flow_of(j), GROUP * i), 0.0
        )
        step = out - edge("field", k)
        weight = jnp.where(level_face > float(k), 0.5 * (outer(base_mix, k) + edge("mix", k)), 0.0)
        flow = weight * step
        out_value = (part - flow) * inverse + bond_above * inverse * out_value
        added = flow * edge("inv_down", k) + edge("up_down", k) * added
        mix_corner = rim(corner(tiles + j), GROUP * i)
        weight_corner = jnp.where(
            level_corner > float(k), 0.5 * (mix_corner + edge("mix_column", k)), 0.0
        )
        step_corner = at_edges(corner(j), GROUP * i) - edge("column", k)
        column_added = (
            weight_corner * step_corner * edge("inv_column", k)
            + edge("up_column", k) * column_added
        )
        rows[0, k] = out_value
        rows[1, k] = bond_here * inverse
        rows[2, k] = added
        rows[3, k] = column_added
        rows[4, k] = weight
        rows[5, k] = exchange(step)
        bond_above = bond_here

    out_value = added = column_added = later_0 = later_1 = zero
    for k in range(depth - 1, -1, -1):
        out_value = rows[0, k] + rows[1, k] * out_value
        added = rows[2, k] + edge("down_down", k) * added
        column_added = rows[3, k] + edge("down_column", k) * column_added
        value = edge("inside", k) + added
        rows[0, k] = value
        east_step = jnp.where(lane == LANES - 1, column_added, roll(added, -1, 1)) - added
        west_step = jnp.where(lane == 0, column_added, roll(added, 1, 1)) - added
        out_step = out_value - value
        inner_flow = edge("to_inner", k) * added
        change = (
            added
            + edge("to_east", k) * east_step
            + edge("to_west", k) * west_step
            - inner_flow
            + rows[4, k] * out_step
        )
        later_0 = change * edge("inv_up", k) + edge("up_up", k) * later_0
        later_1 = inner_flow * edge("inv_up_1", k) + edge("up_up_1", k) * later_1
        later[0, k] = later_0
        later[1, k] = later_1
        result = edge("after", k) + change
        result_1 = edge("after_1", k) + inner_flow
        for t in range(2):
            for at, source, row in (
                (0, result, 2),
                (ROWS - 1, result, 6),
                (1, result_1, 2),
                (ROWS - 2, result_1, 6),
            ):
                adjoint[t, k, at : at + 1] = source[row + t : row + t + 1]
        product_1 = jnp.where(
            edge_level("inner") > float(k), -edge("cross_inner", k) * added, 0.0
        )
        product = (
            product_1
            + jnp.where(edge_level("east") > float(k), edge("cross_east", k) * east_step, 0.0)
            + jnp.where(edge_level("west") > float(k), edge("cross_west", k) * west_step, 0.0)
            + jnp.where(level_face > float(k), rows[5, k] * out_step, 0.0)
        )
        for name, inset, value in (("grad_h", 0, product), ("grad_h_1", 1, product_1)):
            value = value + roll(value, -1, 0)
            value = edge(name, k) - 0.5 * (value + roll(value, -2, 0))
            grad_h[k, inset : inset + 1] = value[:1]
            grad_h[k, ROWS - 1 - inset : ROWS - inset] = value[4:5]

    copies = [
        pltpu.make_async_copy(source, target, sems.at[n])
        for n, (source, target) in enumerate(
            ((adjoint, adjoint_out), (grad_h, grad_h_out), (grad_v, grad_v_out))
        )
    ]
    copies[0].start()
    copies[1].start()

    face_0 = face_1 = later_0 = later_1 = zero
    for k in range(depth + 1):
        if k < depth:
            above_0, above_1 = later_0, later_1
            later_0 = later[0, k] + edge("down_up", k) * later_0
            later_1 = later[1, k] + edge("down_up_1", k) * later_1
        if k == 0:
            continue
        next_0 = next_1 = zero
        if k < depth:
            step = rows[0, k - 1] - rows[0, k]
            next_0 = step * roll(step, -2, 0) + (edge("ahead", k - 1) - edge("ahead", k)) * (
                edge("after", k - 1) + above_0 - edge("after", k) - later_0
            )
            next_1 = (edge("ahead_1", k - 1) - edge("ahead_1", k)) * (above_1 - later_1)
            next_0 = jnp.where(
                edge_level("own") > float(k), next_0 + roll(next_0, -1, 0), 0.0
            )
            next_1 = jnp.where(
                edge_level("own_1") > float(k), next_1 + roll(next_1, -1, 0), 0.0
            )
        value_0 = -0.5 * (face_0 + next_0)
        value_1 = edge("grad_v_1", k - 1) - 0.5 * (face_1 + next_1)
        for inset, value in ((0, value_0), (1, value_1)):
            grad_v[k - 1, inset : inset + 1] = value[:1]
            grad_v[k - 1, ROWS - 1 - inset : ROWS - inset] = value[4:5]
        face_0, face_1 = next_0, next_1
    copies[2].start()
    for copy in copies:
        copy.wait()


def per_device(tracers, costate, mixing_h, mixing_v, levels, seam_code):
    depth = tracers.shape[1]
    tiles = depth // PER_TILE
    height = 10 * depth + 8
    params = pltpu.CompilerParams(vmem_limit_bytes=48 * 2**20)
    smem = pl.BlockSpec(memory_space=pltpu.SMEM)
    vmem = pl.BlockSpec(memory_space=pltpu.VMEM)
    hbm = pl.BlockSpec(memory_space=pltpu.HBM)
    tile = (ROWS, LANES)

    def flat(array):
        return array.reshape(-1, LANES)

    fields, factors, own, mix_h, mix_v, levels_here = pl.pallas_call(
        prepare,
        out_shape=(
            vmem_out(4 * depth * ROWS, LANES),
            vmem_out(3, depth, *tile),
            vmem_out(2 * tiles, *tile),
            vmem_out(depth, *tile),
            vmem_out(depth, *tile),
            pltpu.VMEM(tile, jnp.int32),
        ),
        in_specs=[smem] + [hbm] * 5,
        scratch_shapes=[pltpu.SemaphoreType.DMA((5,))],
        compiler_params=params,
        name="prepare",
    )(seam_code, *(in_hbm(a) for a in (flat(tracers), flat(costate), mixing_h, mixing_v, levels)))

    count = lax.axis_size("ty")
    near_pairs = [(i, i ^ 1) for i in range(count)]
    far_pairs = [(i, (i + 1 if i % 2 else i - 1) % count) for i in range(count)]
    far = lax.ppermute(own, "ty", far_pairs)
    near = lax.ppermute(own, "ty", near_pairs)

    def cost(work):
        return pl.CostEstimate(flops=work, bytes_accessed=work, transcendentals=0)

    def call(body, outs, *operands, **options):
        return pl.pallas_call(
            body, out_shape=outs, compiler_params=params, name=body.__name__, **options
        )(*(in_vmem(a) for a in operands))

    count = lax.axis_size("tx")
    upward = [(i, (i + 1) % count) for i in range(count)]
    downward = [(i, (i - 1) % count) for i in range(count)]
    early, upper = call(
        pack_rows,
        (vmem_out(height, LANES), vmem_out(height, LANES)),
        *(fields, mix_h, mix_v, levels_here),
    )
    from_below = lax.ppermute(upper, "tx", upward)
    merged, corner, lower = call(
        pack_sides,
        (vmem_out(2 * tiles, *tile), vmem_out(8, LANES), vmem_out(height, LANES)),
        *(near, far, own, early),
    )
    corner_below = lax.ppermute(corner, "tx", upward)
    from_above = lax.ppermute(lower, "tx", downward)
    row_block = (depth, 8, LANES)
    inside, steps, weights, columns, column_factors, up_factors, shallow = call(
        interior_down,
        (
            vmem_out(depth, 4 * ROWS, LANES),
            vmem_out(depth, 4, 4, *tile),
            vmem_out(depth, 4, *tile),
            vmem_out(depth, *tile),
            vmem_out(3, depth, *tile),
            vmem_out(3, depth, *tile),
            vmem_out(4, *tile),
        ),
        *(merged, own, fields, factors, mix_h, mix_v, levels_here, lower),
        scratch_shapes=[vmem_out(2, tiles, *tile)],
        cost_estimate=cost(30_000_000),
    )
    inside, after, adjoint, grad_h = call(
        interior_up,
        (
            vmem_out(depth, 4 * ROWS, LANES),
            vmem_out(depth, 4 * ROWS, LANES),
            vmem_out(2, depth, *tile),
            vmem_out(depth, *tile),
        ),
        *(inside, steps, weights, columns, column_factors, up_factors, shallow, factors),
        cost_estimate=cost(30_000_000),
    )
    edges, edge_levels, grad_v = call(
        interior_edges,
        (
            vmem_out(len(EDGES), *row_block),
            vmem_out(len(EDGE_LEVELS), 8, LANES),
            vmem_out(depth, *tile),
        ),
        *(merged, fields, factors, mix_h, levels_here, inside, after),
        *(weights, column_factors, up_factors, shallow, grad_h),
        scratch_shapes=[vmem_out(depth, 2 * ROWS, LANES)],
        cost_estimate=cost(40_000_000),
    )
    inner = (edges, edge_levels, adjoint, grad_h, grad_v)
    opened = pl.pallas_call(
        open_below,
        out_shape=vmem_out(2, 8, LANES),
        in_specs=[smem] + [vmem] * 3,
        compiler_params=params,
        cost_estimate=cost(900_000_000),
        name="open_below",
    )(seam_code, *(in_vmem(a) for a in (corner_below, merged, inner[1])))
    block = jax.ShapeDtypeStruct(mixing_h.shape, jnp.float32)
    return pl.pallas_call(
        finish,
        out_shape=(jax.ShapeDtypeStruct(tracers.shape, jnp.float32), block, block),
        in_specs=[smem] + [vmem] * 9,
        out_specs=(hbm, hbm, hbm),
        scratch_shapes=[
            vmem_out(height, LANES),
            vmem_out(height, LANES),
            vmem_out(6, *row_block),
            vmem_out(2, *row_block),
            vmem_out(2, depth, *tile),
            vmem_out(depth, *tile),
            vmem_out(depth, *tile),
            pltpu.SemaphoreType.DMA((3,)),
        ],
        compiler_params=params,
        name="finish",
    )(seam_code, *(in_vmem(a) for a in (from_below, from_above, opened, merged, *inner)))


def solution(mesh):
    placed = (
        P("members", None, "tx", "ty"),
        P("members", None, "tx", "ty"),
        P("members", "tx", "ty"),
        P("members", "tx", "ty"),
        P("tx", "ty"),
        P("ty"),
    )
    return jax.shard_map(
        per_device,
        mesh=mesh,
        in_specs=placed,
        out_specs=(
            P("members", None, "tx", "ty"),
            P("members", "tx", "ty"),
            P("members", "tx", "ty"),
        ),
        check_vma=False,
    )
```

```python
import jax
import jax.numpy as jnp
from jax import lax
from jax.experimental import pallas as pl
from jax.experimental.pallas import tpu as pltpu
from jax.sharding import PartitionSpec as P

LANES = 128
ROWS = 16
GROUP = 16
PER_TILE = LANES // GROUP


FILLER = 3


def in_vmem(array):
    return pltpu.with_memory_space_constraint(array, pltpu.VMEM)


def in_hbm(array):
    return pltpu.with_memory_space_constraint(array, pltpu.HBM)


def vmem_out(*shape):
    return pltpu.VMEM(shape, jnp.float32)


def iota(rows, dim):
    return lax.broadcasted_iota(jnp.int32, (rows, LANES), dim)


def roll(value, shift, axis):
    return pltpu.roll(value, shift % value.shape[axis], axis)


def fold(value):
    return jnp.where(iota(8, 0) < 4, value[:8], value[8:])


def east(value, halo):
    return jnp.where(iota(value.shape[0], 1) == LANES - 1, halo, roll(value, -1, 1))


def west(value, halo):
    return jnp.where(iota(value.shape[0], 1) == 0, halo, roll(value, 1, 1))


def rim(tile, base):
    return roll(tile, LANES - 2 - base, 1)


def crossed(tile):
    column = iota(tile.shape[0], 1) % 4
    return jnp.where(
        column == 1, roll(tile, -1, 1), jnp.where(column == 2, roll(tile, 1, 1), tile)
    )


def tile_of(q, k, depth):
    return slice((q * depth + k) * ROWS, (q * depth + k + 1) * ROWS)


def up(value):
    low, high = roll(value[:8], -1, 0), roll(value[8:], -1, 0)
    return jnp.concatenate([jnp.where(iota(8, 0) == 7, high, low), high], axis=0)


def down(value):
    low, high = roll(value[:8], 1, 0), roll(value[8:], 1, 0)
    return jnp.concatenate([low, jnp.where(iota(8, 0) == 0, low, high)], axis=0)


def bond(mix_v, level, k, depth):
    if k in (-1, depth - 1):
        return jnp.zeros(level.shape, jnp.float32)
    return jnp.where(level > k + 1, 0.5 * (mix_v[k] + mix_v[k + 1]), 0.0)


def factorize(depth, level, mix_v, put):
    bond_above = jnp.zeros(level.shape, jnp.float32)
    inverse = bond_above
    for k in range(depth):
        bond_here = bond(mix_v, level, k, depth)
        inverse = pivot(bond_above, bond_here, inverse)
        put(k, inverse, bond_above * inverse, bond_here * inverse)
        bond_above = bond_here


def pivot(bond_above, bond_here, inverse):
    return 1.0 / (1.0 + bond_above + bond_here - bond_above * bond_above * inverse)


def prepare(
    seam,
    tracers,
    costate,
    mix_h_in,
    mix_v_in,
    levels_in,
    fields,
    factors,
    message,
    mix_h,
    mix_v,
    levels,
    sems,
):
    depth = mix_h.shape[0]
    tiles = depth // PER_TILE
    copies = []
    for n, (source, target, parts) in enumerate(
        (
            (levels_in, levels, 1),
            (mix_v_in, mix_v, 4),
            (tracers, fields.at[: 2 * depth * ROWS], 4),
            (mix_h_in, mix_h, 4),
            (costate, fields.at[2 * depth * ROWS :], 4),
        )
    ):
        size = source.shape[0] // parts
        for m in range(parts):
            cut = slice(m * size, (m + 1) * size)
            pltpu.make_async_copy(source.at[cut], target.at[cut], sems.at[n]).start()
        copies.append(pltpu.make_async_copy(source, target, sems.at[n]))
    for copy in copies[:2]:
        copy.wait()
    level = levels[...]
    place = iota(ROWS, 1) // 4
    zero = jnp.zeros((ROWS, LANES), jnp.float32)

    def put(k, *three):
        for n in range(3):
            factors[n, k] = three[n]

    factorize(depth, level, mix_v, put)
    seconds = [jnp.where(place % 4 == FILLER, seam[0].astype(jnp.float32), zero)] * tiles
    level_f = level.astype(jnp.float32)
    for k in range(depth):
        tile, base = k // PER_TILE, GROUP * (k % PER_TILE)
        for n, value in ((1, mix_v[k]), (2, level_f)):
            seconds[tile] = jnp.where(
                place == base // 4 + n, roll(value, base + 4 * n + 2, 1), seconds[tile]
            )
    firsts = [zero] * tiles

    def add(k, q, value):
        tile, base = k // PER_TILE, GROUP * (k % PER_TILE) + 4 * q
        firsts[tile] = jnp.where(place == base // 4, roll(value, base + 2, 1), firsts[tile])

    for copy in copies[2:4]:
        copy.wait()
    for k in range(depth):
        tile, base = k // PER_TILE, GROUP * (k % PER_TILE)
        for t in range(2):
            add(k, t, fields[tile_of(t, k, depth)])
        seconds[tile] = jnp.where(
            place == base // 4, roll(mix_h[k], base + 2, 1), seconds[tile]
        )
    copies[4].wait()
    values = [zero, zero]
    for k in range(depth):
        for t in range(2):
            values[t] = fields[tile_of(2 + t, k, depth)] * factors[0, k] + factors[1, k] * values[t]
            fields[tile_of(2 + t, k, depth)] = values[t]
    values = [zero, zero]
    for k in range(depth - 1, -1, -1):
        for t in range(2):
            values[t] = fields[tile_of(2 + t, k, depth)] + factors[2, k] * values[t]
            fields[tile_of(2 + t, k, depth)] = values[t]
            add(k, 2 + t, values[t])
    for tile in range(tiles):
        message[tile] = firsts[tile]
        message[tiles + tile] = seconds[tile]


def pack_rows(fields, mix_h, mix_v, levels, lower, upper):
    depth = mix_h.shape[0]
    sub = iota(8, 0)

    def nears(value):
        inner = jnp.where(sub < 4, roll(value, -1, 0), roll(value, 1, 0))
        return east(value, 0.0), west(value, 0.0), inner

    level = fold(levels[...].astype(jnp.float32))
    shallow = [jnp.minimum(level, near) for near in nears(level)]
    for k in range(depth):
        mix = fold(mix_h[k])
        weights = [
            jnp.where(open_to > float(k), 0.5 * (mix + near), 0.0)
            for open_to, near in zip(shallow, nears(mix))
        ]
        low = jnp.zeros((8, LANES), jnp.float32)
        high = low
        for q in range(4):
            value = fold(fields[tile_of(q, k, depth)])
            part = value
            for near, weight in zip(nears(value), weights):
                part = part + weight * (near - value)
            for n, thing in ((q, value), (4 + q, part)):
                low = jnp.where(sub == n, roll(thing, n, 0), low)
                high = jnp.where(sub == n, roll(thing, n - 7, 0), high)
        lower[8 * k : 8 * k + 8] = low
        upper[8 * k : 8 * k + 8] = high
        at_mix = slice(8 * depth + k, 8 * depth + k + 1)
        lower[at_mix] = mix_h[k, :1]
        upper[at_mix] = mix_h[k, ROWS - 1 :]
        if k < depth - 1:
            between = 0.5 * (mix_v[k] + mix_v[k + 1])
            at_bond = slice(9 * depth + k, 9 * depth + k + 1)
            lower[at_bond] = between[:1]
            upper[at_bond] = between[ROWS - 1 :]
    lower[10 * depth - 1 :] = level[:1]
    upper[10 * depth - 1 :] = level[7:]


def pack_sides(near, far, own, early, merged, corner, lower):
    tiles = near.shape[0] // 2
    place = lax.axis_index("ty")
    last = lax.axis_size("ty") - 1
    even = place % 2 == 0
    column = iota(ROWS, 1) % 4
    corners = []
    edge = iota(8, 1) % 4
    for j in range(2 * tiles):
        west_tile = jnp.where(even, far[j], near[j])
        east_tile = jnp.where(even, near[j], far[j])
        if j >= tiles:
            west_tile = jnp.where(place == 0, 0.0, west_tile)
            east_tile = jnp.where(place == last, 0.0, east_tile)
        middle = jnp.where(column == 1, roll(east_tile, -1, 1), roll(west_tile, 1, 1))
        merged[j] = jnp.where(
            column == 0, west_tile, jnp.where(column == 3, east_tile, middle)
        )
        west_rows, east_rows = fold(west_tile), fold(east_tile)
        middle = jnp.where(edge == 1, roll(east_rows, -1, 1), roll(west_rows, 1, 1))
        corners.append(
            jnp.where(
                edge == 0,
                roll(west_rows, -2, 1),
                jnp.where(edge == 3, roll(east_rows, 2, 1), middle),
            )
        )
    lane = iota(1, 1)

    def for_row(row, sub):
        flows = []
        for j in range(tiles):
            level_k = (lane // GROUP + j * PER_TILE).astype(jnp.float32)
            mix, level = [
                [coefficient(ref[tiles + j, row : row + 1], n) for ref in (merged, own)]
                for n in (0, 2)
            ]
            weight = jnp.where(jnp.minimum(*level) > level_k, 0.5 * (mix[0] + mix[1]), 0.0)
            flows.append(weight * (merged[j, row : row + 1] - own[j, row : row + 1]))
        return [value[sub : sub + 1] for value in corners] + flows

    corner[...] = stacked(*for_row(ROWS - 1, 7))
    size = early.shape[0]
    for r in range(0, size, 8):
        lower[r : r + 8] = early[r : r + 8]
    lower[size:] = stacked(*for_row(0, 0))


def both(low, high):
    return jnp.where(iota(8, 0) < 4, low, high)


def coefficient(value, n):
    kept = iota(value.shape[0], 1) % GROUP // 4 == n
    value = jnp.where(kept, value, 0.0)
    out = roll(value, -4 * n, 1)
    for q in range(1, 4):
        out = out + roll(value, 4 * (q - n), 1)
    return out


EDGES = (
    "field",
    "mix",
    "inv_down",
    "up_down",
    "down_down",
    "inv_up",
    "up_up",
    "down_up",
    "inv_up_1",
    "up_up_1",
    "down_up_1",
    "to_east",
    "to_west",
    "to_inner",
    "cross_east",
    "cross_west",
    "cross_inner",
    "inside",
    "after",
    "after_1",
    "ahead",
    "ahead_1",
    "grad_h",
    "grad_h_1",
    "grad_v_1",
    "column",
    "mix_column",
    "inv_column",
    "up_column",
    "down_column",
)
EDGE_LEVELS = ("own", "own_1", "east", "west", "inner", "column")


def exchange(value):
    return jnp.where(iota(8, 0) % 4 < 2, roll(value, -2, 0), roll(value, 2, 0))


def at_edges(rows, shift):
    sub = iota(8, 0) % 4
    out = roll(rows, LANES - 2 - shift, 1)
    for q in range(1, 4):
        out = jnp.where(sub == q, roll(rows, LANES - 2 - shift - 4 * q, 1), out)
    return jnp.broadcast_to(out, (8, LANES))


def stacked(*rows):
    sub = iota(8, 0)
    out = jnp.zeros((8, LANES), jnp.float32)
    for n, row in enumerate(rows):
        if row is not None:
            out = jnp.where(sub == n, row, out)
    return out


def nears_of(value, halo):
    return east(value, halo), west(value, halo), up(value), down(value)


def at(q):
    return slice(q * ROWS, (q + 1) * ROWS)


def interior_down(
    merged,
    own,
    fields,
    factors,
    mix_h,
    mix_v,
    levels,
    sent,
    inside,
    steps,
    weights,
    columns,
    column_factors,
    up_factors,
    shallow_out,
    packed,
):
    depth = mix_h.shape[0]
    tiles = depth // PER_TILE
    lane = iota(ROWS, 1)
    zero = jnp.zeros((ROWS, LANES), jnp.float32)
    level = levels[...]
    face_below = inverse = zero
    for k in range(depth - 1, -1, -1):
        face_above = bond(mix_v, level, k - 1, depth)
        inverse = pivot(face_below, face_above, inverse)
        up_factors[0, k] = inverse
        up_factors[1, k] = face_below * inverse
        up_factors[2, k] = face_above * inverse
        face_below = face_above

    column = lane % 4
    last_row, first_row = iota(ROWS, 0) == ROWS - 1, iota(ROWS, 0) == 0
    for j in range(tiles):
        level_k = (lane // GROUP + j * PER_TILE).astype(jnp.float32)
        mix, bonds, depths = [coefficient(merged[tiles + j], n) for n in range(3)]
        own_mix, own_depths = [coefficient(own[tiles + j], n) for n in (0, 2)]
        value = merged[j]

        def outer(array):
            return jnp.where(column == 1, roll(array, -2, 1), roll(array, 2, 1))

        def weight(near_depths, near_mix):
            return jnp.where(
                jnp.minimum(depths, near_depths) > level_k, 0.5 * (mix + near_mix), 0.0
            )

        mixed = value + weight(own_depths, own_mix) * (own[j] - value)
        mixed = mixed + weight(outer(depths), outer(mix)) * (outer(value) - value)
        for border, shift in ((last_row, up), (first_row, down)):
            flow = weight(shift(depths), shift(mix)) * (shift(value) - value)
            mixed = mixed + jnp.where(border, 0.0, flow)
        packed[0, j] = mixed
        packed[1, j] = bonds
        if j == 0:
            level_columns = depths

    def unpacked(n, k):
        return roll(packed[n, k // PER_TILE], -GROUP * (k % PER_TILE), 1)

    level = level.astype(jnp.float32)
    shallow = [jnp.minimum(level, near) for near in nears_of(level, rim(merged[tiles], 8))]
    shallow[2] = jnp.where(last_row, 0.0, shallow[2])
    shallow[3] = jnp.where(first_row, 0.0, shallow[3])
    for n in range(4):
        shallow_out[n] = shallow[n]

    bond_above = col_inverse = col_value = zero
    values = [zero] * 4
    for k in range(depth):
        j, i = divmod(k, PER_TILE)
        under = min(k + 1, depth - 1)
        bond_here = jnp.where(
            level_columns > k + 1.0, 0.5 * (unpacked(1, k) + unpacked(1, under)), 0.0
        )
        col_inverse = pivot(bond_above, bond_here, col_inverse)
        col_factor = bond_above * col_inverse
        col_value = unpacked(0, k) * col_inverse + col_factor * col_value
        columns[k] = col_value
        column_factors[0, k] = col_inverse
        column_factors[1, k] = col_factor
        column_factors[2, k] = bond_here * col_inverse
        bond_above = bond_here
        mix = mix_h[k]
        weight = [
            jnp.where(open_to > float(k), 0.5 * (mix + near), 0.0)
            for open_to, near in zip(shallow, nears_of(mix, rim(merged[tiles + j], GROUP * i)))
        ]
        for n in range(4):
            weights[k, n] = weight[n]
        for q in range(4):
            value = fields[tile_of(q, k, depth)]
            step = [near - value for near in nears_of(value, rim(merged[j], GROUP * i + 4 * q))]
            for n in range(4):
                steps[k, q, n] = step[n]
                value = value + weight[n] * step[n]
            values[q] = value * factors[0, k] + factors[1, k] * values[q]
            inside[k, at(q)] = values[q]


def interior_up(
    inside_in,
    steps,
    weights,
    columns,
    column_factors,
    up_factors,
    shallow_in,
    factors,
    inside,
    after,
    adjoint,
    grad_h,
):
    depth = grad_h.shape[0]
    zero = jnp.zeros((ROWS, LANES), jnp.float32)
    shallow = [shallow_in[n] for n in range(4)]
    col_value = zero
    values = [zero] * 4
    later_values = [zero] * 2
    for k in range(depth - 1, -1, -1):
        col_value = columns[k] + column_factors[2, k] * col_value
        later_steps = []
        for q in range(4):
            value = inside_in[k, at(q)] + factors[2, k] * values[q]
            inside[k, at(q)] = value
            values[q] = value
            step = [near - value for near in nears_of(value, rim(col_value, 4 * q))]
            later_steps.append(step)
            for n in range(4):
                value = value + weights[k, n] * step[n]
            if q < 2:
                later_values[q] = value * up_factors[0, k] + up_factors[1, k] * later_values[q]
                value = later_values[q]
            else:
                adjoint[q - 2, k] = value
            after[k, at(q)] = value
        total = zero
        for n in range(4):
            face = zero
            for t in range(2):
                face = face + steps[k, t, n] * later_steps[2 + t][n]
                face = face + later_steps[t][n] * steps[k, 2 + t, n]
            total = total + jnp.where(shallow[n] > float(k), face, 0.0)
        grad_h[k] = -0.5 * total


def interior_edges(
    merged,
    fields,
    factors,
    mix_h,
    levels,
    inside,
    after,
    weights,
    column_factors,
    up_factors,
    shallow,
    grad_h,
    edges,
    edge_levels,
    grad_v,
    later,
):
    depth = mix_h.shape[0]
    tiles = depth // PER_TILE
    zero = jnp.zeros((ROWS, LANES), jnp.float32)
    level = levels[...].astype(jnp.float32)
    face_above = zero
    for t in range(2):
        later[0, at(t)] = after[0, at(t)]
    for k in range(depth):
        if k > 0:
            total = zero
            for t in range(2):
                later_here = after[k, at(t)] + up_factors[2, k] * later[k - 1, at(t)]
                later[k, at(t)] = later_here
                total = total + (inside[k - 1, at(2 + t)] - inside[k, at(2 + t)]) * (
                    inside[k - 1, at(t)] - inside[k, at(t)]
                )
                total = total + (
                    fields[tile_of(2 + t, k - 1, depth)] - fields[tile_of(2 + t, k, depth)]
                ) * (later[k - 1, at(t)] - later_here)
            face = jnp.where(level > float(k), total, 0.0)
            grad_v[k - 1] = -0.5 * (face + face_above)
            face_above = face
    grad_v[depth - 1] = -0.5 * face_above

    def ends(value, inset=0):
        return both(value[inset : inset + 1], value[ROWS - 1 - inset : ROWS - inset])

    def four(ref, start, stride, inset=0):
        low, high = start + inset, start + ROWS - 1 - inset
        return stacked(
            *(ref[row + q * stride : row + q * stride + 1] for row in (low, high) for q in range(4))
        )

    last_lane, first_lane = iota(8, 1) == LANES - 1, iota(8, 1) == 0

    coef_rows = ends(merged[tiles])
    for n, value in enumerate(
        (
            ends(level),
            ends(level, 1),
            ends(shallow[0]),
            ends(shallow[1]),
            both(shallow[2, :1], shallow[3, ROWS - 1 :]),
            rim(coef_rows, 8),
        )
    ):
        edge_levels[n] = value

    for k in range(depth):
        j, i = divmod(k, PER_TILE)
        field = four(fields, k * ROWS, depth * ROWS)
        field_1 = four(fields, k * ROWS, depth * ROWS, 1)
        column = at_edges(ends(merged[j]), GROUP * i)
        things = dict(
            field=field,
            mix=ends(mix_h[k]),
            to_east=ends(weights[k, 0]),
            to_west=ends(weights[k, 1]),
            to_inner=both(weights[k, 2, :1], weights[k, 3, ROWS - 1 :]),
            cross_east=exchange(jnp.where(last_lane, column, roll(field, -1, 1)) - field),
            cross_west=exchange(jnp.where(first_lane, column, roll(field, 1, 1)) - field),
            cross_inner=exchange(field_1 - field),
            inside=four(inside.at[k], 0, ROWS),
            after=stacked(
                *(
                    (later if q < 2 else after)[k, q * ROWS + row : q * ROWS + row + 1]
                    for row in (0, ROWS - 1)
                    for q in range(4)
                )
            ),
            after_1=four(after.at[k], 0, ROWS, 1),
            ahead=roll(field, -2, 0),
            ahead_1=roll(field_1, -2, 0),
            grad_h=ends(grad_h[k]),
            grad_h_1=ends(grad_h[k], 1),
            grad_v_1=ends(grad_v[k], 1),
            column=column,
            mix_column=rim(ends(merged[tiles + j]), GROUP * i),
        )
        for n, name in enumerate(("inv", "up", "down")):
            things[name + "_down"] = ends(factors[n, k])
            things[name + "_up"] = ends(up_factors[n, k])
            things[name + "_up_1"] = ends(up_factors[n, k], 1)
            things[name + "_column"] = rim(ends(column_factors[n, k]), 0)
        for name, value in things.items():
            edges[EDGES.index(name), k] = value


def turned_corner(block, merged, tiles, border):
    code = coefficient(merged[tiles, :8], FILLER)[:1]
    swapped = jnp.where(iota(8, 1) % 4 == 1, roll(block, -2, 1), roll(block, 2, 1))
    return jnp.where((lax.axis_index("tx") == border) & (code > 0.5), swapped, block)


def open_below(seam, corner, merged, edge_levels, opened):
    tiles = merged.shape[0] // 2
    turn = (seam[0] == 1) & (lax.axis_index("tx") == 0)
    block = corner[...]
    flows = jnp.where(turn, crossed(block), block)
    block = turned_corner(block, merged, tiles, 0)
    opened[0] = jnp.where(iota(8, 0) < 2 * tiles, block, flows)
    opened[1] = jnp.minimum(
        rim(block[tiles : tiles + 1], 8), edge_levels[EDGE_LEVELS.index("column")]
    )


def finish(
    seam,
    from_below,
    from_above,
    opened,
    merged,
    edges,
    edge_levels,
    adjoint_in,
    grad_h_in,
    grad_v_in,
    adjoint_out,
    grad_h_out,
    grad_v_out,
    below,
    above,
    rows,
    later,
    adjoint,
    grad_h,
    grad_v,
    sems,
):
    depth, tiles = grad_h.shape[0], grad_h.shape[0] // PER_TILE
    sub = iota(8, 0)
    lane = iota(8, 1)
    place = lax.axis_index("tx")
    last = lax.axis_size("tx") - 1
    base_mix, base_bond, base_level = 8 * depth, 9 * depth, 10 * depth - 1
    size = 10 * depth
    zero = jnp.zeros((8, LANES), jnp.float32)

    def edge(name, k):
        return edges[EDGES.index(name), k]

    def edge_level(name):
        return edge_levels[EDGE_LEVELS.index(name)]

    for source, target, border in ((from_below, below, 0), (from_above, above, last)):
        turn = (seam[0] == 1) & (place == border)

        @pl.when(turn)
        def _():
            back = LANES - 1 - lane
            for r in range(0, size, 8):
                target[r : r + 8] = jnp.take_along_axis(source[r : r + 8], back, axis=1)

        @pl.when(jnp.logical_not(turn))
        def _():
            for r in range(0, size, 8):
                target[r : r + 8] = source[r : r + 8]

    for k in range(depth):
        for t in range(2):
            adjoint[t, k] = adjoint_in[t, k]
        grad_h[k] = grad_h_in[k]
        grad_v[k] = grad_v_in[k]

    last_block = from_above[size:]
    corner_above = turned_corner(last_block, merged, tiles, last)
    turn_above = (seam[0] == 1) & (place == last)
    flows_above = jnp.where(turn_above, crossed(last_block), last_block)

    def corner(r):
        return both(opened[0, r : r + 1], corner_above[r : r + 1])

    def flow_of(j):
        r = 2 * tiles + j
        return both(opened[0, r : r + 1], flows_above[r : r + 1])

    beside = (lane == 0) | (lane == LANES - 1)

    def outer(start, k=0):
        at = slice(start + k, start + k + 1)
        return both(below[at], above[at])

    level_out = outer(base_level)
    level_face = jnp.minimum(level_out, edge_level("own"))
    level_corner = both(
        opened[1],
        jnp.minimum(rim(corner_above[tiles : tiles + 1], 8), edge_level("column")),
    )

    bond_above = inverse = out_value = added = column_added = zero
    flows = []
    for k in range(depth):
        j, i = divmod(k, PER_TILE)
        block = slice(8 * k, 8 * k + 8)
        below_block, above_block = below[block], above[block]
        bond_here = zero
        if k < depth - 1:
            bond_here = jnp.where(level_out > k + 1.0, outer(base_bond, k), 0.0)
        inverse = pivot(bond_above, bond_here, inverse)
        out = both(below_block, roll(above_block, 4, 0))
        part = both(roll(below_block, 4, 0), above_block) + jnp.where(
            beside, at_edges(flow_of(j), GROUP * i), 0.0
        )
        step = out - edge("field", k)
        weight = jnp.where(level_face > float(k), 0.5 * (outer(base_mix, k) + edge("mix", k)), 0.0)
        flow = weight * step
        out_value = (part - flow) * inverse + bond_above * inverse * out_value
        added = flow * edge("inv_down", k) + edge("up_down", k) * added
        mix_corner = rim(corner(tiles + j), GROUP * i)
        weight_corner = jnp.where(
            level_corner > float(k), 0.5 * (mix_corner + edge("mix_column", k)), 0.0
        )
        step_corner = at_edges(corner(j), GROUP * i) - edge("column", k)
        column_added = (
            weight_corner * step_corner * edge("inv_column", k)
            + edge("up_column", k) * column_added
        )
        rows[0, k] = out_value
        rows[1, k] = bond_here * inverse
        rows[2, k] = added
        rows[3, k] = column_added
        rows[4, k] = weight
        rows[5, k] = exchange(step)
        bond_above = bond_here

    out_value = added = column_added = later_0 = later_1 = zero
    for k in range(depth - 1, -1, -1):
        out_value = rows[0, k] + rows[1, k] * out_value
        added = rows[2, k] + edge("down_down", k) * added
        column_added = rows[3, k] + edge("down_column", k) * column_added
        value = edge("inside", k) + added
        rows[0, k] = value
        east_step = jnp.where(lane == LANES - 1, column_added, roll(added, -1, 1)) - added
        west_step = jnp.where(lane == 0, column_added, roll(added, 1, 1)) - added
        out_step = out_value - value
        inner_flow = edge("to_inner", k) * added
        change = (
            added
            + edge("to_east", k) * east_step
            + edge("to_west", k) * west_step
            - inner_flow
            + rows[4, k] * out_step
        )
        later_0 = change * edge("inv_up", k) + edge("up_up", k) * later_0
        later_1 = inner_flow * edge("inv_up_1", k) + edge("up_up_1", k) * later_1
        later[0, k] = later_0
        later[1, k] = later_1
        result = edge("after", k) + change
        result_1 = edge("after_1", k) + inner_flow
        for t in range(2):
            for at, source, row in (
                (0, result, 2),
                (ROWS - 1, result, 6),
                (1, result_1, 2),
                (ROWS - 2, result_1, 6),
            ):
                adjoint[t, k, at : at + 1] = source[row + t : row + t + 1]
        product_1 = jnp.where(
            edge_level("inner") > float(k), -edge("cross_inner", k) * added, 0.0
        )
        product = (
            product_1
            + jnp.where(edge_level("east") > float(k), edge("cross_east", k) * east_step, 0.0)
            + jnp.where(edge_level("west") > float(k), edge("cross_west", k) * west_step, 0.0)
            + jnp.where(level_face > float(k), rows[5, k] * out_step, 0.0)
        )
        for name, inset, value in (("grad_h", 0, product), ("grad_h_1", 1, product_1)):
            value = value + roll(value, -1, 0)
            value = edge(name, k) - 0.5 * (value + roll(value, -2, 0))
            grad_h[k, inset : inset + 1] = value[:1]
            grad_h[k, ROWS - 1 - inset : ROWS - inset] = value[4:5]

    copies = [
        pltpu.make_async_copy(source, target, sems.at[n])
        for n, (source, target) in enumerate(
            ((adjoint, adjoint_out), (grad_h, grad_h_out), (grad_v, grad_v_out))
        )
    ]
    copies[0].start()
    copies[1].start()

    face_0 = face_1 = later_0 = later_1 = zero
    for k in range(depth + 1):
        if k < depth:
            above_0, above_1 = later_0, later_1
            later_0 = later[0, k] + edge("down_up", k) * later_0
            later_1 = later[1, k] + edge("down_up_1", k) * later_1
        if k == 0:
            continue
        next_0 = next_1 = zero
        if k < depth:
            step = rows[0, k - 1] - rows[0, k]
            next_0 = step * roll(step, -2, 0) + (edge("ahead", k - 1) - edge("ahead", k)) * (
                edge("after", k - 1) + above_0 - edge("after", k) - later_0
            )
            next_1 = (edge("ahead_1", k - 1) - edge("ahead_1", k)) * (above_1 - later_1)
            next_0 = jnp.where(
                edge_level("own") > float(k), next_0 + roll(next_0, -1, 0), 0.0
            )
            next_1 = jnp.where(
                edge_level("own_1") > float(k), next_1 + roll(next_1, -1, 0), 0.0
            )
        value_0 = -0.5 * (face_0 + next_0)
        value_1 = edge("grad_v_1", k - 1) - 0.5 * (face_1 + next_1)
        for inset, value in ((0, value_0), (1, value_1)):
            grad_v[k - 1, inset : inset + 1] = value[:1]
            grad_v[k - 1, ROWS - 1 - inset : ROWS - inset] = value[4:5]
        face_0, face_1 = next_0, next_1
    copies[2].start()
    for copy in copies:
        copy.wait()


def per_device(tracers, costate, mixing_h, mixing_v, levels, seam_code):
    depth = tracers.shape[1]
    tiles = depth // PER_TILE
    height = 10 * depth
    params = pltpu.CompilerParams(vmem_limit_bytes=48 * 2**20)
    smem = pl.BlockSpec(memory_space=pltpu.SMEM)
    vmem = pl.BlockSpec(memory_space=pltpu.VMEM)
    hbm = pl.BlockSpec(memory_space=pltpu.HBM)
    tile = (ROWS, LANES)

    def flat(array):
        return array.reshape(-1, LANES)

    fields, factors, own, mix_h, mix_v, levels_here = pl.pallas_call(
        prepare,
        out_shape=(
            vmem_out(4 * depth * ROWS, LANES),
            vmem_out(3, depth, *tile),
            vmem_out(2 * tiles, *tile),
            vmem_out(depth, *tile),
            vmem_out(depth, *tile),
            pltpu.VMEM(tile, jnp.int32),
        ),
        in_specs=[smem] + [hbm] * 5,
        scratch_shapes=[pltpu.SemaphoreType.DMA((5,))],
        compiler_params=params,
        name="prepare",
    )(seam_code, *(in_hbm(a) for a in (flat(tracers), flat(costate), mixing_h, mixing_v, levels)))

    count = lax.axis_size("ty")
    near_pairs = [(i, i ^ 1) for i in range(count)]
    far_pairs = [(i, (i + 1 if i % 2 else i - 1) % count) for i in range(count)]
    far = lax.ppermute(own, "ty", far_pairs)
    near = lax.ppermute(own, "ty", near_pairs)

    def cost(work):
        return pl.CostEstimate(flops=work, bytes_accessed=work, transcendentals=0)

    def call(body, outs, *operands, **options):
        return pl.pallas_call(
            body, out_shape=outs, compiler_params=params, name=body.__name__, **options
        )(*(in_vmem(a) for a in operands))

    count = lax.axis_size("tx")
    upward = [(i, (i + 1) % count) for i in range(count)]
    downward = [(i, (i - 1) % count) for i in range(count)]
    early, upper = call(
        pack_rows,
        (vmem_out(height, LANES), vmem_out(height, LANES)),
        *(fields, mix_h, mix_v, levels_here),
    )
    from_below = lax.ppermute(upper, "tx", upward)
    merged, corner, lower = call(
        pack_sides,
        (vmem_out(2 * tiles, *tile), vmem_out(8, LANES), vmem_out(height + 8, LANES)),
        *(near, far, own, early),
    )
    corner_below = lax.ppermute(corner, "tx", upward)
    from_above = lax.ppermute(lower, "tx", downward)
    row_block = (depth, 8, LANES)
    inside, steps, weights, columns, column_factors, up_factors, shallow = call(
        interior_down,
        (
            vmem_out(depth, 4 * ROWS, LANES),
            vmem_out(depth, 4, 4, *tile),
            vmem_out(depth, 4, *tile),
            vmem_out(depth, *tile),
            vmem_out(3, depth, *tile),
            vmem_out(3, depth, *tile),
            vmem_out(4, *tile),
        ),
        *(merged, own, fields, factors, mix_h, mix_v, levels_here, lower),
        scratch_shapes=[vmem_out(2, tiles, *tile)],
        cost_estimate=cost(30_000_000),
    )
    inside, after, adjoint, grad_h = call(
        interior_up,
        (
            vmem_out(depth, 4 * ROWS, LANES),
            vmem_out(depth, 4 * ROWS, LANES),
            vmem_out(2, depth, *tile),
            vmem_out(depth, *tile),
        ),
        *(inside, steps, weights, columns, column_factors, up_factors, shallow, factors),
        cost_estimate=cost(30_000_000),
    )
    edges, edge_levels, grad_v = call(
        interior_edges,
        (
            vmem_out(len(EDGES), *row_block),
            vmem_out(len(EDGE_LEVELS), 8, LANES),
            vmem_out(depth, *tile),
        ),
        *(merged, fields, factors, mix_h, levels_here, inside, after),
        *(weights, column_factors, up_factors, shallow, grad_h),
        scratch_shapes=[vmem_out(depth, 2 * ROWS, LANES)],
        cost_estimate=cost(40_000_000),
    )
    inner = (edges, edge_levels, adjoint, grad_h, grad_v)
    opened = pl.pallas_call(
        open_below,
        out_shape=vmem_out(2, 8, LANES),
        in_specs=[smem] + [vmem] * 3,
        compiler_params=params,
        cost_estimate=cost(900_000_000),
        name="open_below",
    )(seam_code, *(in_vmem(a) for a in (corner_below, merged, inner[1])))
    block = jax.ShapeDtypeStruct(mixing_h.shape, jnp.float32)
    return pl.pallas_call(
        finish,
        out_shape=(jax.ShapeDtypeStruct(tracers.shape, jnp.float32), block, block),
        in_specs=[smem] + [vmem] * 9,
        out_specs=(hbm, hbm, hbm),
        scratch_shapes=[
            vmem_out(height, LANES),
            vmem_out(height, LANES),
            vmem_out(6, *row_block),
            vmem_out(2, *row_block),
            vmem_out(2, depth, *tile),
            vmem_out(depth, *tile),
            vmem_out(depth, *tile),
            pltpu.SemaphoreType.DMA((3,)),
        ],
        compiler_params=params,
        name="finish",
    )(seam_code, *(in_vmem(a) for a in (from_below, from_above, opened, merged, *inner)))


def solution(mesh):
    placed = (
        P("members", None, "tx", "ty"),
        P("members", None, "tx", "ty"),
        P("members", "tx", "ty"),
        P("members", "tx", "ty"),
        P("tx", "ty"),
        P("ty"),
    )
    return jax.shard_map(
        per_device,
        mesh=mesh,
        in_specs=placed,
        out_specs=(
            P("members", None, "tx", "ty"),
            P("members", "tx", "ty"),
            P("members", "tx", "ty"),
        ),
        check_vma=False,
    )
```

```python
import jax
import jax.numpy as jnp
from jax import lax
from jax.experimental import pallas as pl
from jax.experimental.pallas import tpu as pltpu
from jax.sharding import PartitionSpec as P

LANES = 128
ROWS = 16
GROUP = 16
PER_TILE = LANES // GROUP


FILLER = 3


def in_vmem(array):
    return pltpu.with_memory_space_constraint(array, pltpu.VMEM)


def in_hbm(array):
    return pltpu.with_memory_space_constraint(array, pltpu.HBM)


def vmem_out(*shape):
    return pltpu.VMEM(shape, jnp.float32)


def iota(rows, dim):
    return lax.broadcasted_iota(jnp.int32, (rows, LANES), dim)


def roll(value, shift, axis):
    return pltpu.roll(value, shift % value.shape[axis], axis)


def fold(value):
    return jnp.where(iota(8, 0) < 4, value[:8], value[8:])


def east(value, halo):
    return jnp.where(iota(value.shape[0], 1) == LANES - 1, halo, roll(value, -1, 1))


def west(value, halo):
    return jnp.where(iota(value.shape[0], 1) == 0, halo, roll(value, 1, 1))


def rim(tile, base):
    return roll(tile, LANES - 2 - base, 1)


def crossed(tile):
    column = iota(tile.shape[0], 1) % 4
    return jnp.where(
        column == 1, roll(tile, -1, 1), jnp.where(column == 2, roll(tile, 1, 1), tile)
    )


def lane_of(i, q):
    return GROUP * i + 4 * (3 - q)


def tile_of(q, k, depth):
    return slice((q * depth + k) * ROWS, (q * depth + k + 1) * ROWS)


def up(value):
    low, high = roll(value[:8], -1, 0), roll(value[8:], -1, 0)
    return jnp.concatenate([jnp.where(iota(8, 0) == 7, high, low), high], axis=0)


def down(value):
    low, high = roll(value[:8], 1, 0), roll(value[8:], 1, 0)
    return jnp.concatenate([low, jnp.where(iota(8, 0) == 0, low, high)], axis=0)


def bond(mix_v, level, k, depth):
    if k in (-1, depth - 1):
        return jnp.zeros(level.shape, jnp.float32)
    return jnp.where(level > k + 1, 0.5 * (mix_v[k] + mix_v[k + 1]), 0.0)


def factorize(depth, level, mix_v, put):
    bond_above = jnp.zeros(level.shape, jnp.float32)
    inverse = bond_above
    for k in range(depth):
        bond_here = bond(mix_v, level, k, depth)
        inverse = pivot(bond_above, bond_here, inverse)
        put(k, inverse, bond_above * inverse, bond_here * inverse)
        bond_above = bond_here


def pivot(bond_above, bond_here, inverse):
    return 1.0 / (1.0 + bond_above + bond_here - bond_above * bond_above * inverse)


def prepare(
    seam,
    tracers,
    costate,
    mix_h_in,
    mix_v_in,
    levels_in,
    fields,
    factors,
    message,
    mix_h,
    mix_v,
    levels,
    sems,
):
    depth = mix_h.shape[0]
    tiles = depth // PER_TILE
    copies = []
    for n, (source, target, parts) in enumerate(
        (
            (levels_in, levels, 1),
            (mix_v_in, mix_v, 4),
            (tracers, fields.at[: 2 * depth * ROWS], 4),
            (mix_h_in, mix_h, 4),
            (costate, fields.at[2 * depth * ROWS :], 4),
        )
    ):
        size = source.shape[0] // parts
        for m in range(parts):
            cut = slice(m * size, (m + 1) * size)
            pltpu.make_async_copy(source.at[cut], target.at[cut], sems.at[n]).start()
        copies.append(pltpu.make_async_copy(source, target, sems.at[n]))
    for copy in copies[:2]:
        copy.wait()
    level = levels[...]
    place = iota(ROWS, 1) // 4
    zero = jnp.zeros((ROWS, LANES), jnp.float32)

    def put(k, *three):
        for n in range(3):
            factors[n, k] = three[n]

    factorize(depth, level, mix_v, put)
    seconds = [jnp.where(place % 4 == FILLER, seam[0].astype(jnp.float32), zero)] * tiles
    level_f = level.astype(jnp.float32)
    for k in range(depth):
        tile, base = k // PER_TILE, GROUP * (k % PER_TILE)
        for n, value in ((1, mix_v[k]), (2, level_f)):
            seconds[tile] = jnp.where(
                place == base // 4 + n, roll(value, base + 4 * n + 2, 1), seconds[tile]
            )
    firsts = [zero] * tiles

    def add(k, q, value):
        tile, base = k // PER_TILE, lane_of(k % PER_TILE, q)
        firsts[tile] = jnp.where(place == base // 4, roll(value, base + 2, 1), firsts[tile])

    for copy in copies[2:4]:
        copy.wait()
    for k in range(depth):
        tile, base = k // PER_TILE, GROUP * (k % PER_TILE)
        for t in range(2):
            add(k, t, fields[tile_of(t, k, depth)])
        seconds[tile] = jnp.where(
            place == base // 4, roll(mix_h[k], base + 2, 1), seconds[tile]
        )
    copies[4].wait()
    values = [zero, zero]
    for k in range(depth):
        for t in range(2):
            values[t] = fields[tile_of(2 + t, k, depth)] * factors[0, k] + factors[1, k] * values[t]
            fields[tile_of(2 + t, k, depth)] = values[t]
    values = [zero, zero]
    for k in range(depth - 1, -1, -1):
        for t in range(2):
            values[t] = fields[tile_of(2 + t, k, depth)] + factors[2, k] * values[t]
            fields[tile_of(2 + t, k, depth)] = values[t]
            add(k, 2 + t, values[t])
    for tile in range(tiles):
        message[tile] = firsts[tile]
        message[tiles + tile] = seconds[tile]


def pack_rows(fields, mix_h, mix_v, levels, lower, upper):
    depth = mix_h.shape[0]
    sub = iota(8, 0)

    def nears(value):
        inner = jnp.where(sub < 4, roll(value, -1, 0), roll(value, 1, 0))
        return east(value, 0.0), west(value, 0.0), inner

    level = fold(levels[...].astype(jnp.float32))
    shallow = [jnp.minimum(level, near) for near in nears(level)]
    for k in range(depth):
        mix = fold(mix_h[k])
        weights = [
            jnp.where(open_to > float(k), 0.5 * (mix + near), 0.0)
            for open_to, near in zip(shallow, nears(mix))
        ]
        low = jnp.zeros((8, LANES), jnp.float32)
        high = low
        for q in range(4):
            value = fold(fields[tile_of(q, k, depth)])
            part = value
            for near, weight in zip(nears(value), weights):
                part = part + weight * (near - value)
            for n, thing in ((q, value), (4 + q, part)):
                low = jnp.where(sub == n, roll(thing, n, 0), low)
                high = jnp.where(sub == n, roll(thing, n - 7, 0), high)
        lower[8 * k : 8 * k + 8] = low
        upper[8 * k : 8 * k + 8] = high
        at_mix = slice(8 * depth + k, 8 * depth + k + 1)
        lower[at_mix] = mix_h[k, :1]
        upper[at_mix] = mix_h[k, ROWS - 1 :]
        if k < depth - 1:
            between = 0.5 * (mix_v[k] + mix_v[k + 1])
            at_bond = slice(9 * depth + k, 9 * depth + k + 1)
            lower[at_bond] = between[:1]
            upper[at_bond] = between[ROWS - 1 :]
    lower[10 * depth - 1 :] = level[:1]
    upper[10 * depth - 1 :] = level[7:]


def pack_sides(near, far, own, early, merged, corner, lower):
    tiles = near.shape[0] // 2
    place = lax.axis_index("ty")
    last = lax.axis_size("ty") - 1
    even = place % 2 == 0
    column = iota(ROWS, 1) % 4
    corners = []
    edge = iota(8, 1) % 4
    for j in range(2 * tiles):
        west_tile = jnp.where(even, far[j], near[j])
        east_tile = jnp.where(even, near[j], far[j])
        if j >= tiles:
            west_tile = jnp.where(place == 0, 0.0, west_tile)
            east_tile = jnp.where(place == last, 0.0, east_tile)
        middle = jnp.where(column == 1, roll(east_tile, -1, 1), roll(west_tile, 1, 1))
        merged[j] = jnp.where(
            column == 0, west_tile, jnp.where(column == 3, east_tile, middle)
        )
        west_rows, east_rows = fold(west_tile), fold(east_tile)
        middle = jnp.where(edge == 1, roll(east_rows, -1, 1), roll(west_rows, 1, 1))
        corners.append(
            jnp.where(
                edge == 0,
                roll(west_rows, -2, 1),
                jnp.where(edge == 3, roll(east_rows, 2, 1), middle),
            )
        )
    lane = iota(1, 1)

    def for_row(row, sub):
        flows = []
        for j in range(tiles):
            level_k = (lane // GROUP + j * PER_TILE).astype(jnp.float32)
            mix, level = [
                [coefficient(ref[tiles + j, row : row + 1], n) for ref in (merged, own)]
                for n in (0, 2)
            ]
            weight = jnp.where(jnp.minimum(*level) > level_k, 0.5 * (mix[0] + mix[1]), 0.0)
            flows.append(weight * (merged[j, row : row + 1] - own[j, row : row + 1]))
        return [value[sub : sub + 1] for value in corners] + flows

    corner[...] = stacked(*for_row(ROWS - 1, 7))
    size = early.shape[0]
    for r in range(0, size, 8):
        lower[r : r + 8] = early[r : r + 8]
    lower[size:] = stacked(*for_row(0, 0))


def both(low, high):
    return jnp.where(iota(8, 0) < 4, low, high)


def coefficient(value, n):
    kept = iota(value.shape[0], 1) % GROUP // 4 == n
    value = jnp.where(kept, value, 0.0)
    out = roll(value, -4 * n, 1)
    for q in range(1, 4):
        out = out + roll(value, 4 * (q - n), 1)
    return out


EDGES = (
    "field",
    "mix",
    "inv_down",
    "up_down",
    "down_down",
    "inv_up",
    "up_up",
    "down_up",
    "inv_up_1",
    "up_up_1",
    "down_up_1",
    "to_east",
    "to_west",
    "to_inner",
    "cross_east",
    "cross_west",
    "cross_inner",
    "inside",
    "after",
    "after_1",
    "ahead",
    "ahead_1",
    "grad_h",
    "grad_h_1",
    "grad_v_1",
    "column",
    "mix_column",
    "inv_column",
    "up_column",
    "down_column",
)
EDGE_LEVELS = ("own", "own_1", "east", "west", "inner", "column")


def exchange(value):
    return jnp.where(iota(8, 0) % 4 < 2, roll(value, -2, 0), roll(value, 2, 0))


def at_edges(low, high, i):
    rows = both(low, roll(high, -GROUP, 1))
    shift = LANES - 2 - lane_of(i, 0)
    if i == 0:
        rows, shift = roll(rows, LANES // 2, 1), shift - LANES // 2
    return pltpu.roll(rows, shift % LANES, 1, stride=4, stride_axis=0)


def stacked(*rows):
    sub = iota(8, 0)
    out = jnp.zeros((8, LANES), jnp.float32)
    for n, row in enumerate(rows):
        if row is not None:
            out = jnp.where(sub == n, row, out)
    return out


def nears_of(value, halo):
    return east(value, halo), west(value, halo), up(value), down(value)


def at(q):
    return slice(q * ROWS, (q + 1) * ROWS)


def interior_down(
    merged,
    own,
    fields,
    factors,
    mix_h,
    mix_v,
    levels,
    sent,
    inside,
    steps,
    weights,
    columns,
    column_factors,
    up_factors,
    shallow_out,
    packed,
):
    depth = mix_h.shape[0]
    tiles = depth // PER_TILE
    lane = iota(ROWS, 1)
    zero = jnp.zeros((ROWS, LANES), jnp.float32)
    level = levels[...]
    face_below = inverse = zero
    for k in range(depth - 1, -1, -1):
        face_above = bond(mix_v, level, k - 1, depth)
        inverse = pivot(face_below, face_above, inverse)
        up_factors[0, k] = inverse
        up_factors[1, k] = face_below * inverse
        up_factors[2, k] = face_above * inverse
        face_below = face_above

    column = lane % 4
    last_row, first_row = iota(ROWS, 0) == ROWS - 1, iota(ROWS, 0) == 0
    for j in range(tiles):
        level_k = (lane // GROUP + j * PER_TILE).astype(jnp.float32)
        mix, bonds, depths = [coefficient(merged[tiles + j], n) for n in range(3)]
        own_mix, own_depths = [coefficient(own[tiles + j], n) for n in (0, 2)]
        value = merged[j]

        def outer(array):
            return jnp.where(column == 1, roll(array, -2, 1), roll(array, 2, 1))

        def weight(near_depths, near_mix):
            return jnp.where(
                jnp.minimum(depths, near_depths) > level_k, 0.5 * (mix + near_mix), 0.0
            )

        mixed = value + weight(own_depths, own_mix) * (own[j] - value)
        mixed = mixed + weight(outer(depths), outer(mix)) * (outer(value) - value)
        for border, shift in ((last_row, up), (first_row, down)):
            flow = weight(shift(depths), shift(mix)) * (shift(value) - value)
            mixed = mixed + jnp.where(border, 0.0, flow)
        packed[0, j] = mixed
        packed[1, j] = bonds
        if j == 0:
            level_columns = depths

    def unpacked(n, k):
        return roll(packed[n, k // PER_TILE], -GROUP * (k % PER_TILE), 1)

    level = level.astype(jnp.float32)
    shallow = [jnp.minimum(level, near) for near in nears_of(level, rim(merged[tiles], 8))]
    shallow[2] = jnp.where(last_row, 0.0, shallow[2])
    shallow[3] = jnp.where(first_row, 0.0, shallow[3])
    for n in range(4):
        shallow_out[n] = shallow[n]

    bond_above = col_inverse = col_value = zero
    values = [zero] * 4
    for k in range(depth):
        j, i = divmod(k, PER_TILE)
        under = min(k + 1, depth - 1)
        bond_here = jnp.where(
            level_columns > k + 1.0, 0.5 * (unpacked(1, k) + unpacked(1, under)), 0.0
        )
        col_inverse = pivot(bond_above, bond_here, col_inverse)
        col_factor = bond_above * col_inverse
        col_value = unpacked(0, k) * col_inverse + col_factor * col_value
        columns[k] = col_value
        column_factors[0, k] = col_inverse
        column_factors[1, k] = col_factor
        column_factors[2, k] = bond_here * col_inverse
        bond_above = bond_here
        mix = mix_h[k]
        weight = [
            jnp.where(open_to > float(k), 0.5 * (mix + near), 0.0)
            for open_to, near in zip(shallow, nears_of(mix, rim(merged[tiles + j], GROUP * i)))
        ]
        for n in range(4):
            weights[k, n] = weight[n]
        for q in range(4):
            value = fields[tile_of(q, k, depth)]
            step = [near - value for near in nears_of(value, rim(merged[j], lane_of(i, q)))]
            for n in range(4):
                steps[k, q, n] = step[n]
                value = value + weight[n] * step[n]
            values[q] = value * factors[0, k] + factors[1, k] * values[q]
            inside[k, at(q)] = values[q]


def interior_up(
    inside_in,
    steps,
    weights,
    columns,
    column_factors,
    up_factors,
    shallow_in,
    factors,
    inside,
    after,
    adjoint,
    grad_h,
):
    depth = grad_h.shape[0]
    zero = jnp.zeros((ROWS, LANES), jnp.float32)
    shallow = [shallow_in[n] for n in range(4)]
    col_value = zero
    values = [zero] * 4
    later_values = [zero] * 2
    for k in range(depth - 1, -1, -1):
        col_value = columns[k] + column_factors[2, k] * col_value
        later_steps = []
        for q in range(4):
            value = inside_in[k, at(q)] + factors[2, k] * values[q]
            inside[k, at(q)] = value
            values[q] = value
            step = [near - value for near in nears_of(value, rim(col_value, lane_of(0, q)))]
            later_steps.append(step)
            for n in range(4):
                value = value + weights[k, n] * step[n]
            if q < 2:
                later_values[q] = value * up_factors[0, k] + up_factors[1, k] * later_values[q]
                value = later_values[q]
            else:
                adjoint[q - 2, k] = value
            after[k, at(q)] = value
        total = zero
        for n in range(4):
            face = zero
            for t in range(2):
                face = face + steps[k, t, n] * later_steps[2 + t][n]
                face = face + later_steps[t][n] * steps[k, 2 + t, n]
            total = total + jnp.where(shallow[n] > float(k), face, 0.0)
        grad_h[k] = -0.5 * total


def interior_edges(
    merged,
    fields,
    factors,
    mix_h,
    levels,
    inside,
    after,
    weights,
    column_factors,
    up_factors,
    shallow,
    grad_h,
    edges,
    edge_levels,
    grad_v,
    later,
):
    depth = mix_h.shape[0]
    tiles = depth // PER_TILE
    zero = jnp.zeros((ROWS, LANES), jnp.float32)
    level = levels[...].astype(jnp.float32)
    face_above = zero
    for t in range(2):
        later[0, at(t)] = after[0, at(t)]
    for k in range(depth):
        if k > 0:
            total = zero
            for t in range(2):
                later_here = after[k, at(t)] + up_factors[2, k] * later[k - 1, at(t)]
                later[k, at(t)] = later_here
                total = total + (inside[k - 1, at(2 + t)] - inside[k, at(2 + t)]) * (
                    inside[k - 1, at(t)] - inside[k, at(t)]
                )
                total = total + (
                    fields[tile_of(2 + t, k - 1, depth)] - fields[tile_of(2 + t, k, depth)]
                ) * (later[k - 1, at(t)] - later_here)
            face = jnp.where(level > float(k), total, 0.0)
            grad_v[k - 1] = -0.5 * (face + face_above)
            face_above = face
    grad_v[depth - 1] = -0.5 * face_above

    def ends(value, inset=0):
        return both(value[inset : inset + 1], value[ROWS - 1 - inset : ROWS - inset])

    def four(ref, start, stride, inset=0):
        low, high = start + inset, start + ROWS - 1 - inset
        return stacked(
            *(ref[row + q * stride : row + q * stride + 1] for row in (low, high) for q in range(4))
        )

    last_lane, first_lane = iota(8, 1) == LANES - 1, iota(8, 1) == 0

    coef_rows = ends(merged[tiles])
    for n, value in enumerate(
        (
            ends(level),
            ends(level, 1),
            ends(shallow[0]),
            ends(shallow[1]),
            both(shallow[2, :1], shallow[3, ROWS - 1 :]),
            rim(coef_rows, 8),
        )
    ):
        edge_levels[n] = value

    for k in range(depth):
        j, i = divmod(k, PER_TILE)
        field = four(fields, k * ROWS, depth * ROWS)
        field_1 = four(fields, k * ROWS, depth * ROWS, 1)
        column = at_edges(merged[j, :1], merged[j, ROWS - 1 :], i)
        things = dict(
            field=field,
            mix=ends(mix_h[k]),
            to_east=ends(weights[k, 0]),
            to_west=ends(weights[k, 1]),
            to_inner=both(weights[k, 2, :1], weights[k, 3, ROWS - 1 :]),
            cross_east=exchange(jnp.where(last_lane, column, roll(field, -1, 1)) - field),
            cross_west=exchange(jnp.where(first_lane, column, roll(field, 1, 1)) - field),
            cross_inner=exchange(field_1 - field),
            inside=four(inside.at[k], 0, ROWS),
            after=stacked(
                *(
                    (later if q < 2 else after)[k, q * ROWS + row : q * ROWS + row + 1]
                    for row in (0, ROWS - 1)
                    for q in range(4)
                )
            ),
            after_1=four(after.at[k], 0, ROWS, 1),
            ahead=roll(field, -2, 0),
            ahead_1=roll(field_1, -2, 0),
            grad_h=ends(grad_h[k]),
            grad_h_1=ends(grad_h[k], 1),
            grad_v_1=ends(grad_v[k], 1),
            column=column,
            mix_column=rim(ends(merged[tiles + j]), GROUP * i),
        )
        for n, name in enumerate(("inv", "up", "down")):
            things[name + "_down"] = ends(factors[n, k])
            things[name + "_up"] = ends(up_factors[n, k])
            things[name + "_up_1"] = ends(up_factors[n, k], 1)
            things[name + "_column"] = rim(ends(column_factors[n, k]), 0)
        for name, value in things.items():
            edges[EDGES.index(name), k] = value


def turned_corner(block, merged, tiles, border):
    code = coefficient(merged[tiles, :8], FILLER)[:1]
    swapped = jnp.where(iota(8, 1) % 4 == 1, roll(block, -2, 1), roll(block, 2, 1))
    return jnp.where((lax.axis_index("tx") == border) & (code > 0.5), swapped, block)


def open_below(seam, corner, merged, edge_levels, opened):
    tiles = merged.shape[0] // 2
    turn = (seam[0] == 1) & (lax.axis_index("tx") == 0)
    block = corner[...]
    flows = jnp.where(turn, crossed(block), block)
    block = turned_corner(block, merged, tiles, 0)
    opened[0] = jnp.where(iota(8, 0) < 2 * tiles, block, flows)
    opened[1] = jnp.minimum(
        rim(block[tiles : tiles + 1], 8), edge_levels[EDGE_LEVELS.index("column")]
    )


def turn_rows(seam, border, source, target):
    turn = (seam[0] == 1) & (lax.axis_index("tx") == border)
    size = target.shape[0]

    @pl.when(turn)
    def _():
        back = LANES - 1 - iota(8, 1)
        for r in range(0, size, 8):
            target[r : r + 8] = jnp.take_along_axis(source[r : r + 8], back, axis=1)

    @pl.when(jnp.logical_not(turn))
    def _():
        for r in range(0, size, 8):
            target[r : r + 8] = source[r : r + 8]


def turn_below(seam, from_below, below):
    turn_rows(seam, 0, from_below, below)


def finish(
    seam,
    below,
    from_above,
    opened,
    merged,
    edges,
    edge_levels,
    adjoint_in,
    grad_h_in,
    grad_v_in,
    adjoint_out,
    grad_h_out,
    grad_v_out,
    adjoint,
    grad_h,
    grad_v,
    above,
    rows,
    later,
    sems,
):
    depth, tiles = grad_h.shape[0], grad_h.shape[0] // PER_TILE
    sub = iota(8, 0)
    lane = iota(8, 1)
    place = lax.axis_index("tx")
    last = lax.axis_size("tx") - 1
    base_mix, base_bond, base_level = 8 * depth, 9 * depth, 10 * depth - 1
    size = 10 * depth
    zero = jnp.zeros((8, LANES), jnp.float32)

    def edge(name, k):
        return edges[EDGES.index(name), k]

    def edge_level(name):
        return edge_levels[EDGE_LEVELS.index(name)]

    turn_rows(seam, last, from_above, above)

    last_block = from_above[size:]
    corner_above = turned_corner(last_block, merged, tiles, last)
    turn_above = (seam[0] == 1) & (place == last)
    flows_above = jnp.where(turn_above, crossed(last_block), last_block)

    def corner(r):
        return opened[0, r : r + 1], corner_above[r : r + 1]

    def flow_of(j):
        r = 2 * tiles + j
        return opened[0, r : r + 1], flows_above[r : r + 1]

    beside = (lane == 0) | (lane == LANES - 1)

    def outer(start, k=0):
        at = slice(start + k, start + k + 1)
        return both(below[at], above[at])

    level_out = outer(base_level)
    level_face = jnp.minimum(level_out, edge_level("own"))
    level_corner = both(
        opened[1],
        jnp.minimum(rim(corner_above[tiles : tiles + 1], 8), edge_level("column")),
    )

    bond_above = inverse = out_value = added = column_added = zero
    flows = []
    for k in range(depth):
        j, i = divmod(k, PER_TILE)
        block = slice(8 * k, 8 * k + 8)
        below_block, above_block = below[block], above[block]
        bond_here = zero
        if k < depth - 1:
            bond_here = jnp.where(level_out > k + 1.0, outer(base_bond, k), 0.0)
        inverse = pivot(bond_above, bond_here, inverse)
        out = both(below_block, roll(above_block, 4, 0))
        part = both(roll(below_block, 4, 0), above_block) + jnp.where(
            beside, at_edges(*flow_of(j), i), 0.0
        )
        step = out - edge("field", k)
        weight = jnp.where(level_face > float(k), 0.5 * (outer(base_mix, k) + edge("mix", k)), 0.0)
        flow = weight * step
        out_value = (part - flow) * inverse + bond_above * inverse * out_value
        added = flow * edge("inv_down", k) + edge("up_down", k) * added
        mix_corner = rim(both(*corner(tiles + j)), GROUP * i)
        weight_corner = jnp.where(
            level_corner > float(k), 0.5 * (mix_corner + edge("mix_column", k)), 0.0
        )
        step_corner = at_edges(*corner(j), i) - edge("column", k)
        column_added = (
            weight_corner * step_corner * edge("inv_column", k)
            + edge("up_column", k) * column_added
        )
        rows[0, k] = out_value
        rows[1, k] = bond_here * inverse
        rows[2, k] = added
        rows[3, k] = column_added
        rows[4, k] = weight
        rows[5, k] = exchange(step)
        bond_above = bond_here

    copies = []

    def send(source, target):
        copies.append(pltpu.make_async_copy(source, target, sems.at[len(copies)]))
        copies[-1].start()

    out_value = added = column_added = later_0 = later_1 = zero
    for k in range(depth - 1, -1, -1):
        out_value = rows[0, k] + rows[1, k] * out_value
        added = rows[2, k] + edge("down_down", k) * added
        column_added = rows[3, k] + edge("down_column", k) * column_added
        value = edge("inside", k) + added
        rows[0, k] = value
        east_step = jnp.where(lane == LANES - 1, column_added, roll(added, -1, 1)) - added
        west_step = jnp.where(lane == 0, column_added, roll(added, 1, 1)) - added
        out_step = out_value - value
        inner_flow = edge("to_inner", k) * added
        change = (
            added
            + edge("to_east", k) * east_step
            + edge("to_west", k) * west_step
            - inner_flow
            + rows[4, k] * out_step
        )
        later_0 = change * edge("inv_up", k) + edge("up_up", k) * later_0
        later_1 = inner_flow * edge("inv_up_1", k) + edge("up_up_1", k) * later_1
        later[0, k] = later_0
        later[1, k] = later_1
        result = edge("after", k) + change
        result_1 = edge("after_1", k) + inner_flow
        for t in range(2):
            for at, source, row in (
                (0, result, 2),
                (ROWS - 1, result, 6),
                (1, result_1, 2),
                (ROWS - 2, result_1, 6),
            ):
                adjoint[t, k, at : at + 1] = source[row + t : row + t + 1]
        product_1 = jnp.where(
            edge_level("inner") > float(k), -edge("cross_inner", k) * added, 0.0
        )
        product = (
            product_1
            + jnp.where(edge_level("east") > float(k), edge("cross_east", k) * east_step, 0.0)
            + jnp.where(edge_level("west") > float(k), edge("cross_west", k) * west_step, 0.0)
            + jnp.where(level_face > float(k), rows[5, k] * out_step, 0.0)
        )
        for name, inset, value in (("grad_h", 0, product), ("grad_h_1", 1, product_1)):
            value = value + roll(value, -1, 0)
            value = edge(name, k) - 0.5 * (value + roll(value, -2, 0))
            grad_h[k, inset : inset + 1] = value[:1]
            grad_h[k, ROWS - 1 - inset : ROWS - inset] = value[4:5]
        if k in (0, depth // 2):
            part = slice(k, k + depth // 2)
            send(adjoint.at[:, part], adjoint_out.at[:, part])
            send(grad_h.at[part], grad_h_out.at[part])


    face_0 = face_1 = later_0 = later_1 = zero
    for k in range(depth + 1):
        if k < depth:
            above_0, above_1 = later_0, later_1
            later_0 = later[0, k] + edge("down_up", k) * later_0
            later_1 = later[1, k] + edge("down_up_1", k) * later_1
        if k == 0:
            continue
        next_0 = next_1 = zero
        if k < depth:
            step = rows[0, k - 1] - rows[0, k]
            next_0 = step * roll(step, -2, 0) + (edge("ahead", k - 1) - edge("ahead", k)) * (
                edge("after", k - 1) + above_0 - edge("after", k) - later_0
            )
            next_1 = (edge("ahead_1", k - 1) - edge("ahead_1", k)) * (above_1 - later_1)
            next_0 = jnp.where(
                edge_level("own") > float(k), next_0 + roll(next_0, -1, 0), 0.0
            )
            next_1 = jnp.where(
                edge_level("own_1") > float(k), next_1 + roll(next_1, -1, 0), 0.0
            )
        value_0 = -0.5 * (face_0 + next_0)
        value_1 = edge("grad_v_1", k - 1) - 0.5 * (face_1 + next_1)
        for inset, value in ((0, value_0), (1, value_1)):
            grad_v[k - 1, inset : inset + 1] = value[:1]
            grad_v[k - 1, ROWS - 1 - inset : ROWS - inset] = value[4:5]
        face_0, face_1 = next_0, next_1
    send(grad_v, grad_v_out)
    for copy in copies:
        copy.wait()


def per_device(tracers, costate, mixing_h, mixing_v, levels, seam_code):
    depth = tracers.shape[1]
    tiles = depth // PER_TILE
    height = 10 * depth
    params = pltpu.CompilerParams(vmem_limit_bytes=48 * 2**20)
    smem = pl.BlockSpec(memory_space=pltpu.SMEM)
    vmem = pl.BlockSpec(memory_space=pltpu.VMEM)
    hbm = pl.BlockSpec(memory_space=pltpu.HBM)
    tile = (ROWS, LANES)

    def flat(array):
        return array.reshape(-1, LANES)

    fields, factors, own, mix_h, mix_v, levels_here = pl.pallas_call(
        prepare,
        out_shape=(
            vmem_out(4 * depth * ROWS, LANES),
            vmem_out(3, depth, *tile),
            vmem_out(2 * tiles, *tile),
            vmem_out(depth, *tile),
            vmem_out(depth, *tile),
            pltpu.VMEM(tile, jnp.int32),
        ),
        in_specs=[smem] + [hbm] * 5,
        scratch_shapes=[pltpu.SemaphoreType.DMA((5,))],
        compiler_params=params,
        name="prepare",
    )(seam_code, *(in_hbm(a) for a in (flat(tracers), flat(costate), mixing_h, mixing_v, levels)))

    count = lax.axis_size("ty")
    near_pairs = [(i, i ^ 1) for i in range(count)]
    far_pairs = [(i, (i + 1 if i % 2 else i - 1) % count) for i in range(count)]
    far = lax.ppermute(own, "ty", far_pairs)
    near = lax.ppermute(own, "ty", near_pairs)

    def cost(work):
        return pl.CostEstimate(flops=work, bytes_accessed=work, transcendentals=0)

    def call(body, outs, *operands, **options):
        return pl.pallas_call(
            body, out_shape=outs, compiler_params=params, name=body.__name__, **options
        )(*(in_vmem(a) for a in operands))

    count = lax.axis_size("tx")
    upward = [(i, (i + 1) % count) for i in range(count)]
    downward = [(i, (i - 1) % count) for i in range(count)]
    early, upper = call(
        pack_rows,
        (vmem_out(height, LANES), vmem_out(height, LANES)),
        *(fields, mix_h, mix_v, levels_here),
    )
    from_below = lax.ppermute(upper, "tx", upward)
    merged, corner, lower = call(
        pack_sides,
        (vmem_out(2 * tiles, *tile), vmem_out(8, LANES), vmem_out(height + 8, LANES)),
        *(near, far, own, early),
    )
    corner_below = lax.ppermute(corner, "tx", upward)
    from_above = lax.ppermute(lower, "tx", downward)
    row_block = (depth, 8, LANES)
    inside, steps, weights, columns, column_factors, up_factors, shallow = call(
        interior_down,
        (
            vmem_out(depth, 4 * ROWS, LANES),
            vmem_out(depth, 4, 4, *tile),
            vmem_out(depth, 4, *tile),
            vmem_out(depth, *tile),
            vmem_out(3, depth, *tile),
            vmem_out(3, depth, *tile),
            vmem_out(4, *tile),
        ),
        *(merged, own, fields, factors, mix_h, mix_v, levels_here, lower),
        scratch_shapes=[vmem_out(2, tiles, *tile)],
        cost_estimate=cost(30_000_000),
    )
    inside, after, adjoint, grad_h = call(
        interior_up,
        (
            vmem_out(depth, 4 * ROWS, LANES),
            vmem_out(depth, 4 * ROWS, LANES),
            vmem_out(2, depth, *tile),
            vmem_out(depth, *tile),
        ),
        *(inside, steps, weights, columns, column_factors, up_factors, shallow, factors),
        cost_estimate=cost(30_000_000),
    )
    edges, edge_levels, grad_v = call(
        interior_edges,
        (
            vmem_out(len(EDGES), *row_block),
            vmem_out(len(EDGE_LEVELS), 8, LANES),
            vmem_out(depth, *tile),
        ),
        *(merged, fields, factors, mix_h, levels_here, inside, after),
        *(weights, column_factors, up_factors, shallow, grad_h),
        scratch_shapes=[vmem_out(depth, 2 * ROWS, LANES)],
        cost_estimate=cost(40_000_000),
    )
    inner = (edges, edge_levels, adjoint, grad_h, grad_v)
    opened = pl.pallas_call(
        open_below,
        out_shape=vmem_out(2, 8, LANES),
        in_specs=[smem] + [vmem] * 3,
        compiler_params=params,
        cost_estimate=cost(900_000_000),
        name="open_below",
    )(seam_code, *(in_vmem(a) for a in (corner_below, merged, inner[1])))
    below = pl.pallas_call(
        turn_below,
        out_shape=vmem_out(height, LANES),
        in_specs=[smem, vmem],
        compiler_params=params,
        name="turn_below",
    )(seam_code, in_vmem(from_below))
    block = jax.ShapeDtypeStruct(mixing_h.shape, jnp.float32)
    return pl.pallas_call(
        finish,
        out_shape=(
            jax.ShapeDtypeStruct(tracers.shape, jnp.float32),
            block,
            block,
            vmem_out(2, depth, *tile),
            vmem_out(depth, *tile),
            vmem_out(depth, *tile),
        ),
        input_output_aliases={7: 3, 8: 4, 9: 5},
        in_specs=[smem] + [vmem] * 9,
        out_specs=(hbm, hbm, hbm, vmem, vmem, vmem),
        scratch_shapes=[
            vmem_out(height, LANES),
            vmem_out(6, *row_block),
            vmem_out(2, *row_block),
            pltpu.SemaphoreType.DMA((5,)),
        ],
        compiler_params=params,
        name="finish",
    )(seam_code, *(in_vmem(a) for a in (below, from_above, opened, merged, *inner)))[:3]


def solution(mesh):
    placed = (
        P("members", None, "tx", "ty"),
        P("members", None, "tx", "ty"),
        P("members", "tx", "ty"),
        P("members", "tx", "ty"),
        P("tx", "ty"),
        P("ty"),
    )
    return jax.shard_map(
        per_device,
        mesh=mesh,
        in_specs=placed,
        out_specs=(
            P("members", None, "tx", "ty"),
            P("members", "tx", "ty"),
            P("members", "tx", "ty"),
        ),
        check_vma=False,
    )
```

```python
import jax
import jax.numpy as jnp
from jax import lax
from jax.experimental import pallas as pl
from jax.experimental.pallas import tpu as pltpu
from jax.sharding import PartitionSpec as P

LANES = 128
ROWS = 16
GROUP = 16
PER_TILE = LANES // GROUP


FILLER = 3


def in_vmem(array):
    return pltpu.with_memory_space_constraint(array, pltpu.VMEM)


def in_hbm(array):
    return pltpu.with_memory_space_constraint(array, pltpu.HBM)


def vmem_out(*shape):
    return pltpu.VMEM(shape, jnp.float32)


def iota(rows, dim):
    return lax.broadcasted_iota(jnp.int32, (rows, LANES), dim)


def roll(value, shift, axis):
    return pltpu.roll(value, shift % value.shape[axis], axis)


def fold(value):
    return jnp.where(iota(8, 0) < 4, value[:8], value[8:])


def east(value, halo):
    return jnp.where(iota(value.shape[0], 1) == LANES - 1, halo, roll(value, -1, 1))


def west(value, halo):
    return jnp.where(iota(value.shape[0], 1) == 0, halo, roll(value, 1, 1))


def rim(tile, base):
    return roll(tile, LANES - 2 - base, 1)


def crossed(tile):
    column = iota(tile.shape[0], 1) % 4
    return jnp.where(
        column == 1, roll(tile, -1, 1), jnp.where(column == 2, roll(tile, 1, 1), tile)
    )


def lane_of(i, q):
    return GROUP * i + 4 * (3 - q)


def tile_of(q, k, depth):
    return slice((q * depth + k) * ROWS, (q * depth + k + 1) * ROWS)


def up(value):
    low, high = roll(value[:8], -1, 0), roll(value[8:], -1, 0)
    return jnp.concatenate([jnp.where(iota(8, 0) == 7, high, low), high], axis=0)


def down(value):
    low, high = roll(value[:8], 1, 0), roll(value[8:], 1, 0)
    return jnp.concatenate([low, jnp.where(iota(8, 0) == 0, low, high)], axis=0)


def bond(mix_v, level, k, depth):
    if k in (-1, depth - 1):
        return jnp.zeros(level.shape, jnp.float32)
    return jnp.where(level > k + 1, 0.5 * (mix_v[k] + mix_v[k + 1]), 0.0)


def factorize(depth, level, mix_v, put):
    bond_above = jnp.zeros(level.shape, jnp.float32)
    inverse = bond_above
    for k in range(depth):
        bond_here = bond(mix_v, level, k, depth)
        inverse = pivot(bond_above, bond_here, inverse)
        put(k, inverse, bond_above * inverse, bond_here * inverse)
        bond_above = bond_here


def pivot(bond_above, bond_here, inverse):
    return 1.0 / (1.0 + bond_above + bond_here - bond_above * bond_above * inverse)


def prepare(
    seam,
    tracers,
    costate,
    mix_h_in,
    mix_v_in,
    levels_in,
    fields,
    factors,
    message,
    mix_h,
    mix_v,
    levels,
    sems,
):
    depth = mix_h.shape[0]
    tiles = depth // PER_TILE
    copies = []
    for n, (source, target, parts) in enumerate(
        (
            (levels_in, levels, 1),
            (mix_v_in, mix_v, 4),
            (tracers, fields.at[: 2 * depth * ROWS], 4),
            (mix_h_in, mix_h, 4),
            (costate, fields.at[2 * depth * ROWS :], 4),
        )
    ):
        size = source.shape[0] // parts
        for m in range(parts):
            cut = slice(m * size, (m + 1) * size)
            pltpu.make_async_copy(source.at[cut], target.at[cut], sems.at[n]).start()
        copies.append(pltpu.make_async_copy(source, target, sems.at[n]))
    for copy in copies[:2]:
        copy.wait()
    level = levels[...]
    place = iota(ROWS, 1) // 4
    zero = jnp.zeros((ROWS, LANES), jnp.float32)

    def put(k, *three):
        for n in range(3):
            factors[n, k] = three[n]

    factorize(depth, level, mix_v, put)
    seconds = [jnp.where(place % 4 == FILLER, seam[0].astype(jnp.float32), zero)] * tiles
    level_f = level.astype(jnp.float32)
    for k in range(depth):
        tile, base = k // PER_TILE, GROUP * (k % PER_TILE)
        for n, value in ((1, mix_v[k]), (2, level_f)):
            seconds[tile] = jnp.where(
                place == base // 4 + n, roll(value, base + 4 * n + 2, 1), seconds[tile]
            )
    firsts = [zero] * tiles

    def add(k, q, value):
        tile, base = k // PER_TILE, lane_of(k % PER_TILE, q)
        firsts[tile] = jnp.where(place == base // 4, roll(value, base + 2, 1), firsts[tile])

    for copy in copies[2:4]:
        copy.wait()
    for k in range(depth):
        tile, base = k // PER_TILE, GROUP * (k % PER_TILE)
        for t in range(2):
            add(k, t, fields[tile_of(t, k, depth)])
        seconds[tile] = jnp.where(
            place == base // 4, roll(mix_h[k], base + 2, 1), seconds[tile]
        )
    copies[4].wait()
    values = [zero, zero]
    for k in range(depth):
        for t in range(2):
            values[t] = fields[tile_of(2 + t, k, depth)] * factors[0, k] + factors[1, k] * values[t]
            fields[tile_of(2 + t, k, depth)] = values[t]
    values = [zero, zero]
    for k in range(depth - 1, -1, -1):
        for t in range(2):
            values[t] = fields[tile_of(2 + t, k, depth)] + factors[2, k] * values[t]
            fields[tile_of(2 + t, k, depth)] = values[t]
            add(k, 2 + t, values[t])
    for tile in range(tiles):
        message[tile] = firsts[tile]
        message[tiles + tile] = seconds[tile]


def pack_rows(fields, mix_h, mix_v, levels, lower, upper):
    depth = mix_h.shape[0]

    def four(k, inset):
        low, high = [
            fields[pl.ds(k * ROWS + row, 4, stride=depth * ROWS)]
            for row in (inset, ROWS - 1 - inset)
        ]
        return jnp.concatenate([low, high], axis=0)

    def ends(ref, inset):
        return both(ref[inset : inset + 1], ref[ROWS - 1 - inset : ROWS - inset])

    def nears(value, inner):
        return east(value, 0.0), west(value, 0.0), inner

    depths = levels[...].astype(jnp.float32)
    level = ends(depths, 0)
    shallow = [jnp.minimum(level, near) for near in nears(level, ends(depths, 1))]
    for k in range(depth):
        mix = ends(mix_h.at[k], 0)
        value = four(k, 0)
        part = value
        for open_to, near_mix, near in zip(
            shallow, nears(mix, ends(mix_h.at[k], 1)), nears(value, four(k, 1))
        ):
            weight = jnp.where(open_to > float(k), 0.5 * (mix + near_mix), 0.0)
            part = part + weight * (near - value)
        lower[8 * k : 8 * k + 8] = both(value, roll(part, 4, 0))
        upper[8 * k : 8 * k + 8] = both(roll(value, 4, 0), part)
        at_mix = slice(8 * depth + k, 8 * depth + k + 1)
        lower[at_mix] = mix_h[k, :1]
        upper[at_mix] = mix_h[k, ROWS - 1 :]
        if k < depth - 1:
            between = 0.5 * (mix_v[k] + mix_v[k + 1])
            at_bond = slice(9 * depth + k, 9 * depth + k + 1)
            lower[at_bond] = between[:1]
            upper[at_bond] = between[ROWS - 1 :]
    lower[10 * depth - 1 :] = depths[:1]
    upper[10 * depth - 1 :] = depths[ROWS - 1 :]


def pack_sides(near, far, own, early, merged, corner, lower):
    tiles = near.shape[0] // 2
    place = lax.axis_index("ty")
    last = lax.axis_size("ty") - 1
    even = place % 2 == 0
    column = iota(ROWS, 1) % 4
    corners = []
    edge = iota(8, 1) % 4
    for j in range(2 * tiles):
        west_tile = jnp.where(even, far[j], near[j])
        east_tile = jnp.where(even, near[j], far[j])
        if j >= tiles:
            west_tile = jnp.where(place == 0, 0.0, west_tile)
            east_tile = jnp.where(place == last, 0.0, east_tile)
        middle = jnp.where(column == 1, roll(east_tile, -1, 1), roll(west_tile, 1, 1))
        merged[j] = jnp.where(
            column == 0, west_tile, jnp.where(column == 3, east_tile, middle)
        )
        west_rows, east_rows = fold(west_tile), fold(east_tile)
        middle = jnp.where(edge == 1, roll(east_rows, -1, 1), roll(west_rows, 1, 1))
        corners.append(
            jnp.where(
                edge == 0,
                roll(west_rows, -2, 1),
                jnp.where(edge == 3, roll(east_rows, 2, 1), middle),
            )
        )
    lane = iota(1, 1)

    def for_row(row, sub):
        flows = []
        for j in range(tiles):
            level_k = (lane // GROUP + j * PER_TILE).astype(jnp.float32)
            mix, level = [
                [coefficient(ref[tiles + j, row : row + 1], n) for ref in (merged, own)]
                for n in (0, 2)
            ]
            weight = jnp.where(jnp.minimum(*level) > level_k, 0.5 * (mix[0] + mix[1]), 0.0)
            flows.append(weight * (merged[j, row : row + 1] - own[j, row : row + 1]))
        return [value[sub : sub + 1] for value in corners] + flows

    corner[...] = stacked(*for_row(ROWS - 1, 7))
    size = early.shape[0]
    for r in range(0, size, 8):
        lower[r : r + 8] = early[r : r + 8]
    lower[size:] = stacked(*for_row(0, 0))


def both(low, high):
    return jnp.where(iota(8, 0) < 4, low, high)


def coefficient(value, n):
    kept = iota(value.shape[0], 1) % GROUP // 4 == n
    value = jnp.where(kept, value, 0.0)
    out = roll(value, -4 * n, 1)
    for q in range(1, 4):
        out = out + roll(value, 4 * (q - n), 1)
    return out


EDGES = (
    "field",
    "mix",
    "inv_down",
    "up_down",
    "down_down",
    "inv_up",
    "up_up",
    "down_up",
    "inv_up_1",
    "up_up_1",
    "down_up_1",
    "to_east",
    "to_west",
    "to_inner",
    "cross_east",
    "cross_west",
    "cross_inner",
    "inside",
    "after",
    "after_1",
    "ahead",
    "ahead_1",
    "grad_h",
    "grad_h_1",
    "grad_v_1",
    "column",
    "mix_column",
    "inv_column",
    "up_column",
    "down_column",
)
EDGE_LEVELS = ("own", "own_1", "east", "west", "inner", "column")


def exchange(value):
    return jnp.where(iota(8, 0) % 4 < 2, roll(value, -2, 0), roll(value, 2, 0))


def at_edges(low, high, i):
    rows = both(low, roll(high, -GROUP, 1))
    shift = LANES - 2 - lane_of(i, 0)
    if i == 0:
        rows, shift = roll(rows, LANES // 2, 1), shift - LANES // 2
    return pltpu.roll(rows, shift % LANES, 1, stride=4, stride_axis=0)


def stacked(*rows):
    sub = iota(8, 0)
    out = jnp.zeros((8, LANES), jnp.float32)
    for n, row in enumerate(rows):
        if row is not None:
            out = jnp.where(sub == n, row, out)
    return out


def nears_of(value, halo):
    return east(value, halo), west(value, halo), up(value), down(value)


def at(q):
    return slice(q * ROWS, (q + 1) * ROWS)


def interior_down(
    merged,
    own,
    fields,
    factors,
    mix_h,
    mix_v,
    levels,
    sent,
    inside,
    steps,
    weights,
    columns,
    column_factors,
    up_factors,
    shallow_out,
    packed,
):
    depth = mix_h.shape[0]
    tiles = depth // PER_TILE
    lane = iota(ROWS, 1)
    zero = jnp.zeros((ROWS, LANES), jnp.float32)
    level = levels[...]
    face_below = inverse = zero
    for k in range(depth - 1, -1, -1):
        face_above = bond(mix_v, level, k - 1, depth)
        inverse = pivot(face_below, face_above, inverse)
        up_factors[0, k] = inverse
        up_factors[1, k] = face_below * inverse
        up_factors[2, k] = face_above * inverse
        face_below = face_above

    column = lane % 4
    last_row, first_row = iota(ROWS, 0) == ROWS - 1, iota(ROWS, 0) == 0
    for j in range(tiles):
        level_k = (lane // GROUP + j * PER_TILE).astype(jnp.float32)
        mix, bonds, depths = [coefficient(merged[tiles + j], n) for n in range(3)]
        own_mix, own_depths = [coefficient(own[tiles + j], n) for n in (0, 2)]
        value = merged[j]

        def outer(array):
            return jnp.where(column == 1, roll(array, -2, 1), roll(array, 2, 1))

        def weight(near_depths, near_mix):
            return jnp.where(
                jnp.minimum(depths, near_depths) > level_k, 0.5 * (mix + near_mix), 0.0
            )

        mixed = value + weight(own_depths, own_mix) * (own[j] - value)
        mixed = mixed + weight(outer(depths), outer(mix)) * (outer(value) - value)
        for border, shift in ((last_row, up), (first_row, down)):
            flow = weight(shift(depths), shift(mix)) * (shift(value) - value)
            mixed = mixed + jnp.where(border, 0.0, flow)
        packed[0, j] = mixed
        packed[1, j] = bonds
        if j == 0:
            level_columns = depths

    def unpacked(n, k):
        return roll(packed[n, k // PER_TILE], -GROUP * (k % PER_TILE), 1)

    level = level.astype(jnp.float32)
    shallow = [jnp.minimum(level, near) for near in nears_of(level, rim(merged[tiles], 8))]
    shallow[2] = jnp.where(last_row, 0.0, shallow[2])
    shallow[3] = jnp.where(first_row, 0.0, shallow[3])
    for n in range(4):
        shallow_out[n] = shallow[n]

    bond_above = col_inverse = col_value = zero
    values = [zero] * 4
    for k in range(depth):
        j, i = divmod(k, PER_TILE)
        under = min(k + 1, depth - 1)
        bond_here = jnp.where(
            level_columns > k + 1.0, 0.5 * (unpacked(1, k) + unpacked(1, under)), 0.0
        )
        col_inverse = pivot(bond_above, bond_here, col_inverse)
        col_factor = bond_above * col_inverse
        col_value = unpacked(0, k) * col_inverse + col_factor * col_value
        columns[k] = col_value
        column_factors[0, k] = col_inverse
        column_factors[1, k] = col_factor
        column_factors[2, k] = bond_here * col_inverse
        bond_above = bond_here
        mix = mix_h[k]
        weight = [
            jnp.where(open_to > float(k), 0.5 * (mix + near), 0.0)
            for open_to, near in zip(shallow, nears_of(mix, rim(merged[tiles + j], GROUP * i)))
        ]
        for n in range(4):
            weights[k, n] = weight[n]
        for q in range(4):
            value = fields[tile_of(q, k, depth)]
            step = [near - value for near in nears_of(value, rim(merged[j], lane_of(i, q)))]
            for n in range(4):
                steps[k, q, n] = step[n]
                value = value + weight[n] * step[n]
            values[q] = value * factors[0, k] + factors[1, k] * values[q]
            inside[k, at(q)] = values[q]


def interior_up(
    inside_in,
    steps,
    weights,
    columns,
    column_factors,
    up_factors,
    shallow_in,
    factors,
    inside,
    after,
    adjoint,
    grad_h,
):
    depth = grad_h.shape[0]
    zero = jnp.zeros((ROWS, LANES), jnp.float32)
    shallow = [shallow_in[n] for n in range(4)]
    col_value = zero
    values = [zero] * 4
    later_values = [zero] * 2
    for k in range(depth - 1, -1, -1):
        col_value = columns[k] + column_factors[2, k] * col_value
        later_steps = []
        for q in range(4):
            value = inside_in[k, at(q)] + factors[2, k] * values[q]
            inside[k, at(q)] = value
            values[q] = value
            step = [near - value for near in nears_of(value, rim(col_value, lane_of(0, q)))]
            later_steps.append(step)
            for n in range(4):
                value = value + weights[k, n] * step[n]
            if q < 2:
                later_values[q] = value * up_factors[0, k] + up_factors[1, k] * later_values[q]
                value = later_values[q]
            else:
                adjoint[q - 2, k] = value
            after[k, at(q)] = value
        total = zero
        for n in range(4):
            face = zero
            for t in range(2):
                face = face + steps[k, t, n] * later_steps[2 + t][n]
                face = face + later_steps[t][n] * steps[k, 2 + t, n]
            total = total + jnp.where(shallow[n] > float(k), face, 0.0)
        grad_h[k] = -0.5 * total


def interior_edges(
    merged,
    fields,
    factors,
    mix_h,
    levels,
    inside,
    after,
    weights,
    column_factors,
    up_factors,
    shallow,
    grad_h,
    edges,
    edge_levels,
    grad_v,
    later,
):
    depth = mix_h.shape[0]
    tiles = depth // PER_TILE
    zero = jnp.zeros((ROWS, LANES), jnp.float32)
    level = levels[...].astype(jnp.float32)
    face_above = zero
    for t in range(2):
        later[0, at(t)] = after[0, at(t)]
    for k in range(depth):
        if k > 0:
            total = zero
            for t in range(2):
                later_here = after[k, at(t)] + up_factors[2, k] * later[k - 1, at(t)]
                later[k, at(t)] = later_here
                total = total + (inside[k - 1, at(2 + t)] - inside[k, at(2 + t)]) * (
                    inside[k - 1, at(t)] - inside[k, at(t)]
                )
                total = total + (
                    fields[tile_of(2 + t, k - 1, depth)] - fields[tile_of(2 + t, k, depth)]
                ) * (later[k - 1, at(t)] - later_here)
            face = jnp.where(level > float(k), total, 0.0)
            grad_v[k - 1] = -0.5 * (face + face_above)
            face_above = face
    grad_v[depth - 1] = -0.5 * face_above

    def ends(value, inset=0):
        return both(value[inset : inset + 1], value[ROWS - 1 - inset : ROWS - inset])

    def four(ref, start, stride, inset=0):
        low, high = start + inset, start + ROWS - 1 - inset
        return stacked(
            *(ref[row + q * stride : row + q * stride + 1] for row in (low, high) for q in range(4))
        )

    last_lane, first_lane = iota(8, 1) == LANES - 1, iota(8, 1) == 0

    coef_rows = ends(merged[tiles])
    for n, value in enumerate(
        (
            ends(level),
            ends(level, 1),
            ends(shallow[0]),
            ends(shallow[1]),
            both(shallow[2, :1], shallow[3, ROWS - 1 :]),
            rim(coef_rows, 8),
        )
    ):
        edge_levels[n] = value

    for k in range(depth):
        j, i = divmod(k, PER_TILE)
        field = four(fields, k * ROWS, depth * ROWS)
        field_1 = four(fields, k * ROWS, depth * ROWS, 1)
        column = at_edges(merged[j, :1], merged[j, ROWS - 1 :], i)
        things = dict(
            field=field,
            mix=ends(mix_h[k]),
            to_east=ends(weights[k, 0]),
            to_west=ends(weights[k, 1]),
            to_inner=both(weights[k, 2, :1], weights[k, 3, ROWS - 1 :]),
            cross_east=exchange(jnp.where(last_lane, column, roll(field, -1, 1)) - field),
            cross_west=exchange(jnp.where(first_lane, column, roll(field, 1, 1)) - field),
            cross_inner=exchange(field_1 - field),
            inside=four(inside.at[k], 0, ROWS),
            after=stacked(
                *(
                    (later if q < 2 else after)[k, q * ROWS + row : q * ROWS + row + 1]
                    for row in (0, ROWS - 1)
                    for q in range(4)
                )
            ),
            after_1=four(after.at[k], 0, ROWS, 1),
            ahead=roll(field, -2, 0),
            ahead_1=roll(field_1, -2, 0),
            grad_h=ends(grad_h[k]),
            grad_h_1=ends(grad_h[k], 1),
            grad_v_1=ends(grad_v[k], 1),
            column=column,
            mix_column=rim(ends(merged[tiles + j]), GROUP * i),
        )
        for n, name in enumerate(("inv", "up", "down")):
            things[name + "_down"] = ends(factors[n, k])
            things[name + "_up"] = ends(up_factors[n, k])
            things[name + "_up_1"] = ends(up_factors[n, k], 1)
            things[name + "_column"] = rim(ends(column_factors[n, k]), 0)
        for name, value in things.items():
            edges[EDGES.index(name), k] = value


def turned_corner(block, merged, tiles, border):
    code = coefficient(merged[tiles, :8], FILLER)[:1]
    swapped = jnp.where(iota(8, 1) % 4 == 1, roll(block, -2, 1), roll(block, 2, 1))
    return jnp.where((lax.axis_index("tx") == border) & (code > 0.5), swapped, block)


def open_below(seam, corner, merged, edge_levels, opened):
    tiles = merged.shape[0] // 2
    turn = (seam[0] == 1) & (lax.axis_index("tx") == 0)
    block = corner[...]
    flows = jnp.where(turn, crossed(block), block)
    block = turned_corner(block, merged, tiles, 0)
    opened[0] = jnp.where(iota(8, 0) < 2 * tiles, block, flows)
    opened[1] = jnp.minimum(
        rim(block[tiles : tiles + 1], 8), edge_levels[EDGE_LEVELS.index("column")]
    )


def turn_rows(seam, border, source, target):
    turn = (seam[0] == 1) & (lax.axis_index("tx") == border)
    size = target.shape[0]

    @pl.when(turn)
    def _():
        back = LANES - 1 - iota(8, 1)
        for r in range(0, size, 8):
            target[r : r + 8] = jnp.take_along_axis(source[r : r + 8], back, axis=1)

    @pl.when(jnp.logical_not(turn))
    def _():
        for r in range(0, size, 8):
            target[r : r + 8] = source[r : r + 8]


def turn_below(seam, from_below, below):
    turn_rows(seam, 0, from_below, below)


def finish(
    seam,
    below,
    from_above,
    opened,
    merged,
    edges,
    edge_levels,
    adjoint_in,
    grad_h_in,
    grad_v_in,
    adjoint_out,
    grad_h_out,
    grad_v_out,
    adjoint,
    grad_h,
    grad_v,
    above,
    rows,
    later,
    sems,
):
    depth, tiles = grad_h.shape[0], grad_h.shape[0] // PER_TILE
    sub = iota(8, 0)
    lane = iota(8, 1)
    place = lax.axis_index("tx")
    last = lax.axis_size("tx") - 1
    base_mix, base_bond, base_level = 8 * depth, 9 * depth, 10 * depth - 1
    size = 10 * depth
    zero = jnp.zeros((8, LANES), jnp.float32)

    def edge(name, k):
        return edges[EDGES.index(name), k]

    def edge_level(name):
        return edge_levels[EDGE_LEVELS.index(name)]

    turn_rows(seam, last, from_above, above)

    last_block = from_above[size:]
    corner_above = turned_corner(last_block, merged, tiles, last)
    turn_above = (seam[0] == 1) & (place == last)
    flows_above = jnp.where(turn_above, crossed(last_block), last_block)

    def corner(r):
        return opened[0, r : r + 1], corner_above[r : r + 1]

    def flow_of(j):
        r = 2 * tiles + j
        return opened[0, r : r + 1], flows_above[r : r + 1]

    beside = (lane == 0) | (lane == LANES - 1)

    def outer(start, k=0):
        at = slice(start + k, start + k + 1)
        return both(below[at], above[at])

    level_out = outer(base_level)
    level_face = jnp.minimum(level_out, edge_level("own"))
    level_corner = both(
        opened[1],
        jnp.minimum(rim(corner_above[tiles : tiles + 1], 8), edge_level("column")),
    )

    bond_above = inverse = out_value = added = column_added = zero
    flows = []
    for k in range(depth):
        j, i = divmod(k, PER_TILE)
        block = slice(8 * k, 8 * k + 8)
        below_block, above_block = below[block], above[block]
        bond_here = zero
        if k < depth - 1:
            bond_here = jnp.where(level_out > k + 1.0, outer(base_bond, k), 0.0)
        inverse = pivot(bond_above, bond_here, inverse)
        out = both(below_block, roll(above_block, 4, 0))
        part = both(roll(below_block, 4, 0), above_block) + jnp.where(
            beside, at_edges(*flow_of(j), i), 0.0
        )
        step = out - edge("field", k)
        weight = jnp.where(level_face > float(k), 0.5 * (outer(base_mix, k) + edge("mix", k)), 0.0)
        flow = weight * step
        out_value = (part - flow) * inverse + bond_above * inverse * out_value
        added = flow * edge("inv_down", k) + edge("up_down", k) * added
        mix_corner = rim(both(*corner(tiles + j)), GROUP * i)
        weight_corner = jnp.where(
            level_corner > float(k), 0.5 * (mix_corner + edge("mix_column", k)), 0.0
        )
        step_corner = at_edges(*corner(j), i) - edge("column", k)
        column_added = (
            weight_corner * step_corner * edge("inv_column", k)
            + edge("up_column", k) * column_added
        )
        rows[0, k] = out_value
        rows[1, k] = bond_here * inverse
        rows[2, k] = added
        rows[3, k] = column_added
        rows[4, k] = weight
        rows[5, k] = exchange(step)
        bond_above = bond_here

    copies = []

    def send(source, target):
        copies.append(pltpu.make_async_copy(source, target, sems.at[len(copies)]))
        copies[-1].start()

    out_value = added = column_added = later_0 = later_1 = zero
    for k in range(depth - 1, -1, -1):
        out_value = rows[0, k] + rows[1, k] * out_value
        added = rows[2, k] + edge("down_down", k) * added
        column_added = rows[3, k] + edge("down_column", k) * column_added
        value = edge("inside", k) + added
        rows[0, k] = value
        east_step = jnp.where(lane == LANES - 1, column_added, roll(added, -1, 1)) - added
        west_step = jnp.where(lane == 0, column_added, roll(added, 1, 1)) - added
        out_step = out_value - value
        inner_flow = edge("to_inner", k) * added
        change = (
            added
            + edge("to_east", k) * east_step
            + edge("to_west", k) * west_step
            - inner_flow
            + rows[4, k] * out_step
        )
        later_0 = change * edge("inv_up", k) + edge("up_up", k) * later_0
        later_1 = inner_flow * edge("inv_up_1", k) + edge("up_up_1", k) * later_1
        later[0, k] = later_0
        later[1, k] = later_1
        result = edge("after", k) + change
        result_1 = edge("after_1", k) + inner_flow
        for t in range(2):
            for at, source, row in (
                (0, result, 2),
                (ROWS - 1, result, 6),
                (1, result_1, 2),
                (ROWS - 2, result_1, 6),
            ):
                adjoint[t, k, at : at + 1] = source[row + t : row + t + 1]
        product_1 = jnp.where(
            edge_level("inner") > float(k), -edge("cross_inner", k) * added, 0.0
        )
        product = (
            product_1
            + jnp.where(edge_level("east") > float(k), edge("cross_east", k) * east_step, 0.0)
            + jnp.where(edge_level("west") > float(k), edge("cross_west", k) * west_step, 0.0)
            + jnp.where(level_face > float(k), rows[5, k] * out_step, 0.0)
        )
        for name, inset, value in (("grad_h", 0, product), ("grad_h_1", 1, product_1)):
            value = value + roll(value, -1, 0)
            value = edge(name, k) - 0.5 * (value + roll(value, -2, 0))
            grad_h[k, inset : inset + 1] = value[:1]
            grad_h[k, ROWS - 1 - inset : ROWS - inset] = value[4:5]
        if k in (0, depth // 2):
            part = slice(k, k + depth // 2)
            send(adjoint.at[:, part], adjoint_out.at[:, part])
            send(grad_h.at[part], grad_h_out.at[part])


    face_0 = face_1 = later_0 = later_1 = zero
    for k in range(depth + 1):
        if k < depth:
            above_0, above_1 = later_0, later_1
            later_0 = later[0, k] + edge("down_up", k) * later_0
            later_1 = later[1, k] + edge("down_up_1", k) * later_1
        if k == 0:
            continue
        next_0 = next_1 = zero
        if k < depth:
            step = rows[0, k - 1] - rows[0, k]
            next_0 = step * roll(step, -2, 0) + (edge("ahead", k - 1) - edge("ahead", k)) * (
                edge("after", k - 1) + above_0 - edge("after", k) - later_0
            )
            next_1 = (edge("ahead_1", k - 1) - edge("ahead_1", k)) * (above_1 - later_1)
            next_0 = jnp.where(
                edge_level("own") > float(k), next_0 + roll(next_0, -1, 0), 0.0
            )
            next_1 = jnp.where(
                edge_level("own_1") > float(k), next_1 + roll(next_1, -1, 0), 0.0
            )
        value_0 = -0.5 * (face_0 + next_0)
        value_1 = edge("grad_v_1", k - 1) - 0.5 * (face_1 + next_1)
        for inset, value in ((0, value_0), (1, value_1)):
            grad_v[k - 1, inset : inset + 1] = value[:1]
            grad_v[k - 1, ROWS - 1 - inset : ROWS - inset] = value[4:5]
        face_0, face_1 = next_0, next_1
    send(grad_v, grad_v_out)
    for copy in copies:
        copy.wait()


def per_device(tracers, costate, mixing_h, mixing_v, levels, seam_code):
    depth = tracers.shape[1]
    tiles = depth // PER_TILE
    height = 10 * depth
    params = pltpu.CompilerParams(vmem_limit_bytes=48 * 2**20)
    smem = pl.BlockSpec(memory_space=pltpu.SMEM)
    vmem = pl.BlockSpec(memory_space=pltpu.VMEM)
    hbm = pl.BlockSpec(memory_space=pltpu.HBM)
    tile = (ROWS, LANES)

    def flat(array):
        return array.reshape(-1, LANES)

    fields, factors, own, mix_h, mix_v, levels_here = pl.pallas_call(
        prepare,
        out_shape=(
            vmem_out(4 * depth * ROWS, LANES),
            vmem_out(3, depth, *tile),
            vmem_out(2 * tiles, *tile),
            vmem_out(depth, *tile),
            vmem_out(depth, *tile),
            pltpu.VMEM(tile, jnp.int32),
        ),
        in_specs=[smem] + [hbm] * 5,
        scratch_shapes=[pltpu.SemaphoreType.DMA((5,))],
        compiler_params=params,
        name="prepare",
    )(seam_code, *(in_hbm(a) for a in (flat(tracers), flat(costate), mixing_h, mixing_v, levels)))

    count = lax.axis_size("ty")
    near_pairs = [(i, i ^ 1) for i in range(count)]
    far_pairs = [(i, (i + 1 if i % 2 else i - 1) % count) for i in range(count)]
    far = lax.ppermute(own, "ty", far_pairs)
    near = lax.ppermute(own, "ty", near_pairs)

    def cost(work):
        return pl.CostEstimate(flops=work, bytes_accessed=work, transcendentals=0)

    def call(body, outs, *operands, **options):
        return pl.pallas_call(
            body, out_shape=outs, compiler_params=params, name=body.__name__, **options
        )(*(in_vmem(a) for a in operands))

    count = lax.axis_size("tx")
    upward = [(i, (i + 1) % count) for i in range(count)]
    downward = [(i, (i - 1) % count) for i in range(count)]
    early, upper = call(
        pack_rows,
        (vmem_out(height, LANES), vmem_out(height, LANES)),
        *(fields, mix_h, mix_v, levels_here),
    )
    from_below = lax.ppermute(upper, "tx", upward)
    merged, corner, lower = call(
        pack_sides,
        (vmem_out(2 * tiles, *tile), vmem_out(8, LANES), vmem_out(height + 8, LANES)),
        *(near, far, own, early),
    )
    corner_below = lax.ppermute(corner, "tx", upward)
    from_above = lax.ppermute(lower, "tx", downward)
    row_block = (depth, 8, LANES)
    inside, steps, weights, columns, column_factors, up_factors, shallow = call(
        interior_down,
        (
            vmem_out(depth, 4 * ROWS, LANES),
            vmem_out(depth, 4, 4, *tile),
            vmem_out(depth, 4, *tile),
            vmem_out(depth, *tile),
            vmem_out(3, depth, *tile),
            vmem_out(3, depth, *tile),
            vmem_out(4, *tile),
        ),
        *(merged, own, fields, factors, mix_h, mix_v, levels_here, lower),
        scratch_shapes=[vmem_out(2, tiles, *tile)],
        cost_estimate=cost(30_000_000),
    )
    inside, after, adjoint, grad_h = call(
        interior_up,
        (
            vmem_out(depth, 4 * ROWS, LANES),
            vmem_out(depth, 4 * ROWS, LANES),
            vmem_out(2, depth, *tile),
            vmem_out(depth, *tile),
        ),
        *(inside, steps, weights, columns, column_factors, up_factors, shallow, factors),
        cost_estimate=cost(30_000_000),
    )
    edges, edge_levels, grad_v = call(
        interior_edges,
        (
            vmem_out(len(EDGES), *row_block),
            vmem_out(len(EDGE_LEVELS), 8, LANES),
            vmem_out(depth, *tile),
        ),
        *(merged, fields, factors, mix_h, levels_here, inside, after),
        *(weights, column_factors, up_factors, shallow, grad_h),
        scratch_shapes=[vmem_out(depth, 2 * ROWS, LANES)],
        cost_estimate=cost(40_000_000),
    )
    inner = (edges, edge_levels, adjoint, grad_h, grad_v)
    opened = pl.pallas_call(
        open_below,
        out_shape=vmem_out(2, 8, LANES),
        in_specs=[smem] + [vmem] * 3,
        compiler_params=params,
        cost_estimate=cost(900_000_000),
        name="open_below",
    )(seam_code, *(in_vmem(a) for a in (corner_below, merged, inner[1])))
    below = pl.pallas_call(
        turn_below,
        out_shape=vmem_out(height, LANES),
        in_specs=[smem, vmem],
        compiler_params=params,
        name="turn_below",
    )(seam_code, in_vmem(from_below))
    block = jax.ShapeDtypeStruct(mixing_h.shape, jnp.float32)
    return pl.pallas_call(
        finish,
        out_shape=(
            jax.ShapeDtypeStruct(tracers.shape, jnp.float32),
            block,
            block,
            vmem_out(2, depth, *tile),
            vmem_out(depth, *tile),
            vmem_out(depth, *tile),
        ),
        input_output_aliases={7: 3, 8: 4, 9: 5},
        in_specs=[smem] + [vmem] * 9,
        out_specs=(hbm, hbm, hbm, vmem, vmem, vmem),
        scratch_shapes=[
            vmem_out(height, LANES),
            vmem_out(6, *row_block),
            vmem_out(2, *row_block),
            pltpu.SemaphoreType.DMA((5,)),
        ],
        compiler_params=params,
        name="finish",
    )(seam_code, *(in_vmem(a) for a in (below, from_above, opened, merged, *inner)))[:3]


def solution(mesh):
    placed = (
        P("members", None, "tx", "ty"),
        P("members", None, "tx", "ty"),
        P("members", "tx", "ty"),
        P("members", "tx", "ty"),
        P("tx", "ty"),
        P("ty"),
    )
    return jax.shard_map(
        per_device,
        mesh=mesh,
        in_specs=placed,
        out_specs=(
            P("members", None, "tx", "ty"),
            P("members", "tx", "ty"),
            P("members", "tx", "ty"),
        ),
        check_vma=False,
    )
```

```python
import jax
import jax.numpy as jnp
from jax import lax
from jax.experimental import pallas as pl
from jax.experimental.pallas import tpu as pltpu
from jax.sharding import PartitionSpec as P

LANES = 128
ROWS = 16
GROUP = 16
PER_TILE = LANES // GROUP


FILLER = 3


def in_vmem(array):
    return pltpu.with_memory_space_constraint(array, pltpu.VMEM)


def in_hbm(array):
    return pltpu.with_memory_space_constraint(array, pltpu.HBM)


def vmem_out(*shape):
    return pltpu.VMEM(shape, jnp.float32)


def iota(rows, dim):
    return lax.broadcasted_iota(jnp.int32, (rows, LANES), dim)


def roll(value, shift, axis):
    return pltpu.roll(value, shift % value.shape[axis], axis)


def fold(value):
    return jnp.where(iota(8, 0) < 4, value[:8], value[8:])


def east(value, halo):
    return jnp.where(iota(value.shape[0], 1) == LANES - 1, halo, roll(value, -1, 1))


def west(value, halo):
    return jnp.where(iota(value.shape[0], 1) == 0, halo, roll(value, 1, 1))


def rim(tile, base):
    return roll(tile, LANES - 2 - base, 1)


def crossed(tile):
    column = iota(tile.shape[0], 1) % 4
    return jnp.where(
        column == 1, roll(tile, -1, 1), jnp.where(column == 2, roll(tile, 1, 1), tile)
    )


def lane_of(i, q):
    return GROUP * i + 4 * (3 - q)


def tile_of(q, k, depth):
    return slice((q * depth + k) * ROWS, (q * depth + k + 1) * ROWS)


def up(value):
    low, high = roll(value[:8], -1, 0), roll(value[8:], -1, 0)
    return jnp.concatenate([jnp.where(iota(8, 0) == 7, high, low), high], axis=0)


def down(value):
    low, high = roll(value[:8], 1, 0), roll(value[8:], 1, 0)
    return jnp.concatenate([low, jnp.where(iota(8, 0) == 0, low, high)], axis=0)


def bond(mix_v, level, k, depth):
    if k in (-1, depth - 1):
        return jnp.zeros(level.shape, jnp.float32)
    return jnp.where(level > k + 1, 0.5 * (mix_v[k] + mix_v[k + 1]), 0.0)


def factorize(depth, level, mix_v, put):
    bond_above = jnp.zeros(level.shape, jnp.float32)
    inverse = bond_above
    for k in range(depth):
        bond_here = bond(mix_v, level, k, depth)
        inverse = pivot(bond_above, bond_here, inverse)
        put(k, inverse, bond_above * inverse, bond_here * inverse)
        bond_above = bond_here


def pivot(bond_above, bond_here, inverse):
    return 1.0 / (1.0 + bond_above + bond_here - bond_above * bond_above * inverse)


def prepare(
    seam,
    tracers,
    costate,
    mix_h_in,
    mix_v_in,
    levels_in,
    fields,
    factors,
    message,
    mix_h,
    mix_v,
    levels,
    sems,
):
    depth = mix_h.shape[0]
    tiles = depth // PER_TILE
    copies = []
    for n, (source, target, parts) in enumerate(
        (
            (levels_in, levels, 1),
            (mix_v_in, mix_v, 4),
            (tracers, fields.at[: 2 * depth * ROWS], 4),
            (mix_h_in, mix_h, 4),
            (costate, fields.at[2 * depth * ROWS :], 4),
        )
    ):
        size = source.shape[0] // parts
        for m in range(parts):
            cut = slice(m * size, (m + 1) * size)
            pltpu.make_async_copy(source.at[cut], target.at[cut], sems.at[n]).start()
        copies.append(pltpu.make_async_copy(source, target, sems.at[n]))
    for copy in copies[:2]:
        copy.wait()
    level = levels[...]
    place = iota(ROWS, 1) // 4
    zero = jnp.zeros((ROWS, LANES), jnp.float32)

    def put(k, *three):
        for n in range(3):
            factors[n, k] = three[n]

    factorize(depth, level, mix_v, put)
    seconds = [jnp.where(place % 4 == FILLER, seam[0].astype(jnp.float32), zero)] * tiles
    level_f = level.astype(jnp.float32)
    for k in range(depth):
        tile, base = k // PER_TILE, GROUP * (k % PER_TILE)
        for n, value in ((1, mix_v[k]), (2, level_f)):
            seconds[tile] = jnp.where(
                place == base // 4 + n, roll(value, base + 4 * n + 2, 1), seconds[tile]
            )
    firsts = [zero] * tiles

    def add(k, q, value):
        tile, base = k // PER_TILE, lane_of(k % PER_TILE, q)
        firsts[tile] = jnp.where(place == base // 4, roll(value, base + 2, 1), firsts[tile])

    for copy in copies[2:4]:
        copy.wait()
    for k in range(depth):
        tile, base = k // PER_TILE, GROUP * (k % PER_TILE)
        for t in range(2):
            add(k, t, fields[tile_of(t, k, depth)])
        seconds[tile] = jnp.where(
            place == base // 4, roll(mix_h[k], base + 2, 1), seconds[tile]
        )
    copies[4].wait()
    values = [zero, zero]
    for k in range(depth):
        for t in range(2):
            values[t] = fields[tile_of(2 + t, k, depth)] * factors[0, k] + factors[1, k] * values[t]
            fields[tile_of(2 + t, k, depth)] = values[t]
    values = [zero, zero]
    for k in range(depth - 1, -1, -1):
        for t in range(2):
            values[t] = fields[tile_of(2 + t, k, depth)] + factors[2, k] * values[t]
            fields[tile_of(2 + t, k, depth)] = values[t]
            add(k, 2 + t, values[t])
    for tile in range(tiles):
        message[tile] = firsts[tile]
        message[tiles + tile] = seconds[tile]


def pack_rows(fields, mix_h, mix_v, levels, lower, upper):
    depth = mix_h.shape[0]

    def four(k, inset):
        low, high = [
            fields[pl.ds(k * ROWS + row, 4, stride=depth * ROWS)]
            for row in (inset, ROWS - 1 - inset)
        ]
        return jnp.concatenate([low, high], axis=0)

    def ends(ref, inset):
        return both(ref[inset : inset + 1], ref[ROWS - 1 - inset : ROWS - inset])

    def nears(value, inner):
        return east(value, 0.0), west(value, 0.0), inner

    depths = levels[...].astype(jnp.float32)
    level = ends(depths, 0)
    shallow = [jnp.minimum(level, near) for near in nears(level, ends(depths, 1))]
    for k in range(depth):
        mix = ends(mix_h.at[k], 0)
        value = four(k, 0)
        part = value
        for open_to, near_mix, near in zip(
            shallow, nears(mix, ends(mix_h.at[k], 1)), nears(value, four(k, 1))
        ):
            weight = jnp.where(open_to > float(k), 0.5 * (mix + near_mix), 0.0)
            part = part + weight * (near - value)
        lower[8 * k : 8 * k + 8] = both(value, roll(part, 4, 0))
        upper[8 * k : 8 * k + 8] = both(roll(value, 4, 0), part)
        at_mix = slice(8 * depth + k, 8 * depth + k + 1)
        lower[at_mix] = mix_h[k, :1]
        upper[at_mix] = mix_h[k, ROWS - 1 :]
        if k < depth - 1:
            between = 0.5 * (mix_v[k] + mix_v[k + 1])
            at_bond = slice(9 * depth + k, 9 * depth + k + 1)
            lower[at_bond] = between[:1]
            upper[at_bond] = between[ROWS - 1 :]
    lower[10 * depth - 1 :] = depths[:1]
    upper[10 * depth - 1 :] = depths[ROWS - 1 :]


def pack_sides(near, far, own, early, merged, corner, lower):
    tiles = near.shape[0] // 2
    place = lax.axis_index("ty")
    last = lax.axis_size("ty") - 1
    even = place % 2 == 0
    column = iota(ROWS, 1) % 4
    corners = []
    edge = iota(8, 1) % 4
    for j in range(2 * tiles):
        west_tile = jnp.where(even, far[j], near[j])
        east_tile = jnp.where(even, near[j], far[j])
        if j >= tiles:
            west_tile = jnp.where(place == 0, 0.0, west_tile)
            east_tile = jnp.where(place == last, 0.0, east_tile)
        middle = jnp.where(column == 1, roll(east_tile, -1, 1), roll(west_tile, 1, 1))
        merged[j] = jnp.where(
            column == 0, west_tile, jnp.where(column == 3, east_tile, middle)
        )
        west_rows, east_rows = fold(west_tile), fold(east_tile)
        middle = jnp.where(edge == 1, roll(east_rows, -1, 1), roll(west_rows, 1, 1))
        corners.append(
            jnp.where(
                edge == 0,
                roll(west_rows, -2, 1),
                jnp.where(edge == 3, roll(east_rows, 2, 1), middle),
            )
        )
    lane = iota(1, 1)

    def for_row(row, sub):
        flows = []
        for j in range(tiles):
            level_k = (lane // GROUP + j * PER_TILE).astype(jnp.float32)
            mix, level = [
                [coefficient(ref[tiles + j, row : row + 1], n) for ref in (merged, own)]
                for n in (0, 2)
            ]
            weight = jnp.where(jnp.minimum(*level) > level_k, 0.5 * (mix[0] + mix[1]), 0.0)
            flows.append(weight * (merged[j, row : row + 1] - own[j, row : row + 1]))
        return [value[sub : sub + 1] for value in corners] + flows

    corner[...] = stacked(*for_row(ROWS - 1, 7))
    size = early.shape[0]
    for r in range(0, size, 8):
        lower[r : r + 8] = early[r : r + 8]
    lower[size:] = stacked(*for_row(0, 0))


def both(low, high):
    return jnp.where(iota(8, 0) < 4, low, high)


def coefficient(value, n):
    kept = iota(value.shape[0], 1) % GROUP // 4 == n
    value = jnp.where(kept, value, 0.0)
    out = roll(value, -4 * n, 1)
    for q in range(1, 4):
        out = out + roll(value, 4 * (q - n), 1)
    return out


EDGES = (
    "field",
    "mix",
    "inv_down",
    "up_down",
    "down_down",
    "inv_up",
    "up_up",
    "down_up",
    "inv_up_1",
    "up_up_1",
    "down_up_1",
    "to_east",
    "to_west",
    "to_inner",
    "cross_east",
    "cross_west",
    "cross_inner",
    "inside",
    "after",
    "after_1",
    "ahead",
    "ahead_1",
    "grad_h",
    "grad_h_1",
    "grad_v_1",
    "column",
    "mix_column",
    "inv_column",
    "up_column",
    "down_column",
)
EDGE_LEVELS = ("own", "own_1", "east", "west", "inner", "column")


def exchange(value):
    return jnp.where(iota(8, 0) % 4 < 2, roll(value, -2, 0), roll(value, 2, 0))


def at_edges(low, high, i):
    rows = both(low, roll(high, -GROUP, 1))
    shift = LANES - 2 - lane_of(i, 0)
    if i == 0:
        rows, shift = roll(rows, LANES // 2, 1), shift - LANES // 2
    return pltpu.roll(rows, shift % LANES, 1, stride=4, stride_axis=0)


def stacked(*rows):
    sub = iota(8, 0)
    out = jnp.zeros((8, LANES), jnp.float32)
    for n, row in enumerate(rows):
        if row is not None:
            out = jnp.where(sub == n, row, out)
    return out


def nears_of(value, halo):
    return east(value, halo), west(value, halo), up(value), down(value)


def at(q):
    return slice(q * ROWS, (q + 1) * ROWS)


def interior_down(
    merged,
    own,
    fields,
    factors,
    mix_h,
    mix_v,
    levels,
    sent,
    inside,
    steps,
    weights,
    columns,
    column_factors,
    up_factors,
    shallow_out,
    packed,
):
    depth = mix_h.shape[0]
    tiles = depth // PER_TILE
    lane = iota(ROWS, 1)
    zero = jnp.zeros((ROWS, LANES), jnp.float32)
    level = levels[...]
    face_below = inverse = zero
    for k in range(depth - 1, -1, -1):
        face_above = bond(mix_v, level, k - 1, depth)
        inverse = pivot(face_below, face_above, inverse)
        up_factors[0, k] = inverse
        up_factors[1, k] = face_below * inverse
        up_factors[2, k] = face_above * inverse
        face_below = face_above

    column = lane % 4
    last_row, first_row = iota(ROWS, 0) == ROWS - 1, iota(ROWS, 0) == 0
    for j in range(tiles):
        level_k = (lane // GROUP + j * PER_TILE).astype(jnp.float32)
        mix, bonds, depths = [coefficient(merged[tiles + j], n) for n in range(3)]
        own_mix, own_depths = [coefficient(own[tiles + j], n) for n in (0, 2)]
        value = merged[j]

        def outer(array):
            return jnp.where(column == 1, roll(array, -2, 1), roll(array, 2, 1))

        def weight(near_depths, near_mix):
            return jnp.where(
                jnp.minimum(depths, near_depths) > level_k, 0.5 * (mix + near_mix), 0.0
            )

        mixed = value + weight(own_depths, own_mix) * (own[j] - value)
        mixed = mixed + weight(outer(depths), outer(mix)) * (outer(value) - value)
        for border, shift in ((last_row, up), (first_row, down)):
            flow = weight(shift(depths), shift(mix)) * (shift(value) - value)
            mixed = mixed + jnp.where(border, 0.0, flow)
        packed[0, j] = mixed
        packed[1, j] = bonds
        if j == 0:
            level_columns = depths

    def unpacked(n, k):
        return roll(packed[n, k // PER_TILE], -GROUP * (k % PER_TILE), 1)

    level = level.astype(jnp.float32)
    shallow = [jnp.minimum(level, near) for near in nears_of(level, rim(merged[tiles], 8))]
    shallow[2] = jnp.where(last_row, 0.0, shallow[2])
    shallow[3] = jnp.where(first_row, 0.0, shallow[3])
    for n in range(4):
        shallow_out[n] = shallow[n]

    bond_above = col_inverse = col_value = zero
    values = [zero] * 4
    for k in range(depth):
        j, i = divmod(k, PER_TILE)
        under = min(k + 1, depth - 1)
        bond_here = jnp.where(
            level_columns > k + 1.0, 0.5 * (unpacked(1, k) + unpacked(1, under)), 0.0
        )
        col_inverse = pivot(bond_above, bond_here, col_inverse)
        col_factor = bond_above * col_inverse
        col_value = unpacked(0, k) * col_inverse + col_factor * col_value
        columns[k] = col_value
        column_factors[0, k] = col_inverse
        column_factors[1, k] = col_factor
        column_factors[2, k] = bond_here * col_inverse
        bond_above = bond_here
        mix = mix_h[k]
        weight = [
            jnp.where(open_to > float(k), 0.5 * (mix + near), 0.0)
            for open_to, near in zip(shallow, nears_of(mix, rim(merged[tiles + j], GROUP * i)))
        ]
        for n in range(4):
            weights[k, n] = weight[n]
        for q in range(4):
            value = fields[tile_of(q, k, depth)]
            step = [near - value for near in nears_of(value, rim(merged[j], lane_of(i, q)))]
            for n in range(4):
                steps[k, q, n] = step[n]
                value = value + weight[n] * step[n]
            values[q] = value * factors[0, k] + factors[1, k] * values[q]
            inside[k, at(q)] = values[q]


def interior_up(
    inside_in,
    steps,
    weights,
    columns,
    column_factors,
    up_factors,
    shallow_in,
    factors,
    inside,
    after,
    adjoint,
    grad_h,
):
    depth = grad_h.shape[0]
    zero = jnp.zeros((ROWS, LANES), jnp.float32)
    shallow = [shallow_in[n] for n in range(4)]
    col_value = zero
    values = [zero] * 4
    later_values = [zero] * 2
    for k in range(depth - 1, -1, -1):
        col_value = columns[k] + column_factors[2, k] * col_value
        later_steps = []
        for q in range(4):
            value = inside_in[k, at(q)] + factors[2, k] * values[q]
            inside[k, at(q)] = value
            values[q] = value
            step = [near - value for near in nears_of(value, rim(col_value, lane_of(0, q)))]
            later_steps.append(step)
            for n in range(4):
                value = value + weights[k, n] * step[n]
            if q < 2:
                later_values[q] = value * up_factors[0, k] + up_factors[1, k] * later_values[q]
                value = later_values[q]
            else:
                adjoint[q - 2, k] = value
            after[k, at(q)] = value
        total = zero
        for n in range(4):
            face = zero
            for t in range(2):
                face = face + steps[k, t, n] * later_steps[2 + t][n]
                face = face + later_steps[t][n] * steps[k, 2 + t, n]
            total = total + jnp.where(shallow[n] > float(k), face, 0.0)
        grad_h[k] = -0.5 * total


def interior_edges(
    merged,
    fields,
    factors,
    mix_h,
    levels,
    inside,
    after,
    weights,
    column_factors,
    up_factors,
    shallow,
    grad_h,
    edges,
    edge_levels,
    grad_v,
    later,
):
    depth = mix_h.shape[0]
    tiles = depth // PER_TILE
    zero = jnp.zeros((ROWS, LANES), jnp.float32)
    level = levels[...].astype(jnp.float32)
    face_above = zero
    for t in range(2):
        later[0, at(t)] = after[0, at(t)]
    for k in range(depth):
        if k > 0:
            total = zero
            for t in range(2):
                later_here = after[k, at(t)] + up_factors[2, k] * later[k - 1, at(t)]
                later[k, at(t)] = later_here
                total = total + (inside[k - 1, at(2 + t)] - inside[k, at(2 + t)]) * (
                    inside[k - 1, at(t)] - inside[k, at(t)]
                )
                total = total + (
                    fields[tile_of(2 + t, k - 1, depth)] - fields[tile_of(2 + t, k, depth)]
                ) * (later[k - 1, at(t)] - later_here)
            face = jnp.where(level > float(k), total, 0.0)
            grad_v[k - 1] = -0.5 * (face + face_above)
            face_above = face
    grad_v[depth - 1] = -0.5 * face_above

    def ends(value, inset=0):
        return both(value[inset : inset + 1], value[ROWS - 1 - inset : ROWS - inset])

    def four(ref, start, stride, inset=0):
        low, high = start + inset, start + ROWS - 1 - inset
        return stacked(
            *(ref[row + q * stride : row + q * stride + 1] for row in (low, high) for q in range(4))
        )

    def opened_step(n, k, step):
        return jnp.where(edge_levels[n] > float(k), exchange(step), 0.0)

    last_lane, first_lane = iota(8, 1) == LANES - 1, iota(8, 1) == 0

    coef_rows = ends(merged[tiles])
    for n, value in enumerate(
        (
            ends(level),
            ends(level, 1),
            ends(shallow[0]),
            ends(shallow[1]),
            both(shallow[2, :1], shallow[3, ROWS - 1 :]),
            rim(coef_rows, 8),
        )
    ):
        edge_levels[n] = value

    for k in range(depth):
        j, i = divmod(k, PER_TILE)
        field = four(fields, k * ROWS, depth * ROWS)
        field_1 = four(fields, k * ROWS, depth * ROWS, 1)
        column = at_edges(merged[j, :1], merged[j, ROWS - 1 :], i)
        things = dict(
            field=field,
            mix=ends(mix_h[k]),
            to_east=ends(weights[k, 0]),
            to_west=ends(weights[k, 1]),
            to_inner=both(weights[k, 2, :1], weights[k, 3, ROWS - 1 :]),
            cross_east=opened_step(2, k, jnp.where(last_lane, column, roll(field, -1, 1)) - field),
            cross_west=opened_step(3, k, jnp.where(first_lane, column, roll(field, 1, 1)) - field),
            cross_inner=opened_step(4, k, field_1 - field),
            inside=four(inside.at[k], 0, ROWS),
            after=stacked(
                *(
                    (later if q < 2 else after)[k, q * ROWS + row : q * ROWS + row + 1]
                    for row in (0, ROWS - 1)
                    for q in range(4)
                )
            ),
            after_1=four(after.at[k], 0, ROWS, 1),
            ahead=roll(field, -2, 0),
            ahead_1=roll(field_1, -2, 0),
            grad_h=ends(grad_h[k]),
            grad_h_1=ends(grad_h[k], 1),
            grad_v_1=ends(grad_v[k], 1),
            column=column,
            mix_column=rim(ends(merged[tiles + j]), GROUP * i),
        )
        for n, name in enumerate(("inv", "up", "down")):
            things[name + "_down"] = ends(factors[n, k])
            things[name + "_up"] = ends(up_factors[n, k])
            things[name + "_up_1"] = ends(up_factors[n, k], 1)
            things[name + "_column"] = rim(ends(column_factors[n, k]), 0)
        for name, value in things.items():
            edges[EDGES.index(name), k] = value


def turned_corner(block, merged, tiles, border):
    code = coefficient(merged[tiles, :8], FILLER)[:1]
    swapped = jnp.where(iota(8, 1) % 4 == 1, roll(block, -2, 1), roll(block, 2, 1))
    return jnp.where((lax.axis_index("tx") == border) & (code > 0.5), swapped, block)


def open_below(seam, corner, merged, edge_levels, opened):
    tiles = merged.shape[0] // 2
    turn = (seam[0] == 1) & (lax.axis_index("tx") == 0)
    block = corner[...]
    flows = jnp.where(turn, crossed(block), block)
    block = turned_corner(block, merged, tiles, 0)
    opened[0] = jnp.where(iota(8, 0) < 2 * tiles, block, flows)
    opened[1] = jnp.minimum(
        rim(block[tiles : tiles + 1], 8), edge_levels[EDGE_LEVELS.index("column")]
    )


def turn_rows(seam, border, source, target):
    turn = (seam[0] == 1) & (lax.axis_index("tx") == border)
    size = target.shape[0]

    @pl.when(turn)
    def _():
        back = LANES - 1 - iota(8, 1)
        for r in range(0, size, 8):
            target[r : r + 8] = jnp.take_along_axis(source[r : r + 8], back, axis=1)

    @pl.when(jnp.logical_not(turn))
    def _():
        for r in range(0, size, 8):
            target[r : r + 8] = source[r : r + 8]


def turn_below(seam, from_below, below):
    turn_rows(seam, 0, from_below, below)


def finish(
    seam,
    below,
    from_above,
    opened,
    merged,
    edges,
    edge_levels,
    adjoint_in,
    grad_h_in,
    grad_v_in,
    adjoint_out,
    grad_h_out,
    grad_v_out,
    adjoint,
    grad_h,
    grad_v,
    above,
    rows,
    later,
    sems,
):
    depth, tiles = grad_h.shape[0], grad_h.shape[0] // PER_TILE
    sub = iota(8, 0)
    lane = iota(8, 1)
    place = lax.axis_index("tx")
    last = lax.axis_size("tx") - 1
    base_mix, base_bond, base_level = 8 * depth, 9 * depth, 10 * depth - 1
    size = 10 * depth
    zero = jnp.zeros((8, LANES), jnp.float32)

    def edge(name, k):
        return edges[EDGES.index(name), k]

    def edge_level(name):
        return edge_levels[EDGE_LEVELS.index(name)]

    turn_rows(seam, last, from_above, above)

    last_block = from_above[size:]
    corner_above = turned_corner(last_block, merged, tiles, last)
    turn_above = (seam[0] == 1) & (place == last)
    flows_above = jnp.where(turn_above, crossed(last_block), last_block)

    def corner(r):
        return opened[0, r : r + 1], corner_above[r : r + 1]

    def flow_of(j):
        r = 2 * tiles + j
        return opened[0, r : r + 1], flows_above[r : r + 1]

    beside = (lane == 0) | (lane == LANES - 1)

    def outer(start, k=0):
        at = slice(start + k, start + k + 1)
        return both(below[at], above[at])

    level_out = outer(base_level)
    level_face = jnp.minimum(level_out, edge_level("own"))
    level_corner = both(
        opened[1],
        jnp.minimum(rim(corner_above[tiles : tiles + 1], 8), edge_level("column")),
    )

    bond_above = inverse = out_value = added = column_added = zero
    flows = []
    for k in range(depth):
        j, i = divmod(k, PER_TILE)
        block = slice(8 * k, 8 * k + 8)
        below_block, above_block = below[block], above[block]
        bond_here = zero
        if k < depth - 1:
            bond_here = jnp.where(level_out > k + 1.0, outer(base_bond, k), 0.0)
        inverse = pivot(bond_above, bond_here, inverse)
        out = both(below_block, roll(above_block, 4, 0))
        part = both(roll(below_block, 4, 0), above_block) + jnp.where(
            beside, at_edges(*flow_of(j), i), 0.0
        )
        step = out - edge("field", k)
        weight = jnp.where(level_face > float(k), 0.5 * (outer(base_mix, k) + edge("mix", k)), 0.0)
        flow = weight * step
        out_value = (part - flow) * inverse + bond_above * inverse * out_value
        added = flow * edge("inv_down", k) + edge("up_down", k) * added
        mix_corner = rim(both(*corner(tiles + j)), GROUP * i)
        weight_corner = jnp.where(
            level_corner > float(k), 0.5 * (mix_corner + edge("mix_column", k)), 0.0
        )
        step_corner = at_edges(*corner(j), i) - edge("column", k)
        column_added = (
            weight_corner * step_corner * edge("inv_column", k)
            + edge("up_column", k) * column_added
        )
        rows[0, k] = out_value
        rows[1, k] = bond_here * inverse
        rows[2, k] = added
        rows[3, k] = column_added
        rows[4, k] = weight
        rows[5, k] = jnp.where(level_face > float(k), exchange(step), 0.0)
        bond_above = bond_here

    copies = []

    def send(source, target):
        copies.append(pltpu.make_async_copy(source, target, sems.at[len(copies)]))
        copies[-1].start()

    out_value = added = column_added = later_0 = later_1 = zero
    for k in range(depth - 1, -1, -1):
        out_value = rows[0, k] + rows[1, k] * out_value
        added = rows[2, k] + edge("down_down", k) * added
        column_added = rows[3, k] + edge("down_column", k) * column_added
        value = edge("inside", k) + added
        rows[0, k] = value
        east_step = jnp.where(lane == LANES - 1, column_added, roll(added, -1, 1)) - added
        west_step = jnp.where(lane == 0, column_added, roll(added, 1, 1)) - added
        out_step = out_value - value
        inner_flow = edge("to_inner", k) * added
        change = (
            added
            + edge("to_east", k) * east_step
            + edge("to_west", k) * west_step
            - inner_flow
            + rows[4, k] * out_step
        )
        later_0 = change * edge("inv_up", k) + edge("up_up", k) * later_0
        later_1 = inner_flow * edge("inv_up_1", k) + edge("up_up_1", k) * later_1
        later[0, k] = later_0
        later[1, k] = later_1
        result = edge("after", k) + change
        result_1 = edge("after_1", k) + inner_flow
        for t in range(2):
            for at, source, row in (
                (0, result, 2),
                (ROWS - 1, result, 6),
                (1, result_1, 2),
                (ROWS - 2, result_1, 6),
            ):
                adjoint[t, k, at : at + 1] = source[row + t : row + t + 1]
        product_1 = -edge("cross_inner", k) * added
        product = (
            product_1
            + edge("cross_east", k) * east_step
            + edge("cross_west", k) * west_step
            + rows[5, k] * out_step
        )
        for name, inset, value in (("grad_h", 0, product), ("grad_h_1", 1, product_1)):
            value = value + roll(value, -1, 0)
            value = edge(name, k) - 0.5 * (value + roll(value, -2, 0))
            grad_h[k, inset : inset + 1] = value[:1]
            grad_h[k, ROWS - 1 - inset : ROWS - inset] = value[4:5]
        if k in (0, depth // 2):
            part = slice(k, k + depth // 2)
            send(adjoint.at[:, part], adjoint_out.at[:, part])
            send(grad_h.at[part], grad_h_out.at[part])


    face_0 = face_1 = later_0 = later_1 = zero
    for k in range(depth + 1):
        if k < depth:
            above_0, above_1 = later_0, later_1
            later_0 = later[0, k] + edge("down_up", k) * later_0
            later_1 = later[1, k] + edge("down_up_1", k) * later_1
        if k == 0:
            continue
        next_0 = next_1 = zero
        if k < depth:
            step = rows[0, k - 1] - rows[0, k]
            next_0 = step * roll(step, -2, 0) + (edge("ahead", k - 1) - edge("ahead", k)) * (
                edge("after", k - 1) + above_0 - edge("after", k) - later_0
            )
            next_1 = (edge("ahead_1", k - 1) - edge("ahead_1", k)) * (above_1 - later_1)
            next_0 = jnp.where(
                edge_level("own") > float(k), next_0 + roll(next_0, -1, 0), 0.0
            )
            next_1 = jnp.where(
                edge_level("own_1") > float(k), next_1 + roll(next_1, -1, 0), 0.0
            )
        value_0 = -0.5 * (face_0 + next_0)
        value_1 = edge("grad_v_1", k - 1) - 0.5 * (face_1 + next_1)
        for inset, value in ((0, value_0), (1, value_1)):
            grad_v[k - 1, inset : inset + 1] = value[:1]
            grad_v[k - 1, ROWS - 1 - inset : ROWS - inset] = value[4:5]
        face_0, face_1 = next_0, next_1
        if k == depth // 2:
            send(grad_v.at[:k], grad_v_out.at[:k])
    send(grad_v.at[depth // 2 :], grad_v_out.at[depth // 2 :])
    for copy in copies:
        copy.wait()


def per_device(tracers, costate, mixing_h, mixing_v, levels, seam_code):
    depth = tracers.shape[1]
    tiles = depth // PER_TILE
    height = 10 * depth
    params = pltpu.CompilerParams(vmem_limit_bytes=48 * 2**20)
    smem = pl.BlockSpec(memory_space=pltpu.SMEM)
    vmem = pl.BlockSpec(memory_space=pltpu.VMEM)
    hbm = pl.BlockSpec(memory_space=pltpu.HBM)
    tile = (ROWS, LANES)

    def flat(array):
        return array.reshape(-1, LANES)

    fields, factors, own, mix_h, mix_v, levels_here = pl.pallas_call(
        prepare,
        out_shape=(
            vmem_out(4 * depth * ROWS, LANES),
            vmem_out(3, depth, *tile),
            vmem_out(2 * tiles, *tile),
            vmem_out(depth, *tile),
            vmem_out(depth, *tile),
            pltpu.VMEM(tile, jnp.int32),
        ),
        in_specs=[smem] + [hbm] * 5,
        scratch_shapes=[pltpu.SemaphoreType.DMA((5,))],
        compiler_params=params,
        name="prepare",
    )(seam_code, *(in_hbm(a) for a in (flat(tracers), flat(costate), mixing_h, mixing_v, levels)))

    count = lax.axis_size("ty")
    near_pairs = [(i, i ^ 1) for i in range(count)]
    far_pairs = [(i, (i + 1 if i % 2 else i - 1) % count) for i in range(count)]
    far = lax.ppermute(own, "ty", far_pairs)
    near = lax.ppermute(own, "ty", near_pairs)

    def cost(work):
        return pl.CostEstimate(flops=work, bytes_accessed=work, transcendentals=0)

    def call(body, outs, *operands, **options):
        return pl.pallas_call(
            body, out_shape=outs, compiler_params=params, name=body.__name__, **options
        )(*(in_vmem(a) for a in operands))

    count = lax.axis_size("tx")
    upward = [(i, (i + 1) % count) for i in range(count)]
    downward = [(i, (i - 1) % count) for i in range(count)]
    early, upper = call(
        pack_rows,
        (vmem_out(height, LANES), vmem_out(height, LANES)),
        *(fields, mix_h, mix_v, levels_here),
    )
    from_below = lax.ppermute(upper, "tx", upward)
    merged, corner, lower = call(
        pack_sides,
        (vmem_out(2 * tiles, *tile), vmem_out(8, LANES), vmem_out(height + 8, LANES)),
        *(near, far, own, early),
    )
    corner_below = lax.ppermute(corner, "tx", upward)
    from_above = lax.ppermute(lower, "tx", downward)
    row_block = (depth, 8, LANES)
    inside, steps, weights, columns, column_factors, up_factors, shallow = call(
        interior_down,
        (
            vmem_out(depth, 4 * ROWS, LANES),
            vmem_out(depth, 4, 4, *tile),
            vmem_out(depth, 4, *tile),
            vmem_out(depth, *tile),
            vmem_out(3, depth, *tile),
            vmem_out(3, depth, *tile),
            vmem_out(4, *tile),
        ),
        *(merged, own, fields, factors, mix_h, mix_v, levels_here, lower),
        scratch_shapes=[vmem_out(2, tiles, *tile)],
        cost_estimate=cost(30_000_000),
    )
    inside, after, adjoint, grad_h = call(
        interior_up,
        (
            vmem_out(depth, 4 * ROWS, LANES),
            vmem_out(depth, 4 * ROWS, LANES),
            vmem_out(2, depth, *tile),
            vmem_out(depth, *tile),
        ),
        *(inside, steps, weights, columns, column_factors, up_factors, shallow, factors),
        cost_estimate=cost(30_000_000),
    )
    edges, edge_levels, grad_v = call(
        interior_edges,
        (
            vmem_out(len(EDGES), *row_block),
            vmem_out(len(EDGE_LEVELS), 8, LANES),
            vmem_out(depth, *tile),
        ),
        *(merged, fields, factors, mix_h, levels_here, inside, after),
        *(weights, column_factors, up_factors, shallow, grad_h),
        scratch_shapes=[vmem_out(depth, 2 * ROWS, LANES)],
        cost_estimate=cost(40_000_000),
    )
    inner = (edges, edge_levels, adjoint, grad_h, grad_v)
    opened = pl.pallas_call(
        open_below,
        out_shape=vmem_out(2, 8, LANES),
        in_specs=[smem] + [vmem] * 3,
        compiler_params=params,
        cost_estimate=cost(900_000_000),
        name="open_below",
    )(seam_code, *(in_vmem(a) for a in (corner_below, merged, inner[1])))
    below = pl.pallas_call(
        turn_below,
        out_shape=vmem_out(height, LANES),
        in_specs=[smem, vmem],
        compiler_params=params,
        name="turn_below",
    )(seam_code, in_vmem(from_below))
    block = jax.ShapeDtypeStruct(mixing_h.shape, jnp.float32)
    return pl.pallas_call(
        finish,
        out_shape=(
            jax.ShapeDtypeStruct(tracers.shape, jnp.float32),
            block,
            block,
            vmem_out(2, depth, *tile),
            vmem_out(depth, *tile),
            vmem_out(depth, *tile),
        ),
        input_output_aliases={7: 3, 8: 4, 9: 5},
        in_specs=[smem] + [vmem] * 9,
        out_specs=(hbm, hbm, hbm, vmem, vmem, vmem),
        scratch_shapes=[
            vmem_out(height, LANES),
            vmem_out(6, *row_block),
            vmem_out(2, *row_block),
            pltpu.SemaphoreType.DMA((6,)),
        ],
        compiler_params=params,
        name="finish",
    )(seam_code, *(in_vmem(a) for a in (below, from_above, opened, merged, *inner)))[:3]


def solution(mesh):
    placed = (
        P("members", None, "tx", "ty"),
        P("members", None, "tx", "ty"),
        P("members", "tx", "ty"),
        P("members", "tx", "ty"),
        P("tx", "ty"),
        P("ty"),
    )
    return jax.shard_map(
        per_device,
        mesh=mesh,
        in_specs=placed,
        out_specs=(
            P("members", None, "tx", "ty"),
            P("members", "tx", "ty"),
            P("members", "tx", "ty"),
        ),
        check_vma=False,
    )
```

```python
import jax
import jax.numpy as jnp
from jax import lax
from jax.experimental import pallas as pl
from jax.experimental.pallas import tpu as pltpu
from jax.sharding import PartitionSpec as P

LANES = 128
ROWS = 16
GROUP = 16
PER_TILE = LANES // GROUP


FILLER = 3


def in_vmem(array):
    return pltpu.with_memory_space_constraint(array, pltpu.VMEM)


def in_hbm(array):
    return pltpu.with_memory_space_constraint(array, pltpu.HBM)


def vmem_out(*shape):
    return pltpu.VMEM(shape, jnp.float32)


def iota(rows, dim):
    return lax.broadcasted_iota(jnp.int32, (rows, LANES), dim)


def roll(value, shift, axis):
    return pltpu.roll(value, shift % value.shape[axis], axis)


def fold(value):
    return jnp.where(iota(8, 0) < 4, value[:8], value[8:])


def east(value, halo):
    return jnp.where(iota(value.shape[0], 1) == LANES - 1, halo, roll(value, -1, 1))


def west(value, halo):
    return jnp.where(iota(value.shape[0], 1) == 0, halo, roll(value, 1, 1))


def rim(tile, base):
    return roll(tile, LANES - 2 - base, 1)


def crossed(tile):
    column = iota(tile.shape[0], 1) % 4
    return jnp.where(
        column == 1, roll(tile, -1, 1), jnp.where(column == 2, roll(tile, 1, 1), tile)
    )


def lane_of(i, q):
    return GROUP * i + 4 * (3 - q)


def tile_of(q, k, depth):
    return slice((q * depth + k) * ROWS, (q * depth + k + 1) * ROWS)


def up(value):
    low, high = roll(value[:8], -1, 0), roll(value[8:], -1, 0)
    return jnp.concatenate([jnp.where(iota(8, 0) == 7, high, low), high], axis=0)


def down(value):
    low, high = roll(value[:8], 1, 0), roll(value[8:], 1, 0)
    return jnp.concatenate([low, jnp.where(iota(8, 0) == 0, low, high)], axis=0)


def bond(mix_v, level, k, depth):
    if k in (-1, depth - 1):
        return jnp.zeros(level.shape, jnp.float32)
    return jnp.where(level > k + 1, 0.5 * (mix_v[k] + mix_v[k + 1]), 0.0)


def factorize(depth, level, mix_v, put):
    bond_above = jnp.zeros(level.shape, jnp.float32)
    inverse = bond_above
    for k in range(depth):
        bond_here = bond(mix_v, level, k, depth)
        inverse = pivot(bond_above, bond_here, inverse)
        put(k, inverse, bond_above * inverse, bond_here * inverse)
        bond_above = bond_here


def pivot(bond_above, bond_here, inverse):
    return 1.0 / (1.0 + bond_above + bond_here - bond_above * bond_above * inverse)


def prepare(
    seam,
    tracers,
    costate,
    mix_h_in,
    mix_v_in,
    levels_in,
    fields,
    factors,
    message,
    mix_h,
    mix_v,
    levels,
    sems,
):
    depth = mix_h.shape[0]
    tiles = depth // PER_TILE
    copies = []
    for n, (source, target, parts) in enumerate(
        (
            (levels_in, levels, 1),
            (mix_v_in, mix_v, 4),
            (tracers, fields.at[: 2 * depth * ROWS], 4),
            (mix_h_in, mix_h, 4),
            (costate, fields.at[2 * depth * ROWS :], 4),
        )
    ):
        size = source.shape[0] // parts
        for m in range(parts):
            cut = slice(m * size, (m + 1) * size)
            pltpu.make_async_copy(source.at[cut], target.at[cut], sems.at[n]).start()
        copies.append(pltpu.make_async_copy(source, target, sems.at[n]))
    for copy in copies[:2]:
        copy.wait()
    level = levels[...]
    place = iota(ROWS, 1) // 4
    zero = jnp.zeros((ROWS, LANES), jnp.float32)

    def put(k, *three):
        for n in range(3):
            factors[n, k] = three[n]

    factorize(depth, level, mix_v, put)
    seconds = [jnp.where(place % 4 == FILLER, seam[0].astype(jnp.float32), zero)] * tiles
    level_f = level.astype(jnp.float32)
    for k in range(depth):
        tile, base = k // PER_TILE, GROUP * (k % PER_TILE)
        for n, value in ((1, mix_v[k]), (2, level_f)):
            seconds[tile] = jnp.where(
                place == base // 4 + n, roll(value, base + 4 * n + 2, 1), seconds[tile]
            )
    firsts = [zero] * tiles

    def add(k, q, value):
        tile, base = k // PER_TILE, lane_of(k % PER_TILE, q)
        firsts[tile] = jnp.where(place == base // 4, roll(value, base + 2, 1), firsts[tile])

    for copy in copies[2:4]:
        copy.wait()
    for k in range(depth):
        tile, base = k // PER_TILE, GROUP * (k % PER_TILE)
        for t in range(2):
            add(k, t, fields[tile_of(t, k, depth)])
        seconds[tile] = jnp.where(
            place == base // 4, roll(mix_h[k], base + 2, 1), seconds[tile]
        )
    copies[4].wait()
    values = [zero, zero]
    for k in range(depth):
        for t in range(2):
            values[t] = fields[tile_of(2 + t, k, depth)] * factors[0, k] + factors[1, k] * values[t]
            fields[tile_of(2 + t, k, depth)] = values[t]
    values = [zero, zero]
    for k in range(depth - 1, -1, -1):
        for t in range(2):
            values[t] = fields[tile_of(2 + t, k, depth)] + factors[2, k] * values[t]
            fields[tile_of(2 + t, k, depth)] = values[t]
            add(k, 2 + t, values[t])
    for tile in range(tiles):
        message[tile] = firsts[tile]
        message[tiles + tile] = seconds[tile]


def pack_rows(fields, mix_h, mix_v, levels, lower, upper):
    depth = mix_h.shape[0]

    def four(k, inset):
        low, high = [
            fields[pl.ds(k * ROWS + row, 4, stride=depth * ROWS)]
            for row in (inset, ROWS - 1 - inset)
        ]
        return jnp.concatenate([low, high], axis=0)

    def ends(ref, inset):
        return both(ref[inset : inset + 1], ref[ROWS - 1 - inset : ROWS - inset])

    def nears(value, inner):
        return east(value, 0.0), west(value, 0.0), inner

    depths = levels[...].astype(jnp.float32)
    level = ends(depths, 0)
    shallow = [jnp.minimum(level, near) for near in nears(level, ends(depths, 1))]
    for k in range(depth):
        mix = ends(mix_h.at[k], 0)
        value = four(k, 0)
        part = value
        for open_to, near_mix, near in zip(
            shallow, nears(mix, ends(mix_h.at[k], 1)), nears(value, four(k, 1))
        ):
            weight = jnp.where(open_to > float(k), 0.5 * (mix + near_mix), 0.0)
            part = part + weight * (near - value)
        lower[8 * k : 8 * k + 8] = both(value, roll(part, 4, 0))
        upper[8 * k : 8 * k + 8] = both(roll(value, 4, 0), part)
        at_mix = slice(8 * depth + k, 8 * depth + k + 1)
        lower[at_mix] = mix_h[k, :1]
        upper[at_mix] = mix_h[k, ROWS - 1 :]
        if k < depth - 1:
            between = 0.5 * (mix_v[k] + mix_v[k + 1])
            at_bond = slice(9 * depth + k, 9 * depth + k + 1)
            lower[at_bond] = between[:1]
            upper[at_bond] = between[ROWS - 1 :]
    lower[10 * depth - 1 :] = depths[:1]
    upper[10 * depth - 1 :] = depths[ROWS - 1 :]


def pack_sides(far, near, own, early, merged, corner, lower):
    tiles = near.shape[0] // 2
    place = lax.axis_index("ty")
    last = lax.axis_size("ty") - 1
    even = place % 2 == 0
    column = iota(ROWS, 1) % 4
    corners = []
    edge = iota(8, 1) % 4
    for j in range(2 * tiles):
        west_tile = jnp.where(even, far[j], near[j])
        east_tile = jnp.where(even, near[j], far[j])
        if j >= tiles:
            west_tile = jnp.where(place == 0, 0.0, west_tile)
            east_tile = jnp.where(place == last, 0.0, east_tile)
        middle = jnp.where(column == 1, roll(east_tile, -1, 1), roll(west_tile, 1, 1))
        merged[j] = jnp.where(
            column == 0, west_tile, jnp.where(column == 3, east_tile, middle)
        )
        west_rows, east_rows = fold(west_tile), fold(east_tile)
        middle = jnp.where(edge == 1, roll(east_rows, -1, 1), roll(west_rows, 1, 1))
        corners.append(
            jnp.where(
                edge == 0,
                roll(west_rows, -2, 1),
                jnp.where(edge == 3, roll(east_rows, 2, 1), middle),
            )
        )
    lane = iota(1, 1)

    def for_row(row, sub):
        flows = []
        for j in range(tiles):
            level_k = (lane // GROUP + j * PER_TILE).astype(jnp.float32)
            mix, level = [
                [coefficient(ref[tiles + j, row : row + 1], n) for ref in (merged, own)]
                for n in (0, 2)
            ]
            weight = jnp.where(jnp.minimum(*level) > level_k, 0.5 * (mix[0] + mix[1]), 0.0)
            flows.append(weight * (merged[j, row : row + 1] - own[j, row : row + 1]))
        return [value[sub : sub + 1] for value in corners] + flows

    corner[...] = stacked(*for_row(ROWS - 1, 7))
    size = early.shape[0]
    for r in range(0, size, 8):
        lower[r : r + 8] = early[r : r + 8]
    lower[size:] = stacked(*for_row(0, 0))


def both(low, high):
    return jnp.where(iota(8, 0) < 4, low, high)


def coefficient(value, n):
    kept = iota(value.shape[0], 1) % GROUP // 4 == n
    value = jnp.where(kept, value, 0.0)
    out = roll(value, -4 * n, 1)
    for q in range(1, 4):
        out = out + roll(value, 4 * (q - n), 1)
    return out


EDGES = (
    "field",
    "mix",
    "inv_down",
    "up_down",
    "down_down",
    "inv_up",
    "up_up",
    "down_up",
    "inv_up_1",
    "up_up_1",
    "down_up_1",
    "to_east",
    "to_west",
    "to_inner",
    "cross_east",
    "cross_west",
    "cross_inner",
    "inside",
    "after",
    "after_1",
    "ahead",
    "ahead_1",
    "grad_h",
    "grad_h_1",
    "grad_v_1",
    "column",
    "mix_column",
    "inv_column",
    "up_column",
    "down_column",
)
EDGE_LEVELS = ("own", "own_1", "east", "west", "inner", "column")


def exchange(value):
    return jnp.where(iota(8, 0) % 4 < 2, roll(value, -2, 0), roll(value, 2, 0))


def at_edges(low, high, i):
    rows = both(low, roll(high, -GROUP, 1))
    shift = LANES - 2 - lane_of(i, 0)
    if i == 0:
        rows, shift = roll(rows, LANES // 2, 1), shift - LANES // 2
    return pltpu.roll(rows, shift % LANES, 1, stride=4, stride_axis=0)


def stacked(*rows):
    sub = iota(8, 0)
    out = jnp.zeros((8, LANES), jnp.float32)
    for n, row in enumerate(rows):
        if row is not None:
            out = jnp.where(sub == n, row, out)
    return out


def nears_of(value, halo):
    return east(value, halo), west(value, halo), up(value), down(value)


def at(q):
    return slice(q * ROWS, (q + 1) * ROWS)


def interior_down(
    merged,
    own,
    fields,
    factors,
    mix_h,
    mix_v,
    levels,
    sent,
    inside,
    steps,
    weights,
    columns,
    column_factors,
    up_factors,
    shallow_out,
    packed,
):
    depth = mix_h.shape[0]
    tiles = depth // PER_TILE
    lane = iota(ROWS, 1)
    zero = jnp.zeros((ROWS, LANES), jnp.float32)
    level = levels[...]
    face_below = inverse = zero
    for k in range(depth - 1, -1, -1):
        face_above = bond(mix_v, level, k - 1, depth)
        inverse = pivot(face_below, face_above, inverse)
        up_factors[0, k] = inverse
        up_factors[1, k] = face_below * inverse
        up_factors[2, k] = face_above * inverse
        face_below = face_above

    column = lane % 4
    last_row, first_row = iota(ROWS, 0) == ROWS - 1, iota(ROWS, 0) == 0
    for j in range(tiles):
        level_k = (lane // GROUP + j * PER_TILE).astype(jnp.float32)
        mix, bonds, depths = [coefficient(merged[tiles + j], n) for n in range(3)]
        own_mix, own_depths = [coefficient(own[tiles + j], n) for n in (0, 2)]
        value = merged[j]

        def outer(array):
            return jnp.where(column == 1, roll(array, -2, 1), roll(array, 2, 1))

        def weight(near_depths, near_mix):
            return jnp.where(
                jnp.minimum(depths, near_depths) > level_k, 0.5 * (mix + near_mix), 0.0
            )

        mixed = value + weight(own_depths, own_mix) * (own[j] - value)
        mixed = mixed + weight(outer(depths), outer(mix)) * (outer(value) - value)
        for border, shift in ((last_row, up), (first_row, down)):
            flow = weight(shift(depths), shift(mix)) * (shift(value) - value)
            mixed = mixed + jnp.where(border, 0.0, flow)
        packed[0, j] = mixed
        packed[1, j] = bonds
        if j == 0:
            level_columns = depths

    def unpacked(n, k):
        return roll(packed[n, k // PER_TILE], -GROUP * (k % PER_TILE), 1)

    level = level.astype(jnp.float32)
    shallow = [jnp.minimum(level, near) for near in nears_of(level, rim(merged[tiles], 8))]
    shallow[2] = jnp.where(last_row, 0.0, shallow[2])
    shallow[3] = jnp.where(first_row, 0.0, shallow[3])
    for n in range(4):
        shallow_out[n] = shallow[n]

    bond_above = col_inverse = col_value = zero
    values = [zero] * 4
    for k in range(depth):
        j, i = divmod(k, PER_TILE)
        under = min(k + 1, depth - 1)
        bond_here = jnp.where(
            level_columns > k + 1.0, 0.5 * (unpacked(1, k) + unpacked(1, under)), 0.0
        )
        col_inverse = pivot(bond_above, bond_here, col_inverse)
        col_factor = bond_above * col_inverse
        col_value = unpacked(0, k) * col_inverse + col_factor * col_value
        columns[k] = col_value
        column_factors[0, k] = col_inverse
        column_factors[1, k] = col_factor
        column_factors[2, k] = bond_here * col_inverse
        bond_above = bond_here
        mix = mix_h[k]
        weight = [
            jnp.where(open_to > float(k), 0.5 * (mix + near), 0.0)
            for open_to, near in zip(shallow, nears_of(mix, rim(merged[tiles + j], GROUP * i)))
        ]
        for n in range(4):
            weights[k, n] = weight[n]
        for q in range(4):
            value = fields[tile_of(q, k, depth)]
            step = [near - value for near in nears_of(value, rim(merged[j], lane_of(i, q)))]
            for n in range(4):
                steps[k, q, n] = step[n]
                value = value + weight[n] * step[n]
            values[q] = value * factors[0, k] + factors[1, k] * values[q]
            inside[k, at(q)] = values[q]


def interior_up(
    inside_in,
    steps,
    weights,
    columns,
    column_factors,
    up_factors,
    shallow_in,
    factors,
    inside,
    after,
    adjoint,
    grad_h,
):
    depth = grad_h.shape[0]
    zero = jnp.zeros((ROWS, LANES), jnp.float32)
    shallow = [shallow_in[n] for n in range(4)]
    col_value = zero
    values = [zero] * 4
    later_values = [zero] * 2
    for k in range(depth - 1, -1, -1):
        col_value = columns[k] + column_factors[2, k] * col_value
        later_steps = []
        for q in range(4):
            value = inside_in[k, at(q)] + factors[2, k] * values[q]
            inside[k, at(q)] = value
            values[q] = value
            step = [near - value for near in nears_of(value, rim(col_value, lane_of(0, q)))]
            later_steps.append(step)
            for n in range(4):
                value = value + weights[k, n] * step[n]
            if q < 2:
                later_values[q] = value * up_factors[0, k] + up_factors[1, k] * later_values[q]
                value = later_values[q]
            else:
                adjoint[q - 2, k] = value
            after[k, at(q)] = value
        total = zero
        for n in range(4):
            face = zero
            for t in range(2):
                face = face + steps[k, t, n] * later_steps[2 + t][n]
                face = face + later_steps[t][n] * steps[k, 2 + t, n]
            total = total + jnp.where(shallow[n] > float(k), face, 0.0)
        grad_h[k] = -0.5 * total


def interior_edges(
    merged,
    fields,
    factors,
    mix_h,
    levels,
    inside,
    after,
    weights,
    column_factors,
    up_factors,
    shallow,
    grad_h,
    edges,
    edge_levels,
    grad_v,
    later,
):
    depth = mix_h.shape[0]
    tiles = depth // PER_TILE
    zero = jnp.zeros((ROWS, LANES), jnp.float32)
    level = levels[...].astype(jnp.float32)
    face_above = zero
    for t in range(2):
        later[0, at(t)] = after[0, at(t)]
    for k in range(depth):
        if k > 0:
            total = zero
            for t in range(2):
                later_here = after[k, at(t)] + up_factors[2, k] * later[k - 1, at(t)]
                later[k, at(t)] = later_here
                total = total + (inside[k - 1, at(2 + t)] - inside[k, at(2 + t)]) * (
                    inside[k - 1, at(t)] - inside[k, at(t)]
                )
                total = total + (
                    fields[tile_of(2 + t, k - 1, depth)] - fields[tile_of(2 + t, k, depth)]
                ) * (later[k - 1, at(t)] - later_here)
            face = jnp.where(level > float(k), total, 0.0)
            grad_v[k - 1] = -0.5 * (face + face_above)
            face_above = face
    grad_v[depth - 1] = -0.5 * face_above

    def ends(value, inset=0):
        return both(value[inset : inset + 1], value[ROWS - 1 - inset : ROWS - inset])

    def four(ref, start, stride, inset=0):
        low, high = start + inset, start + ROWS - 1 - inset
        return stacked(
            *(ref[row + q * stride : row + q * stride + 1] for row in (low, high) for q in range(4))
        )

    def opened_step(n, k, step):
        return jnp.where(edge_levels[n] > float(k), exchange(step), 0.0)

    last_lane, first_lane = iota(8, 1) == LANES - 1, iota(8, 1) == 0

    coef_rows = ends(merged[tiles])
    for n, value in enumerate(
        (
            ends(level),
            ends(level, 1),
            ends(shallow[0]),
            ends(shallow[1]),
            both(shallow[2, :1], shallow[3, ROWS - 1 :]),
            rim(coef_rows, 8),
        )
    ):
        edge_levels[n] = value

    for k in range(depth):
        j, i = divmod(k, PER_TILE)
        field = four(fields, k * ROWS, depth * ROWS)
        field_1 = four(fields, k * ROWS, depth * ROWS, 1)
        column = at_edges(merged[j, :1], merged[j, ROWS - 1 :], i)
        things = dict(
            field=field,
            mix=ends(mix_h[k]),
            to_east=ends(weights[k, 0]),
            to_west=ends(weights[k, 1]),
            to_inner=both(weights[k, 2, :1], weights[k, 3, ROWS - 1 :]),
            cross_east=opened_step(2, k, jnp.where(last_lane, column, roll(field, -1, 1)) - field),
            cross_west=opened_step(3, k, jnp.where(first_lane, column, roll(field, 1, 1)) - field),
            cross_inner=opened_step(4, k, field_1 - field),
            inside=four(inside.at[k], 0, ROWS),
            after=stacked(
                *(
                    (later if q < 2 else after)[k, q * ROWS + row : q * ROWS + row + 1]
                    for row in (0, ROWS - 1)
                    for q in range(4)
                )
            ),
            after_1=four(after.at[k], 0, ROWS, 1),
            ahead=roll(field, -2, 0),
            ahead_1=roll(field_1, -2, 0),
            grad_h=ends(grad_h[k]),
            grad_h_1=ends(grad_h[k], 1),
            grad_v_1=ends(grad_v[k], 1),
            column=column,
            mix_column=rim(ends(merged[tiles + j]), GROUP * i),
        )
        for n, name in enumerate(("inv", "up", "down")):
            things[name + "_down"] = ends(factors[n, k])
            things[name + "_up"] = ends(up_factors[n, k])
            things[name + "_up_1"] = ends(up_factors[n, k], 1)
            things[name + "_column"] = rim(ends(column_factors[n, k]), 0)
        for name, value in things.items():
            edges[EDGES.index(name), k] = value


def turned_corner(block, merged, tiles, border):
    code = coefficient(merged[tiles, :8], FILLER)[:1]
    swapped = jnp.where(iota(8, 1) % 4 == 1, roll(block, -2, 1), roll(block, 2, 1))
    return jnp.where((lax.axis_index("tx") == border) & (code > 0.5), swapped, block)


def open_below(seam, corner, merged, edge_levels, opened):
    tiles = merged.shape[0] // 2
    turn = (seam[0] == 1) & (lax.axis_index("tx") == 0)
    block = corner[...]
    flows = jnp.where(turn, crossed(block), block)
    block = turned_corner(block, merged, tiles, 0)
    opened[0] = jnp.where(iota(8, 0) < 2 * tiles, block, flows)
    opened[1] = jnp.minimum(
        rim(block[tiles : tiles + 1], 8), edge_levels[EDGE_LEVELS.index("column")]
    )


def turn_rows(seam, border, source, target):
    turn = (seam[0] == 1) & (lax.axis_index("tx") == border)
    size = target.shape[0]

    @pl.when(turn)
    def _():
        back = LANES - 1 - iota(8, 1)
        for r in range(0, size, 8):
            target[r : r + 8] = jnp.take_along_axis(source[r : r + 8], back, axis=1)

    @pl.when(jnp.logical_not(turn))
    def _():
        for r in range(0, size, 8):
            target[r : r + 8] = source[r : r + 8]


def turn_below(seam, from_below, below):
    turn_rows(seam, 0, from_below, below)


def finish(
    seam,
    below,
    from_above,
    opened,
    merged,
    edges,
    edge_levels,
    adjoint_in,
    grad_h_in,
    grad_v_in,
    adjoint_out,
    grad_h_out,
    grad_v_out,
    adjoint,
    grad_h,
    grad_v,
    above,
    rows,
    later,
    sems,
):
    depth, tiles = grad_h.shape[0], grad_h.shape[0] // PER_TILE
    sub = iota(8, 0)
    lane = iota(8, 1)
    place = lax.axis_index("tx")
    last = lax.axis_size("tx") - 1
    base_mix, base_bond, base_level = 8 * depth, 9 * depth, 10 * depth - 1
    size = 10 * depth
    zero = jnp.zeros((8, LANES), jnp.float32)

    def edge(name, k):
        return edges[EDGES.index(name), k]

    def edge_level(name):
        return edge_levels[EDGE_LEVELS.index(name)]

    turn_rows(seam, last, from_above, above)

    last_block = from_above[size:]
    corner_above = turned_corner(last_block, merged, tiles, last)
    turn_above = (seam[0] == 1) & (place == last)
    flows_above = jnp.where(turn_above, crossed(last_block), last_block)

    def corner(r):
        return opened[0, r : r + 1], corner_above[r : r + 1]

    def flow_of(j):
        r = 2 * tiles + j
        return opened[0, r : r + 1], flows_above[r : r + 1]

    beside = (lane == 0) | (lane == LANES - 1)

    def outer(start, k=0):
        at = slice(start + k, start + k + 1)
        return both(below[at], above[at])

    level_out = outer(base_level)
    level_face = jnp.minimum(level_out, edge_level("own"))
    level_corner = both(
        opened[1],
        jnp.minimum(rim(corner_above[tiles : tiles + 1], 8), edge_level("column")),
    )

    bond_above = inverse = out_value = added = column_added = zero
    flows = []
    for k in range(depth):
        j, i = divmod(k, PER_TILE)
        block = slice(8 * k, 8 * k + 8)
        below_block, above_block = below[block], above[block]
        bond_here = zero
        if k < depth - 1:
            bond_here = jnp.where(level_out > k + 1.0, outer(base_bond, k), 0.0)
        inverse = pivot(bond_above, bond_here, inverse)
        out = both(below_block, roll(above_block, 4, 0))
        part = both(roll(below_block, 4, 0), above_block) + jnp.where(
            beside, at_edges(*flow_of(j), i), 0.0
        )
        step = out - edge("field", k)
        weight = jnp.where(level_face > float(k), 0.5 * (outer(base_mix, k) + edge("mix", k)), 0.0)
        flow = weight * step
        out_value = (part - flow) * inverse + bond_above * inverse * out_value
        added = flow * edge("inv_down", k) + edge("up_down", k) * added
        mix_corner = rim(both(*corner(tiles + j)), GROUP * i)
        weight_corner = jnp.where(
            level_corner > float(k), 0.5 * (mix_corner + edge("mix_column", k)), 0.0
        )
        step_corner = at_edges(*corner(j), i) - edge("column", k)
        column_added = (
            weight_corner * step_corner * edge("inv_column", k)
            + edge("up_column", k) * column_added
        )
        rows[0, k] = out_value
        rows[1, k] = bond_here * inverse
        rows[2, k] = added
        rows[3, k] = column_added
        rows[4, k] = weight
        rows[5, k] = jnp.where(level_face > float(k), exchange(step), 0.0)
        bond_above = bond_here

    copies = []

    def send(source, target):
        copies.append(pltpu.make_async_copy(source, target, sems.at[len(copies)]))
        copies[-1].start()

    out_value = added = column_added = later_0 = later_1 = zero
    for k in range(depth - 1, -1, -1):
        out_value = rows[0, k] + rows[1, k] * out_value
        added = rows[2, k] + edge("down_down", k) * added
        column_added = rows[3, k] + edge("down_column", k) * column_added
        value = edge("inside", k) + added
        rows[0, k] = value
        east_step = jnp.where(lane == LANES - 1, column_added, roll(added, -1, 1)) - added
        west_step = jnp.where(lane == 0, column_added, roll(added, 1, 1)) - added
        out_step = out_value - value
        inner_flow = edge("to_inner", k) * added
        change = (
            added
            + edge("to_east", k) * east_step
            + edge("to_west", k) * west_step
            - inner_flow
            + rows[4, k] * out_step
        )
        later_0 = change * edge("inv_up", k) + edge("up_up", k) * later_0
        later_1 = inner_flow * edge("inv_up_1", k) + edge("up_up_1", k) * later_1
        later[0, k] = later_0
        later[1, k] = later_1
        result = edge("after", k) + change
        result_1 = edge("after_1", k) + inner_flow
        for t in range(2):
            for at, source, row in (
                (0, result, 2),
                (ROWS - 1, result, 6),
                (1, result_1, 2),
                (ROWS - 2, result_1, 6),
            ):
                adjoint[t, k, at : at + 1] = source[row + t : row + t + 1]
        product_1 = -edge("cross_inner", k) * added
        product = (
            product_1
            + edge("cross_east", k) * east_step
            + edge("cross_west", k) * west_step
            + rows[5, k] * out_step
        )
        for name, inset, value in (("grad_h", 0, product), ("grad_h_1", 1, product_1)):
            value = value + roll(value, -1, 0)
            value = edge(name, k) - 0.5 * (value + roll(value, -2, 0))
            grad_h[k, inset : inset + 1] = value[:1]
            grad_h[k, ROWS - 1 - inset : ROWS - inset] = value[4:5]
        if k in (0, depth // 2):
            part = slice(k, k + depth // 2)
            send(adjoint.at[:, part], adjoint_out.at[:, part])
            send(grad_h.at[part], grad_h_out.at[part])


    face_0 = face_1 = later_0 = later_1 = zero
    for k in range(depth + 1):
        if k < depth:
            above_0, above_1 = later_0, later_1
            later_0 = later[0, k] + edge("down_up", k) * later_0
            later_1 = later[1, k] + edge("down_up_1", k) * later_1
        if k == 0:
            continue
        next_0 = next_1 = zero
        if k < depth:
            step = rows[0, k - 1] - rows[0, k]
            next_0 = step * roll(step, -2, 0) + (edge("ahead", k - 1) - edge("ahead", k)) * (
                edge("after", k - 1) + above_0 - edge("after", k) - later_0
            )
            next_1 = (edge("ahead_1", k - 1) - edge("ahead_1", k)) * (above_1 - later_1)
            next_0 = jnp.where(
                edge_level("own") > float(k), next_0 + roll(next_0, -1, 0), 0.0
            )
            next_1 = jnp.where(
                edge_level("own_1") > float(k), next_1 + roll(next_1, -1, 0), 0.0
            )
        value_0 = -0.5 * (face_0 + next_0)
        value_1 = edge("grad_v_1", k - 1) - 0.5 * (face_1 + next_1)
        for inset, value in ((0, value_0), (1, value_1)):
            grad_v[k - 1, inset : inset + 1] = value[:1]
            grad_v[k - 1, ROWS - 1 - inset : ROWS - inset] = value[4:5]
        face_0, face_1 = next_0, next_1
        if k == depth // 2:
            send(grad_v.at[:k], grad_v_out.at[:k])
    send(grad_v.at[depth // 2 :], grad_v_out.at[depth // 2 :])
    for copy in copies:
        copy.wait()


def per_device(tracers, costate, mixing_h, mixing_v, levels, seam_code):
    depth = tracers.shape[1]
    tiles = depth // PER_TILE
    height = 10 * depth
    params = pltpu.CompilerParams(vmem_limit_bytes=48 * 2**20)
    smem = pl.BlockSpec(memory_space=pltpu.SMEM)
    vmem = pl.BlockSpec(memory_space=pltpu.VMEM)
    hbm = pl.BlockSpec(memory_space=pltpu.HBM)
    tile = (ROWS, LANES)

    def flat(array):
        return array.reshape(-1, LANES)

    fields, factors, own, mix_h, mix_v, levels_here = pl.pallas_call(
        prepare,
        out_shape=(
            vmem_out(4 * depth * ROWS, LANES),
            vmem_out(3, depth, *tile),
            vmem_out(2 * tiles, *tile),
            vmem_out(depth, *tile),
            vmem_out(depth, *tile),
            pltpu.VMEM(tile, jnp.int32),
        ),
        in_specs=[smem] + [hbm] * 5,
        scratch_shapes=[pltpu.SemaphoreType.DMA((5,))],
        compiler_params=params,
        name="prepare",
    )(seam_code, *(in_hbm(a) for a in (flat(tracers), flat(costate), mixing_h, mixing_v, levels)))

    count = lax.axis_size("ty")
    near_pairs = [(i, i ^ 1) for i in range(count)]
    far_pairs = [(i, (i + 1 if i % 2 else i - 1) % count) for i in range(count)]
    far = lax.ppermute(own, "ty", far_pairs)
    near = lax.ppermute(own, "ty", near_pairs)

    def cost(work):
        return pl.CostEstimate(flops=work, bytes_accessed=work, transcendentals=0)

    def call(body, outs, *operands, **options):
        return pl.pallas_call(
            body, out_shape=outs, compiler_params=params, name=body.__name__, **options
        )(*(in_vmem(a) for a in operands))

    count = lax.axis_size("tx")
    upward = [(i, (i + 1) % count) for i in range(count)]
    downward = [(i, (i - 1) % count) for i in range(count)]
    early, upper = call(
        pack_rows,
        (vmem_out(height, LANES), vmem_out(height, LANES)),
        *(fields, mix_h, mix_v, levels_here),
    )
    from_below = lax.ppermute(upper, "tx", upward)
    merged, corner, lower = call(
        pack_sides,
        (vmem_out(2 * tiles, *tile), vmem_out(8, LANES), vmem_out(height + 8, LANES)),
        *(far, near, own, early),
    )
    corner_below = lax.ppermute(corner, "tx", upward)
    from_above = lax.ppermute(lower, "tx", downward)
    row_block = (depth, 8, LANES)
    inside, steps, weights, columns, column_factors, up_factors, shallow = call(
        interior_down,
        (
            vmem_out(depth, 4 * ROWS, LANES),
            vmem_out(depth, 4, 4, *tile),
            vmem_out(depth, 4, *tile),
            vmem_out(depth, *tile),
            vmem_out(3, depth, *tile),
            vmem_out(3, depth, *tile),
            vmem_out(4, *tile),
        ),
        *(merged, own, fields, factors, mix_h, mix_v, levels_here, lower),
        scratch_shapes=[vmem_out(2, tiles, *tile)],
        cost_estimate=cost(30_000_000),
    )
    inside, after, adjoint, grad_h = call(
        interior_up,
        (
            vmem_out(depth, 4 * ROWS, LANES),
            vmem_out(depth, 4 * ROWS, LANES),
            vmem_out(2, depth, *tile),
            vmem_out(depth, *tile),
        ),
        *(inside, steps, weights, columns, column_factors, up_factors, shallow, factors),
        cost_estimate=cost(30_000_000),
    )
    edges, edge_levels, grad_v = call(
        interior_edges,
        (
            vmem_out(len(EDGES), *row_block),
            vmem_out(len(EDGE_LEVELS), 8, LANES),
            vmem_out(depth, *tile),
        ),
        *(merged, fields, factors, mix_h, levels_here, inside, after),
        *(weights, column_factors, up_factors, shallow, grad_h),
        scratch_shapes=[vmem_out(depth, 2 * ROWS, LANES)],
        cost_estimate=cost(40_000_000),
    )
    inner = (edges, edge_levels, adjoint, grad_h, grad_v)
    opened = pl.pallas_call(
        open_below,
        out_shape=vmem_out(2, 8, LANES),
        in_specs=[smem] + [vmem] * 3,
        compiler_params=params,
        cost_estimate=cost(900_000_000),
        name="open_below",
    )(seam_code, *(in_vmem(a) for a in (corner_below, merged, inner[1])))
    below = pl.pallas_call(
        turn_below,
        out_shape=vmem_out(height, LANES),
        in_specs=[smem, vmem],
        compiler_params=params,
        name="turn_below",
    )(seam_code, in_vmem(from_below))
    block = jax.ShapeDtypeStruct(mixing_h.shape, jnp.float32)
    return pl.pallas_call(
        finish,
        out_shape=(
            jax.ShapeDtypeStruct(tracers.shape, jnp.float32),
            block,
            block,
            vmem_out(2, depth, *tile),
            vmem_out(depth, *tile),
            vmem_out(depth, *tile),
        ),
        input_output_aliases={7: 3, 8: 4, 9: 5},
        in_specs=[smem] + [vmem] * 9,
        out_specs=(hbm, hbm, hbm, vmem, vmem, vmem),
        scratch_shapes=[
            vmem_out(height, LANES),
            vmem_out(6, *row_block),
            vmem_out(2, *row_block),
            pltpu.SemaphoreType.DMA((6,)),
        ],
        compiler_params=params,
        name="finish",
    )(seam_code, *(in_vmem(a) for a in (below, from_above, opened, merged, *inner)))[:3]


def solution(mesh):
    placed = (
        P("members", None, "tx", "ty"),
        P("members", None, "tx", "ty"),
        P("members", "tx", "ty"),
        P("members", "tx", "ty"),
        P("tx", "ty"),
        P("ty"),
    )
    return jax.shard_map(
        per_device,
        mesh=mesh,
        in_specs=placed,
        out_specs=(
            P("members", None, "tx", "ty"),
            P("members", "tx", "ty"),
            P("members", "tx", "ty"),
        ),
        check_vma=False,
    )
```
